128 devices in a mesh: seq: 64 (over z, x, y), head: 2 (over core).
Axes of the slice: x: 4, y: 4, z: 4, core: 2. Of those that a mesh axis runs over, the one named last changes fastest.
Arguments:
- queries: bfloat16 [8192, 32, 128], P('seq', 'head'), may hold values from -240 to 240
- keys: bfloat16 [8192, 32, 128], P('seq', 'head'), may hold values from -6 to 6
- values: bfloat16 [8192, 32, 128], P('seq', 'head'), may hold values from -6 to 6
- target: bfloat16 [8192, 32, 128], P('seq', 'head'), may hold values from -6 to 6
- map_q: bfloat16 [128, 64], replicated, may hold values from -0.5 to 0.5
- map_k: bfloat16 [128, 64], replicated, may hold values from -0.5 to 0.5
Outputs:
- hybrid: bfloat16 [8192, 32, 128], P('seq', 'head')
- grad_q: float32 [128, 64], replicated
- grad_k: float32 [128, 64], replicated
The draws below stay inside these ranges and needn't reach their ends.
All inputs are finite; a program needn't handle non-finite values.
Results may differ from the reference program's by a relative error of at most 0.001.
The reference program's roundings to bfloat16 on the way (of `phi_q`, `phi_k`, `far_grad` and `state_grad`) count: a program that leaves them out, or rounds other values in their place, can miss the bound.
Values may be sent and summed in bfloat16 or wider, within the bound.
A program may use at most 192 MiB of HBM per device.

```python
import jax
import jax.numpy as jnp
from jax import lax

HEADS = 32
DH = 128
FEAT = 64
WINDOW = 64
TOKENS = 8192


def draw_pair(key):
    array_shape = (TOKENS, HEADS, DH)
    key_rows = jnp.clip(jax.random.normal(jax.random.fold_in(key, 101), array_shape, jnp.float32), -6.0, 6.0)
    query_rows = jnp.clip(jax.random.normal(jax.random.fold_in(key, 102), array_shape, jnp.float32), -6.0, 6.0)
    return (query_rows, key_rows)


def draw_queries(key, part):
    return draw_pair(key)[0].astype(jnp.bfloat16)


def draw_keys(key, part):
    return draw_pair(key)[1].astype(jnp.bfloat16)


def shard_levels(stream_key, dims, split, low, high):
    factor_of, own = 1.0, jax.random.fold_in(stream_key, 6)
    for position, parts in split:
        draws = jnp.exp(jax.random.uniform(jax.random.fold_in(own, position), (parts,), jnp.float32, low / len(split), high / len(split)))
        factor_of = factor_of * jnp.repeat(draws, dims[position] // parts).reshape([-1 if axis == position else 1 for axis in range(len(dims))])
    return factor_of


def gaussian(own_key, shape, spread, reach, shards=(), kind=jnp.bfloat16):
    result = spread * jax.random.normal(own_key, shape, jnp.float32)
    if shards:
        result = result * shard_levels(own_key, shape, shards, -0.22, 0.18)
    return jnp.clip(result, -reach, reach).astype(kind)


def setup_inputs(seed: int = 0) -> dict:
    key_list = jax.random.split(jax.random.key(seed), 7)
    return {
        "queries": draw_queries(jax.random.fold_in(key_list[6], 71), 0),
        "keys": draw_keys(jax.random.fold_in(key_list[6], 71), 0),
        "values": gaussian(key_list[2], (TOKENS, HEADS, DH), 1.0, 6.0, ((0, 64), (1, 2))),
        "target": gaussian(key_list[3], (TOKENS, HEADS, DH), 1.0, 6.0, ((0, 64), (1, 2))),
        "map_q": gaussian(key_list[4], (DH, FEAT), DH ** -0.5, 0.5),
        "map_k": gaussian(key_list[5], (DH, FEAT), DH ** -0.5, 0.5),
    }


highest_precision = lax.Precision.HIGHEST

def rounded(array_in):
    return lax.optimization_barrier(array_in.astype(jnp.bfloat16)).astype(jnp.float32)

def features(inputs, weight):
    hidden = jnp.einsum('thd,df->thf', inputs.astype(jnp.float32), weight.astype(jnp.float32), precision=highest_precision)
    upper_soft = jax.nn.softmax(hidden, axis=-1)
    lower_soft = jax.nn.softmax(-hidden, axis=-1)
    return (rounded(jnp.concatenate([upper_soft, lower_soft], -1)), upper_soft, lower_soft)

def feature_grad(inputs, upper_soft, lower_soft, upstream):
    feat_width = upper_soft.shape[-1]
    upper_grad = upstream[..., :feat_width]
    lower_grad = upstream[..., feat_width:]
    inner_grad = upper_soft * (upper_grad - lax.optimization_barrier(jnp.sum(upper_grad * upper_soft, -1, keepdims=True)))
    inner_grad = inner_grad - lower_soft * (lower_grad - lax.optimization_barrier(jnp.sum(lower_grad * lower_soft, -1, keepdims=True)))
    return jnp.einsum('thd,thf->df', inputs.astype(jnp.float32), rounded(inner_grad), precision=highest_precision)

def head_group(queries, keys, values, target, map_q, map_k):
    spans = TOKENS // WINDOW
    heads_here = queries.shape[1]
    phi_q, q_upper, q_lower = features(queries, map_q)
    phi_k, k_upper, k_lower = features(keys, map_k)

    def blocked(array_in):
        return array_in.reshape((spans, WINDOW) + array_in.shape[1:])

    def earlier(array_in):
        return jnp.concatenate([jnp.zeros_like(array_in[:1]), array_in[:-1]], 0)
    block_q = blocked(queries.astype(jnp.float32))
    block_k = blocked(keys.astype(jnp.float32))
    block_v = blocked(values.astype(jnp.float32))
    block_t = blocked(target.astype(jnp.float32))
    block_pq = blocked(phi_q)
    block_pk = blocked(phi_k)
    span_ids = jnp.arange(spans, dtype=jnp.int32)
    row_pos = lax.broadcasted_iota(jnp.int32, (1, WINDOW, 2 * WINDOW), 1)
    col_pos = lax.broadcasted_iota(jnp.int32, (1, WINDOW, 2 * WINDOW), 2)

    def forward(carry_in, inputs):
        states, key_sums = carry_in
        q_now, k_now, v_now, t_now, pq_now, pk_now, k_prev, v_prev, pk_prev, span_index = inputs
        near_k = jnp.concatenate([k_prev, k_now], 0)
        near_v = jnp.concatenate([v_prev, v_now], 0)
        near_p = jnp.concatenate([pk_prev, pk_now], 0)
        key_live = (span_index > 0) | (col_pos >= WINDOW)
        in_window = (col_pos > row_pos) & (col_pos <= row_pos + WINDOW) & key_live
        in_far = (col_pos <= row_pos) & key_live
        scores = jnp.einsum('thd,shd->hts', q_now, near_k, precision=highest_precision) * DH ** (-0.5)
        top_score = lax.optimization_barrier(jnp.max(jnp.where(in_window, scores, -jnp.inf), axis=-1))
        damping = jnp.exp(-top_score)
        kernel = jnp.einsum('thf,shf->hts', pq_now, near_p, precision=highest_precision)
        weight = jnp.where(in_window, jnp.exp(scores - top_score[..., None]), 0.0)
        weight = weight + jnp.where(in_far, damping[..., None] * kernel, 0.0)
        damp_rows = damping.T
        numerator = jnp.einsum('hts,shd->thd', rounded(weight), near_v, precision=highest_precision)
        numerator = numerator + damp_rows[..., None] * jnp.einsum('thf,hfd->thd', pq_now, states, precision=highest_precision)
        denominator = lax.optimization_barrier(jnp.sum(weight, -1)).T + damp_rows * jnp.einsum('thf,hf->th', pq_now, key_sums, precision=highest_precision)
        output = numerator / denominator[..., None]
        d_out = 2.0 * (output - t_now) / TOKENS
        d_numer = d_out / denominator[..., None]
        d_denom = -lax.optimization_barrier(jnp.sum(d_out * output, -1)) / denominator
        d_weight = jnp.einsum('thd,shd->hts', rounded(d_numer), near_v, precision=highest_precision) + d_denom.T[..., None]
        far_grad = rounded(jnp.where(in_far, damping[..., None] * d_weight, 0.0))
        d_phi_q = jnp.einsum('hts,shf->thf', far_grad, near_p, precision=highest_precision)
        d_phi_q = d_phi_q + damp_rows[..., None] * (jnp.einsum('thd,hfd->thf', d_numer, states, precision=highest_precision) + d_denom[..., None] * key_sums[None])
        d_near = jnp.einsum('hts,thf->shf', far_grad, pq_now, precision=highest_precision)
        state_grad = rounded(damp_rows[..., None] * d_numer)
        rate_term = damp_rows * d_denom
        states = states + jnp.einsum('shf,shd->hfd', pk_prev, v_prev, precision=highest_precision)
        key_sums = key_sums + lax.optimization_barrier(jnp.sum(pk_prev, 0))
        return ((states, key_sums), (output, d_phi_q, d_near[:WINDOW], d_near[WINDOW:], state_grad, rate_term))
    zero_state = jnp.zeros((heads_here, 2 * FEAT, DH), jnp.float32)
    zero_sum = jnp.zeros((heads_here, 2 * FEAT), jnp.float32)
    inputs_all = (block_q, block_k, block_v, block_t, block_pq, block_pk, earlier(block_k), earlier(block_v), earlier(block_pk), span_ids)
    final_carry, stacked = lax.scan(forward, (zero_state, zero_sum), inputs_all)
    outputs, d_phi_q, d_prev, d_cur, state_grads, rate_terms = stacked

    def backward(carry_in, inputs):
        near_acc, far_acc, near_sum, far_sum = carry_in
        pq_now, grad_now, rate_now, v_now = inputs
        key_grad = jnp.einsum('shd,hfd->shf', v_now, far_acc, precision=highest_precision) + far_sum[None]
        step_states = jnp.einsum('thf,thd->hfd', pq_now, grad_now, precision=highest_precision)
        step_sums = jnp.einsum('th,thf->hf', rate_now, pq_now, precision=highest_precision)
        return ((near_acc + step_states, near_acc, near_sum + step_sums, near_sum), key_grad)
    back_carry, key_grads = lax.scan(backward, (zero_state, zero_state, zero_sum, zero_sum), (block_pq, state_grads, rate_terms, block_v), reverse=True)
    d_phi_k = d_cur + jnp.concatenate([d_prev[1:], jnp.zeros_like(d_prev[:1])], 0) + key_grads
    grad_q = feature_grad(queries, q_upper, q_lower, d_phi_q.reshape(TOKENS, heads_here, 2 * FEAT))
    grad_k = feature_grad(keys, k_upper, k_lower, d_phi_k.reshape(TOKENS, heads_here, 2 * FEAT))
    return (outputs.reshape(TOKENS, heads_here, DH), grad_q, grad_k)

def reference(queries, keys, values, target, map_q, map_k):
    group_heads = 16 if HEADS % 16 == 0 else HEADS
    groups = HEADS // group_heads

    def split_heads(array_in):
        return array_in.reshape(TOKENS, groups, group_heads, DH).transpose(1, 0, 2, 3)

    def run_group(inputs):
        return head_group(inputs[0], inputs[1], inputs[2], inputs[3], map_q, map_k)
    outputs, grads_q, grads_k = lax.map(run_group, (split_heads(queries), split_heads(keys), split_heads(values), split_heads(target)))
    hybrid = outputs.transpose(1, 0, 2, 3).reshape(TOKENS, HEADS, DH).astype(jnp.bfloat16)
    return (hybrid, lax.optimization_barrier(jnp.sum(grads_q, 0)), lax.optimization_barrier(jnp.sum(grads_k, 0)))
```

```python
import functools

import jax
import jax.numpy as jnp
from jax import lax
from jax.experimental import pallas as pl
from jax.experimental.pallas import tpu as pltpu
from jax.sharding import PartitionSpec as P

WINDOW = 64
FEAT = 64
PLANE = 16
ROWS = 136
MESH = pl.DeviceIdType.MESH
F32 = jnp.float32
BF16 = jnp.bfloat16
VMEM_LIMIT = 56 * 1024 * 1024


def dot_nn(a, b):
    return lax.dot_general(a, b, (((1,), (0,)), ((), ())), preferred_element_type=F32)


def dot_nt(a, b):
    return lax.dot_general(a, b, (((1,), (1,)), ((), ())), preferred_element_type=F32)


def dot_tn(a, b):
    return lax.dot_general(a, b, (((0,), (0,)), ((), ())), preferred_element_type=F32)


def split(x):
    high = x.astype(BF16)
    return high, (x - high.astype(F32)).astype(BF16)


def left_half(shape):
    return lax.broadcasted_iota(jnp.int32, shape, len(shape) - 1) < FEAT


def features(x, pair_map):
    hidden = dot_nn(x, pair_map)
    left = left_half(hidden.shape)
    top_left = jnp.max(jnp.where(left, hidden, -jnp.inf), -1, keepdims=True)
    top_right = jnp.max(jnp.where(left, -jnp.inf, hidden), -1, keepdims=True)
    e = jnp.exp(hidden - jnp.where(left, top_left, top_right))
    sum_left = jnp.sum(jnp.where(left, e, 0.0), -1, keepdims=True)
    sum_right = jnp.sum(jnp.where(left, 0.0, e), -1, keepdims=True)
    return e * jnp.where(left, 1.0 / sum_left, 1.0 / sum_right)


def feature_grad(x, soft, upstream):
    left = left_half(soft.shape)
    product = soft * upstream
    inner_left = jnp.sum(jnp.where(left, product, 0.0), -1, keepdims=True)
    inner_right = jnp.sum(jnp.where(left, 0.0, product), -1, keepdims=True)
    part = soft * (upstream - jnp.where(left, inner_left, inner_right))
    u = part - pltpu.roll(part, FEAT, 1)
    return dot_tn(x, u.astype(BF16))


def head_rows(ref, head, rows, heads):
    return ref[pl.ds(head, rows, stride=heads), :]


def widen(src, dst):
    dst[...] = src[...].astype(F32)


def key_kernel(heads, k_ref, v_ref, map_ref, state_ref, soft_ref, kh_ref, vh_ref, k_wide, v_wide):
    rows = k_ref.shape[0] // heads
    widen(k_ref, k_wide)
    widen(v_ref, v_wide)
    pair_map = map_ref[...]

    def step(head, carry):
        k = head_rows(k_wide, head, rows, heads).astype(BF16)
        v = head_rows(v_wide, head, rows, heads).astype(BF16)
        kh_ref[head] = k
        vh_ref[head] = v
        soft = features(k, pair_map)
        soft_ref[head] = soft
        phi = soft.astype(BF16)
        state_ref[head, :128, :] = dot_tn(phi, v)
        state_ref[head, 128:, :] = jnp.broadcast_to(
            jnp.sum(phi.astype(F32), 0, keepdims=True), (ROWS - 128, 128)
        )
        return carry

    lax.fori_loop(0, heads, step, 0)


def main_kernel(
    heads, total_tokens, q_ref, t_ref, k_ref, v_ref, softk_ref, hk_ref, hv_ref, p_ref, mq_ref, mk_ref,
    out_ref, g_ref, gq_ref, near_ref, back_ref, q_wide, t_wide, hk_wide, hv_wide, out_wide,
):
    rows = q_ref.shape[0] // heads
    w = WINDOW
    has_prior = lax.axis_index("seq") > 0
    widen(q_ref, q_wide)
    widen(t_ref, t_wide)
    widen(hk_ref, hk_wide)
    widen(hv_ref, hv_wide)
    map_q = mq_ref[...]
    map_k = mk_ref[...]
    gq_ref[...] = jnp.zeros_like(gq_ref)
    row = lax.broadcasted_iota(jnp.int32, (w, 2 * w), 0)
    col = lax.broadcasted_iota(jnp.int32, (w, 2 * w), 1)
    scale = 128 ** (-0.5)

    def step(head, carry):
        q = head_rows(q_wide, head, rows, heads).astype(BF16)
        target = head_rows(t_wide, head, rows, heads)
        k, v = k_ref[head], v_ref[head]
        hk = head_rows(hk_wide, head, w, heads).astype(BF16)
        hv = head_rows(hv_wide, head, w, heads).astype(BF16)
        soft_q = features(q, map_q)
        phi_q = soft_q.astype(BF16)
        phi_k = softk_ref[head].astype(BF16)
        phi_h = jnp.where(has_prior, features(hk, map_k), 0.0).astype(BF16)
        state1 = p_ref[head, :128, :]
        sum1 = p_ref[head, 128:129, :]
        state0 = state1 - dot_tn(phi_h, hv)
        sum0 = sum1 - jnp.sum(phi_h.astype(F32), 0, keepdims=True)
        d_phi, near, gstate, gsum = [], [], [], []
        for c in range(2):
            if c == 0:
                kn = jnp.concatenate([hk, k[:w]], 0)
                vn = jnp.concatenate([hv, v[:w]], 0)
                pn = jnp.concatenate([phi_h, phi_k[:w]], 0)
                state, ksum = state0, sum0
                live = (col >= w) | has_prior
                in_window = (col > row) & (col <= row + w) & live
                in_far = (col <= row) & live
            else:
                kn, vn, pn = k, v, phi_k
                state, ksum = state1, sum1
                in_window = (col > row) & (col <= row + w)
                in_far = col <= row
            qb = q[c * w : (c + 1) * w]
            pq = phi_q[c * w : (c + 1) * w]
            tb = target[c * w : (c + 1) * w]
            scores = jnp.where(in_window, dot_nt(qb, kn) * scale, -jnp.inf)
            top = jnp.max(scores, -1, keepdims=True)
            damping = jnp.exp(-top)
            weight = jnp.exp(scores - top) + jnp.where(in_far, damping * dot_nt(pq, pn), 0.0)
            state_high, state_low = split(state)
            state_num = dot_nn(pq, state_high) + dot_nn(pq, state_low)
            state_den = jnp.sum(pq.astype(F32) * ksum, -1, keepdims=True)
            numer = dot_nn(weight.astype(BF16), vn) + damping * state_num
            denom = jnp.sum(weight, -1, keepdims=True) + damping * state_den
            inverse = 1.0 / denom
            output = numer * inverse
            out_wide[pl.ds(c * w * heads + head, w, stride=heads), :] = output
            d_out = (output - tb) * (2.0 / total_tokens)
            d_numer = d_out * inverse
            d_denom = -jnp.sum(d_out * output, -1, keepdims=True) * inverse
            dn_high, dn_low = split(d_numer)
            d_weight = dot_nt(dn_high, vn) + d_denom
            far_grad = jnp.where(in_far, damping * d_weight, 0.0).astype(BF16)
            through = dot_nt(dn_high, state_high) + dot_nt(dn_high, state_low) + dot_nt(dn_low, state_high)
            d_phi.append(dot_nn(far_grad, pn) + damping * (through + d_denom * ksum))
            near.append(dot_tn(far_grad, pq))
            grad = (damping * d_numer).astype(BF16)
            gstate.append(dot_tn(pq, grad))
            gsum.append(jnp.sum(damping * d_denom * pq.astype(F32), 0, keepdims=True))
        gq_ref[...] += feature_grad(q, soft_q, jnp.concatenate(d_phi, 0))
        g_ref[head, :128, :] = gstate[0] + gstate[1]
        g_ref[head, 128:, :] = jnp.broadcast_to(gsum[0] + gsum[1], (ROWS - 128, 128))
        near_ref[head, :w, :] = near[0][w:] + near[1][:w]
        near_ref[head, w:, :] = near[1][w:]
        first_high, first_low = split(gstate[0])
        back_ref[head] = near[0][:w] - (dot_nt(hv, first_high) + dot_nt(hv, first_low) + gsum[0])
        return carry

    lax.fori_loop(0, heads, step, 0)
    out_ref[...] = out_wide[...].astype(BF16)


def last_kernel(heads, later_ref, near_ref, back_ref, k_ref, v_ref, softk_ref, gq_ref, out_ref):
    w = WINDOW
    out_ref[...] = jnp.zeros_like(out_ref)

    def step(head, carry):
        v, k = v_ref[head], k_ref[head]
        high, low = split(later_ref[head, :128, :])
        near = near_ref[head]
        near = jnp.concatenate([near[:w], near[w:] + back_ref[head]], 0)
        d_phi = near + dot_nt(v, high) + dot_nt(v, low) + later_ref[head, 128:129, :]
        out_ref[...] += feature_grad(k, softk_ref[head], d_phi)
        return carry

    lax.fori_loop(0, heads, step, 0)
    out_ref[...] = jnp.where(left_half(out_ref.shape), gq_ref[...], -out_ref[...])


def scan_kernel(reverse, x_ref, out_ref, parts, ztotals, send1, recv1, sendz, recvz, send2, recv2):
    me = lax.axis_index("seq")
    layers = lax.axis_size("seq") // PLANE
    z, p = me // PLANE, me % PLANE

    barrier = pltpu.get_barrier_semaphore()

    def greet(i, carry):
        pl.semaphore_signal(
            barrier, inc=1, device_id={"seq": z * PLANE + (p + i) % PLANE}, device_id_type=MESH
        )
        return carry

    lax.fori_loop(1, PLANE, greet, 0)
    for i in range(1, layers):
        pl.semaphore_signal(
            barrier, inc=1, device_id={"seq": ((z + i) % layers) * PLANE + p}, device_id_type=MESH
        )
    pl.semaphore_wait(barrier, PLANE - 1 + layers - 1)

    def up(i):
        to = (p + i) % PLANE
        return pltpu.make_async_remote_copy(
            src_ref=x_ref.at[to], dst_ref=parts.at[p], send_sem=send1.at[to], recv_sem=recv1.at[p],
            device_id={"seq": z * PLANE + to}, device_id_type=MESH,
        )

    def up_from(k):
        return pltpu.make_async_remote_copy(
            src_ref=x_ref.at[k], dst_ref=parts.at[k], send_sem=send1.at[k], recv_sem=recv1.at[k],
            device_id={"seq": z * PLANE + k}, device_id_type=MESH,
        )

    def start_up(i, carry):
        up(i).start()
        return carry

    lax.fori_loop(1, PLANE, start_up, 0)
    parts[p] = x_ref[p]

    def gather(i, total):
        k = PLANE - 1 - i if reverse else i

        @pl.when(k != p)
        def _():
            up_from(k).wait_recv()

        part = parts[k]
        parts[k] = total
        return total + part

    total = lax.fori_loop(0, PLANE, gather, jnp.zeros(x_ref.shape[1:], F32))
    ztotals[z] = total

    def across(i, to):
        other = (z + i) % layers
        return pltpu.make_async_remote_copy(
            src_ref=ztotals.at[z], dst_ref=ztotals.at[z if to else other],
            send_sem=sendz.at[other], recv_sem=recvz.at[z if to else other],
            device_id={"seq": other * PLANE + p}, device_id_type=MESH,
        )

    for i in range(1, layers):
        across(i, True).start()
    for i in range(1, layers):
        across(i, False).wait_recv()
    base = jnp.zeros(x_ref.shape[1:], F32)
    for k in range(layers):
        reached = k > z if reverse else k < z
        base = base + jnp.where(reached, ztotals[k], 0.0)

    def down(k, into):
        return pltpu.make_async_remote_copy(
            src_ref=parts.at[k], dst_ref=out_ref.at[into], send_sem=send2.at[k], recv_sem=recv2.at[into],
            device_id={"seq": z * PLANE + k}, device_id_type=MESH,
        )

    def start_down(i, carry):
        to = (p + i) % PLANE
        parts[to] = parts[to] + base
        down(to, p).start()
        return carry

    lax.fori_loop(1, PLANE, start_down, 0)
    out_ref[p] = parts[p] + base

    def finish(i, carry):
        k = (p + i) % PLANE
        down(k, k).wait_recv()
        down(k, k).wait_send()
        up_from(k).wait_send()
        return carry

    lax.fori_loop(1, PLANE, finish, 0)
    for i in range(1, layers):
        across(i, True).wait_send()


def sum_kernel(x_ref, out_ref, parts, totals, send1, recv1, sendz, recvz, send2, recv2):
    me, core = lax.axis_index("seq"), lax.axis_index("head")
    layers = lax.axis_size("seq") // PLANE
    cores = lax.axis_size("head")
    others = layers * cores
    z, p = me // PLANE, me % PLANE
    here = z * cores + core
    rows = x_ref.shape[0] // PLANE

    def rows_of(k):
        return pl.ds(pl.multiple_of(k * rows, rows), rows)

    def beyond(i):
        at = (here + i) % others
        return at, {"seq": (at // cores) * PLANE + p, "head": at % cores}

    barrier = pltpu.get_barrier_semaphore()

    def greet(i, carry):
        pl.semaphore_signal(
            barrier, inc=1, device_id={"seq": z * PLANE + (p + i) % PLANE}, device_id_type=MESH
        )
        return carry

    lax.fori_loop(1, PLANE, greet, 0)

    def greet_beyond(i, carry):
        pl.semaphore_signal(barrier, inc=1, device_id=beyond(i)[1], device_id_type=MESH)
        return carry

    lax.fori_loop(1, others, greet_beyond, 0)
    pl.semaphore_wait(barrier, PLANE - 1 + others - 1)

    def up(k, into):
        return pltpu.make_async_remote_copy(
            src_ref=x_ref.at[rows_of(k)], dst_ref=parts.at[into], send_sem=send1.at[k], recv_sem=recv1.at[into],
            device_id={"seq": z * PLANE + k}, device_id_type=MESH,
        )

    def start_up(i, carry):
        up((p + i) % PLANE, p).start()
        return carry

    lax.fori_loop(1, PLANE, start_up, 0)
    parts[p] = x_ref[rows_of(p)]

    def gather(k, total):
        @pl.when(k != p)
        def _():
            up(k, k).wait_recv()

        return total + parts[k]

    zero = jnp.zeros((rows, x_ref.shape[1]), F32)
    totals[here] = lax.fori_loop(0, PLANE, gather, zero)

    def across(i, to):
        at, device = beyond(i)
        into = here if to else at
        return pltpu.make_async_remote_copy(
            src_ref=totals.at[here], dst_ref=totals.at[into], send_sem=sendz.at[at], recv_sem=recvz.at[into],
            device_id=device, device_id_type=MESH,
        )

    def start_across(i, carry):
        across(i, True).start()
        return carry

    def await_across(i, carry):
        across(i, False).wait_recv()
        across(i, False).wait_send()
        return carry

    lax.fori_loop(1, others, start_across, 0)
    lax.fori_loop(1, others, await_across, 0)
    result = zero
    for k in range(others):
        result = result + totals[k]
    out_ref[rows_of(p)] = result

    def down(k, into):
        return pltpu.make_async_remote_copy(
            src_ref=out_ref.at[rows_of(p)], dst_ref=out_ref.at[rows_of(into)],
            send_sem=send2.at[k], recv_sem=recv2.at[into],
            device_id={"seq": z * PLANE + k}, device_id_type=MESH,
        )

    def start_down(i, carry):
        down((p + i) % PLANE, p).start()
        return carry

    lax.fori_loop(1, PLANE, start_down, 0)

    def finish(i, carry):
        k = (p + i) % PLANE
        down(k, k).wait_recv()
        down(k, k).wait_send()
        up(k, k).wait_send()
        return carry

    lax.fori_loop(1, PLANE, finish, 0)


def in_vmem(count):
    return [pl.BlockSpec(memory_space=pltpu.VMEM)] * count


def call(kernel, outs, scratch, args, **params):
    shapes = [jax.ShapeDtypeStruct(shape, dtype) for shape, dtype in outs]
    return pl.pallas_call(
        kernel,
        out_shape=shapes,
        in_specs=in_vmem(len(args)),
        out_specs=in_vmem(len(outs)),
        scratch_shapes=scratch,
        compiler_params=pltpu.CompilerParams(vmem_limit_bytes=VMEM_LIMIT, **params),
    )(*args)


def scan(x, reverse, collective_id):
    layers = lax.axis_size("seq") // PLANE
    dma = pltpu.SemaphoreType.DMA
    return call(
        functools.partial(scan_kernel, reverse),
        [(x.shape, F32)],
        [
            pltpu.VMEM(x.shape, F32),
            pltpu.VMEM((layers,) + x.shape[1:], F32),
            dma((PLANE,)), dma((PLANE,)), dma((layers,)), dma((layers,)), dma((PLANE,)), dma((PLANE,)),
        ],
        (x,),
        collective_id=collective_id,
        has_side_effects=True,
    )[0]


def sum_all(x, collective_id):
    others = lax.axis_size("seq") // PLANE * lax.axis_size("head")
    part = (x.shape[0] // PLANE, x.shape[1])
    dma = pltpu.SemaphoreType.DMA
    return call(
        sum_kernel,
        [(x.shape, F32)],
        [
            pltpu.VMEM((PLANE,) + part, F32),
            pltpu.VMEM((others,) + part, F32),
            dma((PLANE,)), dma((PLANE,)), dma((others,)), dma((others,)), dma((PLANE,)), dma((PLANE,)),
        ],
        (x,),
        collective_id=collective_id,
        has_side_effects=True,
    )[0]


def shifted(value, steps):
    count = lax.axis_size("seq")
    first, last = max(0, -steps), min(count, count - steps)
    return lax.ppermute(value, "seq", [(source, source + steps) for source in range(first, last)])


def per_device(queries, keys, values, target, map_q, map_k):
    rows, heads, size = queries.shape
    total_tokens = rows * lax.axis_size("seq")
    flat = (rows * heads, size)
    halo = (WINDOW * heads, size)
    pair_q = jnp.concatenate([map_q, -map_q], 1)
    pair_k = jnp.concatenate([map_k, -map_k], 1)
    edge = rows - WINDOW
    halo_keys, halo_values = shifted((keys[edge:], values[edge:]), 1)
    state, soft_k, k_heads, v_heads = call(
        functools.partial(key_kernel, heads),
        [
            ((heads, ROWS, size), F32),
            ((heads, rows, size), F32),
            ((heads, rows, size), BF16),
            ((heads, rows, size), BF16),
        ],
        [pltpu.VMEM(flat, F32), pltpu.VMEM(flat, F32)],
        (keys.reshape(flat), values.reshape(flat), pair_k),
    )
    prior = scan(state, False, 0)
    hybrid, gstate, grad_q, near, back = call(
        functools.partial(main_kernel, heads, total_tokens),
        [
            (flat, BF16),
            ((heads, ROWS, size), F32),
            ((size, size), F32),
            ((heads, rows, size), F32),
            ((heads, WINDOW, size), F32),
        ],
        [pltpu.VMEM(flat, F32), pltpu.VMEM(flat, F32), pltpu.VMEM(halo, F32), pltpu.VMEM(halo, F32), pltpu.VMEM(flat, F32)],
        (
            queries.reshape(flat), target.reshape(flat), k_heads, v_heads, soft_k,
            halo_keys.reshape(halo), halo_values.reshape(halo), prior, pair_q, pair_k,
        ),
    )
    returned = shifted(back, -1)
    later = scan(gstate, True, 1)
    (packed,) = call(
        functools.partial(last_kernel, heads),
        [((size, size), F32)],
        [],
        (later, near, returned, k_heads, v_heads, soft_k, grad_q),
    )
    summed = sum_all(packed, 2)
    return hybrid.reshape(rows, heads, size), summed[:, :FEAT], summed[:, FEAT:]


def solution(mesh):
    tokens = P("seq", "head", None)
    return jax.shard_map(
        per_device,
        mesh=mesh,
        in_specs=(tokens, tokens, tokens, tokens, P(), P()),
        out_specs=(tokens, P(), P()),
        check_vma=False,
    )
```

```python
import functools

import jax
import jax.numpy as jnp
from jax import lax
from jax.experimental import pallas as pl
from jax.experimental.pallas import tpu as pltpu
from jax.sharding import PartitionSpec as P

WINDOW = 64
FEAT = 64
PLANE = 16
ROWS = 136
MESH = pl.DeviceIdType.MESH
F32 = jnp.float32
BF16 = jnp.bfloat16
VMEM_LIMIT = 56 * 1024 * 1024


def dot_nn(a, b):
    return lax.dot_general(a, b, (((1,), (0,)), ((), ())), preferred_element_type=F32)


def dot_nt(a, b):
    return lax.dot_general(a, b, (((1,), (1,)), ((), ())), preferred_element_type=F32)


def dot_tn(a, b):
    return lax.dot_general(a, b, (((0,), (0,)), ((), ())), preferred_element_type=F32)


def split(x):
    high = x.astype(BF16)
    return high, (x - high.astype(F32)).astype(BF16)


def left_half(shape):
    return lax.broadcasted_iota(jnp.int32, shape, len(shape) - 1) < FEAT


def features(x, pair_map):
    hidden = dot_nn(x, pair_map)
    left = left_half(hidden.shape)
    top_left = jnp.max(jnp.where(left, hidden, -jnp.inf), -1, keepdims=True)
    top_right = jnp.max(jnp.where(left, -jnp.inf, hidden), -1, keepdims=True)
    e = jnp.exp(hidden - jnp.where(left, top_left, top_right))
    sum_left = jnp.sum(jnp.where(left, e, 0.0), -1, keepdims=True)
    sum_right = jnp.sum(jnp.where(left, 0.0, e), -1, keepdims=True)
    return e * jnp.where(left, 1.0 / sum_left, 1.0 / sum_right)


def feature_grad(x, soft, upstream):
    left = left_half(soft.shape)
    product = soft * upstream
    inner_left = jnp.sum(jnp.where(left, product, 0.0), -1, keepdims=True)
    inner_right = jnp.sum(jnp.where(left, 0.0, product), -1, keepdims=True)
    part = soft * (upstream - jnp.where(left, inner_left, inner_right))
    u = part - pltpu.roll(part, FEAT, 1)
    return dot_tn(x, u.astype(BF16))


def head_rows(ref, head, rows, heads):
    return ref[pl.ds(head, rows, stride=heads), :]


def widen(src, dst):
    dst[...] = src[...].astype(F32)


class Scan:
    def __init__(self, x, parts, totals, result, sems, reverse):
        self.x, self.parts, self.totals, self.result, self.reverse = x, parts, totals, result, reverse
        self.send_up, self.recv_up, self.send_z, self.recv_z, self.send_down, self.recv_down = sems
        me = lax.axis_index("seq")
        self.layers = lax.axis_size("seq") // PLANE
        self.z, self.p = me // PLANE, me % PLANE

    def in_plane(self, k):
        return {"seq": self.z * PLANE + k}

    def up(self, k, into):
        return pltpu.make_async_remote_copy(
            src_ref=self.x.at[k], dst_ref=self.parts.at[into],
            send_sem=self.send_up.at[k], recv_sem=self.recv_up.at[into],
            device_id=self.in_plane(k), device_id_type=MESH,
        )

    def down(self, k, into):
        return pltpu.make_async_remote_copy(
            src_ref=self.parts.at[k], dst_ref=self.result.at[into],
            send_sem=self.send_down.at[k], recv_sem=self.recv_down.at[into],
            device_id=self.in_plane(k), device_id_type=MESH,
        )

    def across(self, i, to):
        other = (self.z + i) % self.layers
        into = self.z if to else other
        return pltpu.make_async_remote_copy(
            src_ref=self.totals.at[self.z], dst_ref=self.totals.at[into],
            send_sem=self.send_z.at[other], recv_sem=self.recv_z.at[into],
            device_id={"seq": other * PLANE + self.p}, device_id_type=MESH,
        )

    def give(self, head):
        @pl.when(head != self.p)
        def _():
            self.up(head, self.p).start()

        @pl.when(head == self.p)
        def _():
            self.parts[head] = self.x[head]

    def collect(self):
        def gather(i, total):
            k = PLANE - 1 - i if self.reverse else i

            @pl.when(k != self.p)
            def _():
                self.up(k, k).wait_recv()

            part = self.parts[k]
            self.parts[k] = total
            return total + part

        self.totals[self.z] = lax.fori_loop(0, PLANE, gather, jnp.zeros(self.x.shape[1:], F32))
        for i in range(1, self.layers):
            self.across(i, True).start()

    def spread(self):
        for i in range(1, self.layers):
            self.across(i, False).wait_recv()
        base = jnp.zeros(self.x.shape[1:], F32)
        for k in range(self.layers):
            reached = k > self.z if self.reverse else k < self.z
            base = base + jnp.where(reached, self.totals[k], 0.0)

        def start(i, carry):
            to = (self.p + i) % PLANE
            self.parts[to] = self.parts[to] + base
            self.down(to, self.p).start()
            return carry

        lax.fori_loop(1, PLANE, start, 0)
        self.result[self.p] = self.parts[self.p] + base

    def receive(self, head):
        @pl.when(head != self.p)
        def _():
            self.down(head, head).wait_recv()

    def finish(self):
        def wait(i, carry):
            k = (self.p + i) % PLANE
            self.down(k, k).wait_send()
            self.up(k, k).wait_send()
            return carry

        lax.fori_loop(1, PLANE, wait, 0)
        for i in range(1, self.layers):
            self.across(i, True).wait_send()


class Total:
    def __init__(self, x, out, parts, totals, sems):
        self.x, self.out, self.parts, self.totals = x, out, parts, totals
        self.send1, self.recv1, self.send_z, self.recv_z, self.send2, self.recv2 = sems
        me, core = lax.axis_index("seq"), lax.axis_index("head")
        self.cores = lax.axis_size("head")
        self.others = lax.axis_size("seq") // PLANE * self.cores
        self.z, self.p = me // PLANE, me % PLANE
        self.here = self.z * self.cores + core
        self.rows = x.shape[0] // PLANE

    def rows_of(self, k):
        return pl.ds(pl.multiple_of(k * self.rows, self.rows), self.rows)

    def beyond(self, i):
        at = (self.here + i) % self.others
        return at, {"seq": (at // self.cores) * PLANE + self.p, "head": at % self.cores}

    def up(self, k, into):
        return pltpu.make_async_remote_copy(
            src_ref=self.x.at[self.rows_of(k)], dst_ref=self.parts.at[into],
            send_sem=self.send1.at[k], recv_sem=self.recv1.at[into],
            device_id={"seq": self.z * PLANE + k}, device_id_type=MESH,
        )

    def across(self, i, to):
        at, device = self.beyond(i)
        into = self.here if to else at
        return pltpu.make_async_remote_copy(
            src_ref=self.totals.at[self.here], dst_ref=self.totals.at[into],
            send_sem=self.send_z.at[at], recv_sem=self.recv_z.at[into],
            device_id=device, device_id_type=MESH,
        )

    def down(self, k, into):
        return pltpu.make_async_remote_copy(
            src_ref=self.out.at[self.rows_of(self.p)], dst_ref=self.out.at[self.rows_of(into)],
            send_sem=self.send2.at[k], recv_sem=self.recv2.at[into],
            device_id={"seq": self.z * PLANE + k}, device_id_type=MESH,
        )

    def give(self):
        def start(i, carry):
            self.up((self.p + i) % PLANE, self.p).start()
            return carry

        lax.fori_loop(1, PLANE, start, 0)
        self.parts[self.p] = self.x[self.rows_of(self.p)]

    def collect(self):
        def gather(k, total):
            @pl.when(k != self.p)
            def _():
                self.up(k, k).wait_recv()

            return total + self.parts[k]

        zero = jnp.zeros((self.rows, self.x.shape[1]), F32)
        self.totals[self.here] = lax.fori_loop(0, PLANE, gather, zero)

        def start(i, carry):
            self.across(i, True).start()
            return carry

        lax.fori_loop(1, self.others, start, 0)

    def spread(self):
        def wait(i, carry):
            self.across(i, False).wait_recv()
            return carry

        lax.fori_loop(1, self.others, wait, 0)
        result = self.totals[0]
        for k in range(1, self.others):
            result = result + self.totals[k]
        self.out[self.rows_of(self.p)] = result

        def start(i, carry):
            self.down((self.p + i) % PLANE, self.p).start()
            return carry

        lax.fori_loop(1, PLANE, start, 0)

    def finish(self):
        def wait(i, carry):
            k = (self.p + i) % PLANE
            self.down(k, k).wait_recv()
            self.down(k, k).wait_send()
            self.up(k, k).wait_send()
            return carry

        lax.fori_loop(1, PLANE, wait, 0)

        def wait_across(i, carry):
            self.across(i, False).wait_send()
            return carry

        lax.fori_loop(1, self.others, wait_across, 0)


def greet():
    me, core = lax.axis_index("seq"), lax.axis_index("head")
    count, cores = lax.axis_size("seq"), lax.axis_size("head")
    others = count // PLANE * cores
    z, p = me // PLANE, me % PLANE
    barrier = pltpu.get_barrier_semaphore()

    def plane(i, carry):
        device = {"seq": z * PLANE + (p + i) % PLANE}
        pl.semaphore_signal(barrier, inc=1, device_id=device, device_id_type=MESH)
        return carry

    def beyond(i, carry):
        at = (z * cores + core + i) % others
        device = {"seq": (at // cores) * PLANE + p, "head": at % cores}
        pl.semaphore_signal(barrier, inc=1, device_id=device, device_id_type=MESH)
        return carry

    lax.fori_loop(1, PLANE, plane, 0)
    lax.fori_loop(1, others, beyond, 0)
    for other in ((me + 1) % count, (me + count - 1) % count):
        pl.semaphore_signal(barrier, inc=1, device_id={"seq": other}, device_id_type=MESH)
    pl.semaphore_wait(barrier, PLANE - 1 + others - 1 + 2)


def kernel(
    heads, total_tokens, q_ref, k_ref, v_ref, t_ref, mq_ref, mk_ref, out_ref, grad_ref,
    q_wide, k_wide, v_wide, t_wide, out_wide, halo, hk_wide, hv_wide,
    ext_k, ext_v, ext_phi, q_heads, soft_q, soft_k, numer_near, denom_near, damp, halo_state, halo_sum,
    d_numer_all, d_denom_all, first_grad, first_sum, near, back, back_in,
    x1, parts1, totals1, prior, x2, parts2, totals2, later, gq, gk, packed, parts3, totals3,
    send_halo, recv_halo, send_back, recv_back, *sems,
):
    w = WINDOW
    rows = 2 * w
    me, count = lax.axis_index("seq"), lax.axis_size("seq")
    p = me % PLANE
    has_prior = me > 0
    has_later = me < count - 1
    forward = Scan(x1, parts1, totals1, prior, sems[0:6], False)
    backward = Scan(x2, parts2, totals2, later, sems[6:12], True)
    final = Total(packed, grad_ref, parts3, totals3, sems[12:18])
    greet()

    def halo_copy(i, ref):
        return pltpu.make_async_remote_copy(
            src_ref=ref.at[pl.ds(w * heads, w * heads)], dst_ref=halo.at[i],
            send_sem=send_halo.at[i], recv_sem=recv_halo.at[i],
            device_id={"seq": (me + 1) % count}, device_id_type=MESH,
        )

    def back_copy(pair):
        return pltpu.make_async_remote_copy(
            src_ref=back.at[pl.ds(2 * pair, 2)], dst_ref=back_in.at[pl.ds(2 * pair, 2)],
            send_sem=send_back.at[pair], recv_sem=recv_back.at[pair],
            device_id={"seq": (me + count - 1) % count}, device_id_type=MESH,
        )

    @pl.when(has_later)
    def _():
        halo_copy(0, k_ref).start()
        halo_copy(1, v_ref).start()

    widen(k_ref, k_wide)
    widen(v_ref, v_wide)
    map_q, map_k = mq_ref[...], mk_ref[...]

    def key_part(i, carry):
        pair = [(p + 2 * i) % PLANE, (p + 2 * i + 1) % PLANE]
        for head in pair:
            k = head_rows(k_wide, head, rows, heads).astype(BF16)
            v = head_rows(v_wide, head, rows, heads).astype(BF16)
            soft = features(k, map_k)
            phi = soft.astype(BF16)
            ext_k[head, w:, :] = k
            ext_v[head, w:, :] = v
            ext_phi[head, w:, :] = phi
            soft_k[head] = soft
            x1[head, :128, :] = dot_tn(phi, v)
            x1[head, 128:, :] = jnp.broadcast_to(jnp.sum(phi.astype(F32), 0, keepdims=True), (ROWS - 128, 128))
        for head in pair:
            forward.give(head)
        return carry

    lax.fori_loop(0, heads // 2, key_part, 0)

    widen(q_ref, q_wide)
    widen(t_ref, t_wide)

    @pl.when(has_prior)
    def _():
        halo_copy(0, k_ref).wait_recv()
        halo_copy(1, v_ref).wait_recv()

    @pl.when(jnp.logical_not(has_prior))
    def _():
        halo[...] = jnp.zeros_like(halo)

    hk_wide[...] = halo[0].astype(F32)
    hv_wide[...] = halo[1].astype(F32)
    row = lax.broadcasted_iota(jnp.int32, (w, rows), 0)
    col = lax.broadcasted_iota(jnp.int32, (w, rows), 1)
    scale = 128 ** (-0.5)

    def masks(c):
        in_window = (col > row) & (col <= row + w)
        in_far = col <= row
        if c:
            return in_window, in_far
        live = (col >= w) | has_prior
        return in_window & live, in_far & live

    def near_part(i, carry):
        for head in (2 * i, 2 * i + 1):
            hk = head_rows(hk_wide, head, w, heads).astype(BF16)
            hv = head_rows(hv_wide, head, w, heads).astype(BF16)
            phi_h = jnp.where(has_prior, features(hk, map_k), 0.0).astype(BF16)
            ext_k[head, :w, :] = hk
            ext_v[head, :w, :] = hv
            ext_phi[head, :w, :] = phi_h
            halo_state[head] = dot_tn(phi_h, hv)
            halo_sum[head] = jnp.broadcast_to(jnp.sum(phi_h.astype(F32), 0, keepdims=True), (8, 128))
            q = head_rows(q_wide, head, rows, heads).astype(BF16)
            q_heads[head] = q
            soft = features(q, map_q)
            soft_q[head] = soft
            phi_q = soft.astype(BF16)
            for c in range(2):
                block, span = pl.ds(c * w, w), pl.ds(c * w, rows)
                in_window, in_far = masks(c)
                scores = dot_nt(q[c * w : (c + 1) * w], ext_k[head, span, :]) * scale
                scores = jnp.where(in_window, scores, -jnp.inf)
                top = jnp.max(scores, -1, keepdims=True)
                damping = jnp.exp(-top)
                far = damping * dot_nt(phi_q[c * w : (c + 1) * w], ext_phi[head, span, :])
                weight = jnp.exp(scores - top) + jnp.where(in_far, far, 0.0)
                numer_near[head, block, :] = dot_nn(weight.astype(BF16), ext_v[head, span, :])
                denom_near[head, block, :] = jnp.sum(weight, -1, keepdims=True)
                damp[head, block, :] = damping

        @pl.when(i == 4)
        def _():
            forward.collect()

        @pl.when(i == 6)
        def _():
            forward.spread()

        return carry

    lax.fori_loop(0, heads // 2, near_part, 0)

    def states(head):
        one = prior[head, :128, :]
        zero = one - halo_state[head]
        sum_one = prior[head, 128:129, :]
        return (zero, one), (sum_one - halo_sum[head, 0:1, :], sum_one)

    def middle_part(i, carry):
        pair = [(p + 2 * PLANE - 2 * i) % PLANE, (p + 2 * PLANE - 2 * i - 1) % PLANE]
        for head in pair:
            forward.receive(head)
        for head in pair:
            state, ksum = states(head)
            phi_q = soft_q[head].astype(BF16)
            grads = []
            for c in range(2):
                block = pl.ds(c * w, w)
                pq = phi_q[c * w : (c + 1) * w]
                wide_pq = pq.astype(F32)
                damping = damp[head, block, :]
                high, low = split(state[c])
                state_den = jnp.sum(wide_pq * ksum[c], -1, keepdims=True)
                numer = numer_near[head, block, :] + damping * (dot_nn(pq, high) + dot_nn(pq, low))
                inverse = 1.0 / (denom_near[head, block, :] + damping * state_den)
                output = numer * inverse
                at = pl.ds(c * w * heads + head, w, stride=heads)
                out_wide[at, :] = output
                d_out = (output - t_wide[at, :]) * (2.0 / total_tokens)
                d_numer = d_out * inverse
                d_denom = -jnp.sum(d_out * output, -1, keepdims=True) * inverse
                d_numer_all[head, block, :] = d_numer
                d_denom_all[head, block, :] = d_denom
                g_state = dot_tn(pq, (damping * d_numer).astype(BF16))
                g_sum = jnp.sum(damping * d_denom * wide_pq, 0, keepdims=True)
                grads.append((g_state, g_sum))
            first_grad[head] = grads[0][0]
            first_sum[head] = jnp.broadcast_to(grads[0][1], (8, 128))
            x2[head, :128, :] = grads[0][0] + grads[1][0]
            x2[head, 128:, :] = jnp.broadcast_to(grads[0][1] + grads[1][1], (ROWS - 128, 128))
        for head in pair:
            backward.give(head)
        return carry

    lax.fori_loop(0, heads // 2, middle_part, 0)
    gq[...] = jnp.zeros_like(gq)
    gk[...] = jnp.zeros_like(gk)

    def far_part(i, carry):
        for head in (2 * i, 2 * i + 1):
            state, ksum = states(head)
            soft = soft_q[head]
            phi_q = soft.astype(BF16)
            d_phi, d_near = [], []
            for c in range(2):
                block, span = pl.ds(c * w, w), pl.ds(c * w, rows)
                in_far = masks(c)[1]
                damping = damp[head, block, :]
                d_numer = d_numer_all[head, block, :]
                d_denom = d_denom_all[head, block, :]
                high, low = split(state[c])
                dn_high, dn_low = split(d_numer)
                d_weight = dot_nt(dn_high, ext_v[head, span, :]) + d_denom
                far_grad = jnp.where(in_far, damping * d_weight, 0.0).astype(BF16)
                through = dot_nt(dn_high, high) + dot_nt(dn_high, low) + dot_nt(dn_low, high)
                d_phi.append(dot_nn(far_grad, ext_phi[head, span, :]) + damping * (through + d_denom * ksum[c]))
                d_near.append(dot_tn(far_grad, phi_q[c * w : (c + 1) * w]))
            high, low = split(first_grad[head])
            hv = ext_v[head, :w, :]
            back[head] = d_near[0][:w] - (dot_nt(hv, high) + dot_nt(hv, low) + first_sum[head, 0:1, :])
            near[head, :w, :] = d_near[0][w:] + d_near[1][:w]
            near[head, w:, :] = d_near[1][w:]
            gq[...] += feature_grad(q_heads[head], soft, jnp.concatenate(d_phi, 0))

        @pl.when(has_prior)
        def _():
            back_copy(i).start()

        @pl.when(i == 2)
        def _():
            backward.collect()

        @pl.when(i == 4)
        def _():
            backward.spread()

        return carry

    lax.fori_loop(0, heads // 2, far_part, 0)
    out_ref[...] = out_wide[...].astype(BF16)

    @pl.when(has_later)
    def _():
        def wait(i, carry):
            back_copy(i).wait_recv()
            return carry

        lax.fori_loop(0, heads // 2, wait, 0)

    @pl.when(jnp.logical_not(has_later))
    def _():
        back_in[...] = jnp.zeros_like(back_in)

    def last_part(i, carry):
        pair = [(p + 2 * PLANE - 2 * i) % PLANE, (p + 2 * PLANE - 2 * i - 1) % PLANE]
        for head in pair:
            backward.receive(head)
        for head in pair:
            v, k = ext_v[head, w:, :], ext_k[head, w:, :]
            high, low = split(later[head, :128, :])
            d_near = near[head]
            d_near = jnp.concatenate([d_near[:w], d_near[w:] + back_in[head]], 0)
            d_phi = d_near + dot_nt(v, high) + dot_nt(v, low) + later[head, 128:129, :]
            gk[...] += feature_grad(k, soft_k[head], d_phi)
        return carry

    lax.fori_loop(0, heads // 2, last_part, 0)
    packed[...] = jnp.where(left_half(packed.shape), gq[...], -gk[...])
    final.give()
    final.collect()
    final.spread()
    final.finish()
    forward.finish()
    backward.finish()

    @pl.when(has_later)
    def _():
        halo_copy(0, k_ref).wait_send()
        halo_copy(1, v_ref).wait_send()

    @pl.when(has_prior)
    def _():
        def wait(i, carry):
            back_copy(i).wait_send()
            return carry

        lax.fori_loop(0, heads // 2, wait, 0)


def per_device(queries, keys, values, target, map_q, map_k):
    rows, heads, size = queries.shape
    total_tokens = rows * lax.axis_size("seq")
    layers = lax.axis_size("seq") // PLANE
    others = layers * lax.axis_size("head")
    flat = (rows * heads, size)
    half = (WINDOW * heads, size)
    wide = pltpu.VMEM(flat, F32)
    tiles = pltpu.VMEM((heads, rows, size), F32)
    halves = pltpu.VMEM((heads, WINDOW, size), F32)
    ext = pltpu.VMEM((heads, rows + WINDOW, size), BF16)
    column = pltpu.VMEM((heads, rows, 1), F32)
    row = pltpu.VMEM((heads, 8, size), F32)
    square = pltpu.VMEM((heads, size, size), F32)
    slices = pltpu.VMEM((heads, ROWS, size), F32)
    layer = pltpu.VMEM((layers, ROWS, size), F32)
    grad = pltpu.VMEM((size, size), F32)
    dma = pltpu.SemaphoreType.DMA
    in_plane, scan_z, sum_z = dma((PLANE,)), dma((layers,)), dma((others,))
    scan_sems = [in_plane, in_plane, scan_z, scan_z, in_plane, in_plane]
    pair_q = jnp.concatenate([map_q, -map_q], 1)
    pair_k = jnp.concatenate([map_k, -map_k], 1)
    vmem = pl.BlockSpec(memory_space=pltpu.VMEM)
    hybrid, grads = pl.pallas_call(
        functools.partial(kernel, heads, total_tokens),
        out_shape=[jax.ShapeDtypeStruct(flat, BF16), jax.ShapeDtypeStruct((size, size), F32)],
        in_specs=[vmem] * 6,
        out_specs=[vmem] * 2,
        scratch_shapes=[
            wide, wide, wide, wide, wide, pltpu.VMEM((2,) + half, BF16), pltpu.VMEM(half, F32), pltpu.VMEM(half, F32),
            ext, ext, ext, pltpu.VMEM((heads, rows, size), BF16), tiles, tiles, tiles, column, column, square, row,
            tiles, column, square, row, tiles, halves, halves,
            slices, slices, layer, slices, slices, slices, layer, slices, grad, grad, grad,
            pltpu.VMEM((PLANE, size // PLANE, size), F32), pltpu.VMEM((others, size // PLANE, size), F32),
            dma((2,)), dma((2,)), dma((heads // 2,)), dma((heads // 2,)),
            *scan_sems, *scan_sems, in_plane, in_plane, sum_z, sum_z, in_plane, in_plane,
        ],
        compiler_params=pltpu.CompilerParams(vmem_limit_bytes=VMEM_LIMIT, collective_id=0, has_side_effects=True),
    )(queries.reshape(flat), keys.reshape(flat), values.reshape(flat), target.reshape(flat), pair_q, pair_k)
    return hybrid.reshape(rows, heads, size), grads[:, :FEAT], grads[:, FEAT:]


def solution(mesh):
    tokens = P("seq", "head", None)
    return jax.shard_map(
        per_device,
        mesh=mesh,
        in_specs=(tokens, tokens, tokens, tokens, P(), P()),
        out_specs=(tokens, P(), P()),
        check_vma=False,
    )
```

```python
import functools

import jax
import jax.numpy as jnp
from jax import lax
from jax.experimental import pallas as pl
from jax.experimental.pallas import tpu as pltpu
from jax.sharding import PartitionSpec as P

WINDOW = 64
FEAT = 64
PLANE = 16
ROWS = 136
MESH = pl.DeviceIdType.MESH
F32 = jnp.float32
BF16 = jnp.bfloat16
VMEM_LIMIT = 56 * 1024 * 1024


def dot_nn(a, b):
    return lax.dot_general(a, b, (((1,), (0,)), ((), ())), preferred_element_type=F32)


def dot_nt(a, b):
    return lax.dot_general(a, b, (((1,), (1,)), ((), ())), preferred_element_type=F32)


def dot_tn(a, b):
    return lax.dot_general(a, b, (((0,), (0,)), ((), ())), preferred_element_type=F32)


def split(x):
    high = x.astype(BF16)
    return high, (x - high.astype(F32)).astype(BF16)


def left_half(shape):
    return lax.broadcasted_iota(jnp.int32, shape, len(shape) - 1) < FEAT


def features(x, pair_map):
    hidden = dot_nt(x, pair_map)
    left = left_half(hidden.shape)
    top_left = jnp.max(jnp.where(left, hidden, -jnp.inf), -1, keepdims=True)
    top_right = jnp.max(jnp.where(left, -jnp.inf, hidden), -1, keepdims=True)
    e = jnp.exp(hidden - jnp.where(left, top_left, top_right))
    sum_left = jnp.sum(jnp.where(left, e, 0.0), -1, keepdims=True)
    sum_right = jnp.sum(jnp.where(left, 0.0, e), -1, keepdims=True)
    return e * jnp.where(left, 1.0 / sum_left, 1.0 / sum_right)


def feature_grad(x, soft, upstream):
    left = left_half(soft.shape)
    product = soft * upstream
    inner_left = jnp.sum(jnp.where(left, product, 0.0), -1, keepdims=True)
    inner_right = jnp.sum(jnp.where(left, 0.0, product), -1, keepdims=True)
    part = soft * (upstream - jnp.where(left, inner_left, inner_right))
    u = part - pltpu.roll(part, FEAT, 1)
    return dot_tn(u.astype(BF16), x)


def head_rows(ref, head, rows, heads):
    return ref[pl.ds(head, rows, stride=heads), :]


def widen(src, dst):
    dst[...] = src[...].astype(F32)


def wrapped(k, count):
    return jnp.where(k >= count, k - count, k)


def await_bytes(ref, sem):
    pltpu.make_async_copy(ref, ref, sem).wait()


class Scan:
    def __init__(self, x, parts, totals, result, sems, reverse):
        self.x, self.parts, self.totals, self.result, self.reverse = x, parts, totals, result, reverse
        self.send_up, self.recv_up, self.send_z, self.recv_z, self.send_down, self.recv_down = sems
        me = lax.axis_index("seq")
        self.layers = lax.axis_size("seq") // PLANE
        self.z, self.p = me // PLANE, me % PLANE

    def in_plane(self, k):
        return {"seq": self.z * PLANE + k}

    def give(self, head):
        @pl.when(head != self.p)
        def _():
            pltpu.make_async_remote_copy(
                src_ref=self.x.at[head], dst_ref=self.parts.at[self.p], send_sem=self.send_up, recv_sem=self.recv_up,
                device_id=self.in_plane(head), device_id_type=MESH,
            ).start()

        @pl.when(head == self.p)
        def _():
            pltpu.make_async_copy(self.x.at[head], self.parts.at[self.p], self.recv_up).start()

    def collect(self):
        await_bytes(self.parts, self.recv_up)

        def gather(i, total):
            k = PLANE - 1 - i if self.reverse else i
            part = self.parts[k]
            self.parts[k] = total
            return total + part

        self.totals[self.z] = lax.fori_loop(0, PLANE, gather, jnp.zeros(self.x.shape[1:], F32))
        for i in range(1, self.layers):
            other = wrapped(self.z + i, self.layers)
            pltpu.make_async_remote_copy(
                src_ref=self.totals.at[self.z], dst_ref=self.totals.at[self.z],
                send_sem=self.send_z, recv_sem=self.recv_z,
                device_id={"seq": other * PLANE + self.p}, device_id_type=MESH,
            ).start()

    def down(self, k, into):
        return pltpu.make_async_remote_copy(
            src_ref=self.parts.at[k], dst_ref=self.result.at[into],
            send_sem=self.send_down, recv_sem=self.recv_down.at[into],
            device_id=self.in_plane(k), device_id_type=MESH,
        )

    def spread(self):
        await_bytes(self.totals.at[pl.ds(0, self.layers - 1)], self.recv_z)
        base = jnp.zeros(self.x.shape[1:], F32)
        for k in range(self.layers):
            reached = k > self.z if self.reverse else k < self.z
            base = base + jnp.where(reached, self.totals[k], 0.0)

        def start(i, carry):
            to = wrapped(self.p + i, PLANE)
            self.parts[to] = self.parts[to] + base
            self.down(to, self.p).start()
            return carry

        lax.fori_loop(1, PLANE, start, 0)
        self.result[self.p] = self.parts[self.p] + base

    def receive(self, head):
        @pl.when(head != self.p)
        def _():
            self.down(head, head).wait_recv()

    def finish(self):
        most = pl.ds(0, PLANE - 1)
        await_bytes(self.x.at[most], self.send_up)
        await_bytes(self.parts.at[most], self.send_down)
        await_bytes(self.totals.at[pl.ds(0, self.layers - 1)], self.send_z)


class Total:
    def __init__(self, x, out, parts, totals, sems):
        self.x, self.out, self.parts, self.totals = x, out, parts, totals
        self.send1, self.recv1, self.send_z, self.recv_z, self.send2, self.recv2 = sems
        me, core = lax.axis_index("seq"), lax.axis_index("head")
        self.cores = lax.axis_size("head")
        self.others = lax.axis_size("seq") // PLANE * self.cores
        self.z, self.p = me // PLANE, me % PLANE
        self.here = self.z * self.cores + core

    def in_plane(self, k):
        return {"seq": self.z * PLANE + k}

    def give(self):
        for i in range(1, PLANE):
            to = wrapped(self.p + i, PLANE)
            pltpu.make_async_remote_copy(
                src_ref=self.x.at[to], dst_ref=self.parts.at[self.p], send_sem=self.send1, recv_sem=self.recv1,
                device_id=self.in_plane(to), device_id_type=MESH,
            ).start()
        pltpu.make_async_copy(self.x.at[self.p], self.parts.at[self.p], self.recv1).start()

    def collect(self):
        await_bytes(self.parts, self.recv1)
        self.totals[self.here] = jnp.sum(self.parts[...], 0)
        for i in range(1, self.others):
            at = wrapped(self.here + i, self.others)
            pltpu.make_async_remote_copy(
                src_ref=self.totals.at[self.here], dst_ref=self.totals.at[self.here],
                send_sem=self.send_z, recv_sem=self.recv_z,
                device_id={"seq": (at // self.cores) * PLANE + self.p, "head": at % self.cores}, device_id_type=MESH,
            ).start()

    def spread(self):
        await_bytes(self.totals.at[pl.ds(0, self.others - 1)], self.recv_z)
        self.out[self.p] = jnp.sum(self.totals[...], 0)
        for i in range(1, PLANE):
            pltpu.make_async_remote_copy(
                src_ref=self.out.at[self.p], dst_ref=self.out.at[self.p], send_sem=self.send2, recv_sem=self.recv2,
                device_id=self.in_plane(wrapped(self.p + i, PLANE)), device_id_type=MESH,
            ).start()

    def finish(self):
        most = pl.ds(0, PLANE - 1)
        await_bytes(self.out.at[most], self.recv2)
        await_bytes(self.out.at[most], self.send2)
        await_bytes(self.x.at[most], self.send1)
        await_bytes(self.totals.at[pl.ds(0, self.others - 1)], self.send_z)


def greet():
    me, core = lax.axis_index("seq"), lax.axis_index("head")
    count, cores = lax.axis_size("seq"), lax.axis_size("head")
    others = count // PLANE * cores
    z, p = me // PLANE, me % PLANE
    barrier = pltpu.get_barrier_semaphore()

    def plane(i, carry):
        device = {"seq": z * PLANE + (p + i) % PLANE}
        pl.semaphore_signal(barrier, inc=1, device_id=device, device_id_type=MESH)
        return carry

    def beyond(i, carry):
        at = (z * cores + core + i) % others
        device = {"seq": (at // cores) * PLANE + p, "head": at % cores}
        pl.semaphore_signal(barrier, inc=1, device_id=device, device_id_type=MESH)
        return carry

    lax.fori_loop(1, PLANE, plane, 0)
    lax.fori_loop(1, others, beyond, 0)
    for other in ((me + 1) % count, (me + count - 1) % count):
        pl.semaphore_signal(barrier, inc=1, device_id={"seq": other}, device_id_type=MESH)
    return PLANE - 1 + others - 1 + 2


def kernel(
    heads, total_tokens, q_ref, k_ref, v_ref, t_ref, mq_ref, mk_ref, out_ref, grad_ref,
    q_in, k_in, v_in, t_in, q_wide, k_wide, v_wide, t_wide, halo, hk_wide, hv_wide,
    ext_k, ext_v, ext_phi, q_heads, soft_q, soft_k, numer_near, denom_near, damp, halo_state, halo_sum,
    d_numer_all, d_denom_all, first_grad, first_sum, near, back, back_in,
    x1, parts1, totals1, prior, x2, parts2, totals2, later, gq, gk, packed, parts3, totals3,
    load, send_halo, recv_halo, send_back, recv_back, *sems,
):
    w = WINDOW
    rows = 2 * w
    greeted = greet()
    loads = [
        pltpu.make_async_copy(source, target, load.at[i])
        for i, (source, target) in enumerate([(k_ref, k_in), (v_ref, v_in), (q_ref, q_in), (t_ref, t_in)])
    ]
    for copy in loads:
        copy.start()
    me, count = lax.axis_index("seq"), lax.axis_size("seq")
    p = me % PLANE
    has_prior = me > 0
    has_later = me < count - 1
    forward = Scan(x1, parts1, totals1, prior, sems[0:6], False)
    backward = Scan(x2, parts2, totals2, later, sems[6:12], True)
    final = Total(packed, grad_ref, parts3, totals3, sems[12:18])

    def halo_copy(i, ref):
        return pltpu.make_async_remote_copy(
            src_ref=ref.at[pl.ds(w * heads, w * heads)], dst_ref=halo.at[i],
            send_sem=send_halo.at[i], recv_sem=recv_halo.at[i],
            device_id={"seq": (me + 1) % count}, device_id_type=MESH,
        )

    def back_copy(pair):
        return pltpu.make_async_remote_copy(
            src_ref=back.at[pl.ds(2 * pair, 2)], dst_ref=back_in.at[pl.ds(2 * pair, 2)],
            send_sem=send_back.at[pair], recv_sem=recv_back.at[pair],
            device_id={"seq": (me + count - 1) % count}, device_id_type=MESH,
        )

    loads[0].wait()
    loads[1].wait()
    pl.semaphore_wait(pltpu.get_barrier_semaphore(), greeted)

    @pl.when(has_later)
    def _():
        halo_copy(0, k_in).start()
        halo_copy(1, v_in).start()

    widen(k_in, k_wide)
    widen(v_in, v_wide)
    map_q, map_k = (
        jnp.concatenate([ref[...], (-ref[...].astype(F32)).astype(BF16)], 0) for ref in (mq_ref, mk_ref)
    )

    def key_part(i, carry):
        pair = [(p + 2 * i) % PLANE, (p + 2 * i + 1) % PLANE]
        for head in pair:
            k = head_rows(k_wide, head, rows, heads).astype(BF16)
            v = head_rows(v_wide, head, rows, heads).astype(BF16)
            soft = features(k, map_k)
            phi = soft.astype(BF16)
            ext_k[head, w:, :] = k
            ext_v[head, w:, :] = v
            ext_phi[head, w:, :] = phi
            soft_k[head] = soft
            x1[head, :128, :] = dot_tn(phi, v)
            x1[head, 128:, :] = jnp.broadcast_to(jnp.sum(phi.astype(F32), 0, keepdims=True), (ROWS - 128, 128))
        for head in pair:
            forward.give(head)
        return carry

    lax.fori_loop(0, heads // 2, key_part, 0)

    loads[2].wait()
    loads[3].wait()
    widen(q_in, q_wide)
    widen(t_in, t_wide)
    row = lax.broadcasted_iota(jnp.int32, (w, rows), 0)
    col = lax.broadcasted_iota(jnp.int32, (w, rows), 1)
    scale = 128 ** (-0.5)

    def masks(c):
        in_window = (col > row) & (col <= row + w)
        in_far = col <= row
        if c:
            return in_window, in_far
        live = (col >= w) | has_prior
        return in_window & live, in_far & live

    def near_block(head, c, q, phi_q):
        block, span = pl.ds(c * w, w), pl.ds(c * w, rows)
        in_window, in_far = masks(c)
        scores = jnp.where(in_window, dot_nt(q, ext_k[head, span, :]) * scale, -jnp.inf)
        top = jnp.max(scores, -1, keepdims=True)
        damping = jnp.exp(-top)
        far = damping * dot_nt(phi_q, ext_phi[head, span, :])
        weight = jnp.exp(scores - top) + jnp.where(in_far, far, 0.0)
        numer_near[head, block, :] = dot_nn(weight.astype(BF16), ext_v[head, span, :])
        denom_near[head, block, :] = jnp.sum(weight, -1, keepdims=True)
        damp[head, block, :] = damping

    def own_part(i, carry):
        for head in (2 * i, 2 * i + 1):
            q = head_rows(q_wide, head, rows, heads).astype(BF16)
            q_heads[head] = q
            soft = features(q, map_q)
            soft_q[head] = soft
            near_block(head, 1, q[w:], soft[w:].astype(BF16))
        return carry

    lax.fori_loop(0, heads // 2, own_part, 0)

    @pl.when(has_prior)
    def _():
        halo_copy(0, k_in).wait_recv()
        halo_copy(1, v_in).wait_recv()

    @pl.when(jnp.logical_not(has_prior))
    def _():
        halo[...] = jnp.zeros_like(halo)

    hk_wide[...] = halo[0].astype(F32)
    hv_wide[...] = halo[1].astype(F32)

    def near_part(i, carry):
        for head in (2 * i, 2 * i + 1):
            hk = head_rows(hk_wide, head, w, heads).astype(BF16)
            hv = head_rows(hv_wide, head, w, heads).astype(BF16)
            phi_h = jnp.where(has_prior, features(hk, map_k), 0.0).astype(BF16)
            ext_k[head, :w, :] = hk
            ext_v[head, :w, :] = hv
            ext_phi[head, :w, :] = phi_h
            halo_state[head] = dot_tn(phi_h, hv)
            halo_sum[head] = jnp.broadcast_to(jnp.sum(phi_h.astype(F32), 0, keepdims=True), (8, 128))
            near_block(head, 0, q_heads[head, :w, :], soft_q[head, :w, :].astype(BF16))

        @pl.when(i == 4)
        def _():
            forward.collect()

        @pl.when(i == 7)
        def _():
            forward.spread()

        return carry

    lax.fori_loop(0, heads // 2, near_part, 0)

    def states(head):
        one = prior[head, :128, :]
        zero = one - halo_state[head]
        sum_one = prior[head, 128:129, :]
        return (zero, one), (sum_one - halo_sum[head, 0:1, :], sum_one)

    def middle_part(i, carry):
        pair = [(p + 2 * PLANE - 2 * i) % PLANE, (p + 2 * PLANE - 2 * i - 1) % PLANE]
        for head in pair:
            forward.receive(head)
        for head in pair:
            state, ksum = states(head)
            phi_q = soft_q[head].astype(BF16)
            grads = []
            for c in range(2):
                block = pl.ds(c * w, w)
                pq = phi_q[c * w : (c + 1) * w]
                wide_pq = pq.astype(F32)
                damping = damp[head, block, :]
                high, low = split(state[c])
                state_den = jnp.sum(wide_pq * ksum[c], -1, keepdims=True)
                numer = numer_near[head, block, :] + damping * (dot_nn(pq, high) + dot_nn(pq, low))
                inverse = 1.0 / (denom_near[head, block, :] + damping * state_den)
                output = numer * inverse
                at = pl.ds(c * w * heads + head, w, stride=heads)
                out_ref[at, :] = output
                d_out = (output - t_wide[at, :]) * (2.0 / total_tokens)
                d_numer = d_out * inverse
                d_denom = -jnp.sum(d_out * output, -1, keepdims=True) * inverse
                d_numer_all[head, block, :] = d_numer
                d_denom_all[head, block, :] = d_denom
                g_state = dot_tn(pq, (damping * d_numer).astype(BF16))
                g_sum = jnp.sum(damping * d_denom * wide_pq, 0, keepdims=True)
                grads.append((g_state, g_sum))
            first_grad[head] = grads[0][0]
            first_sum[head] = jnp.broadcast_to(grads[0][1], (8, 128))
            x2[head, :128, :] = grads[0][0] + grads[1][0]
            x2[head, 128:, :] = jnp.broadcast_to(grads[0][1] + grads[1][1], (ROWS - 128, 128))
        for head in pair:
            backward.give(head)
        return carry

    lax.fori_loop(0, heads // 2, middle_part, 0)
    gq[...] = jnp.zeros_like(gq)
    gk[...] = jnp.zeros_like(gk)

    def far_part(i, carry):
        for head in (2 * i, 2 * i + 1):
            state, ksum = states(head)
            soft = soft_q[head]
            phi_q = soft.astype(BF16)
            d_phi, d_near = [], []
            for c in range(2):
                block, span = pl.ds(c * w, w), pl.ds(c * w, rows)
                in_far = masks(c)[1]
                damping = damp[head, block, :]
                d_numer = d_numer_all[head, block, :]
                d_denom = d_denom_all[head, block, :]
                high, low = split(state[c])
                dn_high, dn_low = split(d_numer)
                d_weight = dot_nt(dn_high, ext_v[head, span, :]) + d_denom
                far_grad = jnp.where(in_far, damping * d_weight, 0.0).astype(BF16)
                through = dot_nt(dn_high, high) + dot_nt(dn_high, low) + dot_nt(dn_low, high)
                d_phi.append(dot_nn(far_grad, ext_phi[head, span, :]) + damping * (through + d_denom * ksum[c]))
                d_near.append(dot_tn(far_grad, phi_q[c * w : (c + 1) * w]))
            high, low = split(first_grad[head])
            hv = ext_v[head, :w, :]
            back[head] = d_near[0][:w] - (dot_nt(hv, high) + dot_nt(hv, low) + first_sum[head, 0:1, :])
            near[head, :w, :] = d_near[0][w:] + d_near[1][:w]
            near[head, w:, :] = d_near[1][w:]
            gq[...] += feature_grad(q_heads[head], soft, jnp.concatenate(d_phi, 0))

        @pl.when(has_prior)
        def _():
            back_copy(i).start()

        @pl.when(i == 2)
        def _():
            backward.collect()

        @pl.when(i == 4)
        def _():
            backward.spread()

        return carry

    lax.fori_loop(0, heads // 2, far_part, 0)

    @pl.when(has_later)
    def _():
        def wait(i, carry):
            back_copy(i).wait_recv()
            return carry

        lax.fori_loop(0, heads // 2, wait, 0)

    @pl.when(jnp.logical_not(has_later))
    def _():
        back_in[...] = jnp.zeros_like(back_in)

    def last_part(i, carry):
        pair = [(p + 2 * PLANE - 2 * i) % PLANE, (p + 2 * PLANE - 2 * i - 1) % PLANE]
        for head in pair:
            backward.receive(head)
        for head in pair:
            v, k = ext_v[head, w:, :], ext_k[head, w:, :]
            high, low = split(later[head, :128, :])
            d_near = near[head]
            d_near = jnp.concatenate([d_near[:w], d_near[w:] + back_in[head]], 0)
            d_phi = d_near + dot_nt(v, high) + dot_nt(v, low) + later[head, 128:129, :]
            gk[...] += feature_grad(k, soft_k[head], d_phi)
        return carry

    lax.fori_loop(0, heads // 2, last_part, 0)
    for k in range(PLANE):
        source = gq if k < PLANE // 2 else gk
        packed[k] = source[k % (PLANE // 2) * 8 : k % (PLANE // 2) * 8 + 8, :]
    final.give()
    final.collect()
    final.spread()
    final.finish()
    forward.finish()
    backward.finish()

    @pl.when(has_later)
    def _():
        halo_copy(0, k_in).wait_send()
        halo_copy(1, v_in).wait_send()

    @pl.when(has_prior)
    def _():
        def wait(i, carry):
            back_copy(i).wait_send()
            return carry

        lax.fori_loop(0, heads // 2, wait, 0)


def per_device(queries, keys, values, target, map_q, map_k):
    rows, heads, size = queries.shape
    total_tokens = rows * lax.axis_size("seq")
    layers = lax.axis_size("seq") // PLANE
    others = layers * lax.axis_size("head")
    flat = (rows * heads, size)
    half = (WINDOW * heads, size)
    wide = pltpu.VMEM(flat, F32)
    tiles = pltpu.VMEM((heads, rows, size), F32)
    halves = pltpu.VMEM((heads, WINDOW, size), F32)
    ext = pltpu.VMEM((heads, rows + WINDOW, size), BF16)
    column = pltpu.VMEM((heads, rows, 1), F32)
    row = pltpu.VMEM((heads, 8, size), F32)
    square = pltpu.VMEM((heads, size, size), F32)
    slices = pltpu.VMEM((heads, ROWS, size), F32)
    layer = pltpu.VMEM((layers, ROWS, size), F32)
    grad = pltpu.VMEM((size, size), F32)
    dma = pltpu.SemaphoreType.DMA
    one = dma(())
    scan_sems = [one, one, one, one, one, dma((PLANE,))]
    bf16_flat = pltpu.VMEM(flat, BF16)
    slice_rows = size // PLANE
    vmem = pl.BlockSpec(memory_space=pltpu.VMEM)
    hbm = pl.BlockSpec(memory_space=pl.ANY)
    output, grads = pl.pallas_call(
        functools.partial(kernel, heads, total_tokens),
        out_shape=[
            jax.ShapeDtypeStruct(flat, F32),
            jax.ShapeDtypeStruct((PLANE, slice_rows, size), F32),
        ],
        in_specs=[hbm] * 4 + [vmem] * 2,
        out_specs=[vmem] * 2,
        scratch_shapes=[
            bf16_flat, bf16_flat, bf16_flat, bf16_flat, wide, wide, wide, wide,
            pltpu.VMEM((2,) + half, BF16), pltpu.VMEM(half, F32), pltpu.VMEM(half, F32),
            ext, ext, ext, pltpu.VMEM((heads, rows, size), BF16), tiles, tiles, tiles, column, column, square, row,
            tiles, column, square, row, tiles, halves, halves,
            slices, slices, layer, slices, slices, slices, layer, slices, grad, grad,
            pltpu.VMEM((PLANE, slice_rows, size), F32), pltpu.VMEM((PLANE, slice_rows, size), F32),
            pltpu.VMEM((others, slice_rows, size), F32),
            dma((4,)), dma((2,)), dma((2,)), dma((heads // 2,)), dma((heads // 2,)),
            *scan_sems, *scan_sems, one, one, one, one, one, one,
        ],
        compiler_params=pltpu.CompilerParams(vmem_limit_bytes=VMEM_LIMIT, collective_id=0, has_side_effects=True),
    )(queries.reshape(flat), keys.reshape(flat), values.reshape(flat), target.reshape(flat), map_q.T, map_k.T)
    hybrid = output.astype(BF16).reshape(rows, heads, size)
    grads = grads.reshape(size, size)
    return hybrid, grads[:FEAT].T, grads[FEAT:].T


def solution(mesh):
    tokens = P("seq", "head", None)
    return jax.shard_map(
        per_device,
        mesh=mesh,
        in_specs=(tokens, tokens, tokens, tokens, P(), P()),
        out_specs=(tokens, P(), P()),
        check_vma=False,
    )
```

```python
import functools

import jax
import jax.numpy as jnp
from jax import lax
from jax.experimental import pallas as pl
from jax.experimental.pallas import tpu as pltpu
from jax.sharding import PartitionSpec as P

WINDOW = 64
FEAT = 64
PLANE = 16
ROWS = 136
MESH = pl.DeviceIdType.MESH
F32 = jnp.float32
BF16 = jnp.bfloat16
VMEM_LIMIT = 56 * 1024 * 1024


def dot_nn(a, b):
    return lax.dot_general(a, b, (((1,), (0,)), ((), ())), preferred_element_type=F32)


def dot_nt(a, b):
    return lax.dot_general(a, b, (((1,), (1,)), ((), ())), preferred_element_type=F32)


def dot_tn(a, b):
    return lax.dot_general(a, b, (((0,), (0,)), ((), ())), preferred_element_type=F32)


def split(x):
    high = x.astype(BF16)
    return high, (x - high.astype(F32)).astype(BF16)


def left_half(shape):
    return lax.broadcasted_iota(jnp.int32, shape, len(shape) - 1) < FEAT


def features(x, pair_map):
    hidden = dot_nt(x, pair_map)
    left = left_half(hidden.shape)
    top_left = jnp.max(jnp.where(left, hidden, -jnp.inf), -1, keepdims=True)
    top_right = jnp.max(jnp.where(left, -jnp.inf, hidden), -1, keepdims=True)
    e = jnp.exp(hidden - jnp.where(left, top_left, top_right))
    sum_left = jnp.sum(jnp.where(left, e, 0.0), -1, keepdims=True)
    sum_right = jnp.sum(jnp.where(left, 0.0, e), -1, keepdims=True)
    return e * jnp.where(left, 1.0 / sum_left, 1.0 / sum_right)


def feature_grad(x, soft, upstream):
    left = left_half(soft.shape)
    product = soft * upstream
    inner_left = jnp.sum(jnp.where(left, product, 0.0), -1, keepdims=True)
    inner_right = jnp.sum(jnp.where(left, 0.0, product), -1, keepdims=True)
    part = soft * (upstream - jnp.where(left, inner_left, inner_right))
    u = part - pltpu.roll(part, FEAT, 1)
    return dot_tn(u.astype(BF16), x)


def head_rows(ref, head, rows, heads):
    return ref[pl.ds(head, rows, stride=heads), :]


def widen(src, dst):
    dst[...] = src[...].astype(F32)


def wrapped(k, count):
    return jnp.where(k >= count, k - count, k)


def await_bytes(ref, sem):
    pltpu.make_async_copy(ref, ref, sem).wait()


class Across:
    def __init__(self, totals, send, recv, reverse):
        self.totals, self.send, self.recv, self.reverse = totals, send, recv, reverse
        me = lax.axis_index("seq")
        self.layers = lax.axis_size("seq") // PLANE
        self.z, self.p = me // PLANE, me % PLANE

    def give(self, total):
        self.totals[self.z] = total
        for i in range(1, self.layers):
            other = wrapped(self.z + i, self.layers)
            pltpu.make_async_remote_copy(
                src_ref=self.totals.at[self.z], dst_ref=self.totals.at[self.z], send_sem=self.send, recv_sem=self.recv,
                device_id={"seq": other * PLANE + self.p}, device_id_type=MESH,
            ).start()

    def base(self):
        await_bytes(self.totals.at[pl.ds(0, self.layers - 1)], self.recv)
        base = jnp.zeros(self.totals.shape[1:], F32)
        for k in range(self.layers):
            reached = k > self.z if self.reverse else k < self.z
            base = base + jnp.where(reached, self.totals[k], 0.0)
        return base

    def finish(self):
        await_bytes(self.totals.at[pl.ds(0, self.layers - 1)], self.send)


class Total:
    def __init__(self, x, out, parts, totals, sems):
        self.x, self.out, self.parts, self.totals = x, out, parts, totals
        self.send1, self.recv1, self.send_z, self.recv_z, self.send2, self.recv2 = sems
        me, core = lax.axis_index("seq"), lax.axis_index("head")
        self.cores = lax.axis_size("head")
        self.others = lax.axis_size("seq") // PLANE * self.cores
        self.z, self.p = me // PLANE, me % PLANE
        self.here = self.z * self.cores + core

    def in_plane(self, k):
        return {"seq": self.z * PLANE + k}

    def give(self):
        for i in range(1, PLANE):
            to = wrapped(self.p + i, PLANE)
            pltpu.make_async_remote_copy(
                src_ref=self.x.at[to], dst_ref=self.parts.at[self.p], send_sem=self.send1, recv_sem=self.recv1,
                device_id=self.in_plane(to), device_id_type=MESH,
            ).start()
        pltpu.make_async_copy(self.x.at[self.p], self.parts.at[self.p], self.recv1).start()

    def collect(self):
        await_bytes(self.parts, self.recv1)
        self.totals[self.here] = jnp.sum(self.parts[...], 0)
        for i in range(1, self.others):
            at = wrapped(self.here + i, self.others)
            pltpu.make_async_remote_copy(
                src_ref=self.totals.at[self.here], dst_ref=self.totals.at[self.here],
                send_sem=self.send_z, recv_sem=self.recv_z,
                device_id={"seq": (at // self.cores) * PLANE + self.p, "head": at % self.cores}, device_id_type=MESH,
            ).start()

    def spread(self):
        await_bytes(self.totals.at[pl.ds(0, self.others - 1)], self.recv_z)
        self.out[self.p] = jnp.sum(self.totals[...], 0)
        for i in range(1, PLANE):
            pltpu.make_async_remote_copy(
                src_ref=self.out.at[self.p], dst_ref=self.out.at[self.p], send_sem=self.send2, recv_sem=self.recv2,
                device_id=self.in_plane(wrapped(self.p + i, PLANE)), device_id_type=MESH,
            ).start()

    def finish(self):
        most = pl.ds(0, PLANE - 1)
        await_bytes(self.out.at[most], self.recv2)
        await_bytes(self.out.at[most], self.send2)
        await_bytes(self.x.at[most], self.send1)
        await_bytes(self.totals.at[pl.ds(0, self.others - 1)], self.send_z)


def greet():
    me, core = lax.axis_index("seq"), lax.axis_index("head")
    count, cores = lax.axis_size("seq"), lax.axis_size("head")
    others = count // PLANE * cores
    z, p = me // PLANE, me % PLANE
    barrier = pltpu.get_barrier_semaphore()

    def plane(i, carry):
        device = {"seq": z * PLANE + (p + i) % PLANE}
        pl.semaphore_signal(barrier, inc=1, device_id=device, device_id_type=MESH)
        return carry

    def beyond(i, carry):
        at = (z * cores + core + i) % others
        device = {"seq": (at // cores) * PLANE + p, "head": at % cores}
        pl.semaphore_signal(barrier, inc=1, device_id=device, device_id_type=MESH)
        return carry

    lax.fori_loop(1, PLANE, plane, 0)
    lax.fori_loop(1, others, beyond, 0)
    return PLANE - 1 + others - 1


def kernel(
    heads, total_tokens, q_ref, k_ref, v_ref, t_ref, mq_ref, mk_ref, out_ref, grad_ref,
    k_in, v_in, q_in, t_in, k_wide, v_wide, q_wide, t_wide, mine, held,
    phi_all, soft_q, soft_k, numer_near, denom_near, damp, state, halo_state, d_numer_all, d_denom_all,
    gstate, near, lead, total, totals1, totals2, out_send, out_held, gq, gk, packed, parts3, totals3,
    load, send, recv, send_halo, recv_halo, send_lead, recv_lead, send_out, recv_out, *sems,
):
    w = WINDOW
    rows = 2 * w
    chunks = PLANE
    K, V, Q, T = range(4)
    greeted = greet()
    arrays = [(k_ref, k_in, k_wide), (v_ref, v_in, v_wide), (q_ref, q_in, q_wide), (t_ref, t_in, t_wide)]
    loads = [pltpu.make_async_copy(source, into, load.at[i]) for i, (source, into, wide) in enumerate(arrays)]
    for copy in loads:
        copy.start()
    me = lax.axis_index("seq")
    layers = lax.axis_size("seq") // PLANE
    z, p = me // PLANE, me % PLANE
    has_prior = z > 0
    has_later = z < layers - 1
    forward = Across(totals1, sems[0], sems[1], False)
    backward = Across(totals2, sems[2], sems[3], True)
    final = Total(packed, grad_ref, parts3, totals3, sems[4:10])

    def in_plane(k):
        return {"seq": z * PLANE + k}

    halo_there = held.at[0, pl.ds(0, 2), pl.ds(w, w)]
    halo_copy = pltpu.make_async_remote_copy(
        src_ref=held.at[chunks, pl.ds(0, 2), pl.ds(w, w)], dst_ref=halo_there, send_sem=send_halo, recv_sem=recv_halo,
        device_id={"seq": jnp.where(has_later, z + 1, 0) * PLANE + p}, device_id_type=MESH,
    )
    lead_copy = pltpu.make_async_remote_copy(
        src_ref=lead.at[0], dst_ref=lead.at[chunks], send_sem=send_lead, recv_sem=recv_lead,
        device_id={"seq": jnp.where(has_prior, z - 1, layers - 1) * PLANE + p}, device_id_type=MESH,
    )

    for copy, (source, into, wide) in zip(loads, arrays):
        copy.wait()
        widen(into, wide)
    pl.semaphore_wait(pltpu.get_barrier_semaphore(), greeted)

    def give(i, carry):
        head = wrapped(p + i, PLANE)
        for j, (source, into, wide) in enumerate(arrays):
            mine[head, j] = head_rows(wide, head, rows, heads).astype(BF16)

        @pl.when(i > 0)
        def _():
            pltpu.make_async_remote_copy(
                src_ref=mine.at[head], dst_ref=held.at[p + 1], send_sem=send, recv_sem=recv.at[p],
                device_id=in_plane(head), device_id_type=MESH,
            ).start()

        @pl.when(i == 0)
        def _():
            pltpu.make_async_copy(mine.at[head], held.at[p + 1], recv.at[p]).start()

        return carry

    lax.fori_loop(0, heads, give, 0)

    map_q, map_k = (
        jnp.concatenate([ref[...], (-ref[...].astype(F32)).astype(BF16)], 0) for ref in (mq_ref, mk_ref)
    )
    row = lax.broadcasted_iota(jnp.int32, (w, rows), 0)
    col = lax.broadcasted_iota(jnp.int32, (w, rows), 1)
    scale = 128 ** (-0.5)
    total[...] = jnp.zeros_like(total)

    def masks(first):
        in_window = (col > row) & (col <= row + w)
        in_far = col <= row
        if not first:
            return in_window, in_far
        live = (col >= w) | has_prior
        return in_window & live, in_far & live

    def before(c):
        return jnp.where(c == 0, 1, c)

    def ext(ref, slot, c):
        return jnp.concatenate([ref[slot, w:, :], ref[c + 1, :w, :]], 0)

    def near_block(c, half, kn, vn, pn, first):
        block = pl.ds(half * w, w)
        in_window, in_far = masks(first)
        scores = jnp.where(in_window, dot_nt(held[c + 1, Q, block, :], kn) * scale, -jnp.inf)
        top = jnp.max(scores, -1, keepdims=True)
        damping = jnp.exp(-top)
        far = damping * dot_nt(soft_q[c, block, :].astype(BF16), pn)
        weight = jnp.exp(scores - top) + jnp.where(in_far, far, 0.0)
        numer_near[c, block, :] = dot_nn(weight.astype(BF16), vn)
        denom_near[c, block, :] = jnp.sum(weight, -1, keepdims=True)
        damp[c, block, :] = damping

    def first_block(c, slot, first=False):
        near_block(c, 0, ext(held.at[:, K], slot, c), ext(held.at[:, V], slot, c), ext(phi_all, slot, c), first)

    def own_part(i, carry):
        c1 = wrapped(p + PLANE - 2 * i, PLANE)
        c2 = wrapped(p + PLANE - 2 * i - 1, PLANE)
        for c in (c1, c2):
            await_bytes(held.at[c + 1], recv.at[c])

            @pl.when((c == chunks - 1) & has_later)
            def _():
                halo_copy.start()

        for c in (c1, c2):
            soft = features(held[c + 1, K], map_k)
            soft_k[c] = soft
            phi = soft.astype(BF16)
            phi_all[c + 1] = phi
            v = held[c + 1, V]
            for half in range(2):
                part = phi[half * w : (half + 1) * w]
                block_state = dot_tn(part, v[half * w : (half + 1) * w])
                block_sum = jnp.sum(part.astype(F32), 0, keepdims=True)
                state[2 * c + half, :128, :] = block_state
                state[2 * c + half, 128:, :] = jnp.broadcast_to(block_sum, (ROWS - 128, 128))
                total[:128, :] += block_state
                total[128:, :] += block_sum
            soft_q[c] = features(held[c + 1, Q], map_q)
            near_block(c, 1, held[c + 1, K], v, phi, False)
        first_block(c1, before(c1))

        @pl.when(i > 0)
        def _():
            c = wrapped(c1 + 1, PLANE)
            first_block(c, before(c))

        return carry

    lax.fori_loop(0, chunks // 2, own_part, 0)
    forward.give(total[...])
    final_chunk = wrapped(p + 1, PLANE)
    first_block(final_chunk, before(final_chunk))

    @pl.when(has_prior)
    def _():
        await_bytes(halo_there, recv_halo)

    @pl.when(jnp.logical_not(has_prior))
    def _():
        held[0, :2, w:, :] = jnp.zeros((2, w, 128), BF16)

    phi_halo = jnp.where(has_prior, features(held[0, K, w:, :], map_k), 0.0).astype(BF16)
    phi_all[0, w:, :] = phi_halo
    halo_state[:128, :] = dot_tn(phi_halo, held[0, V, w:, :])
    halo_state[128:, :] = jnp.broadcast_to(jnp.sum(phi_halo.astype(F32), 0, keepdims=True), (ROWS - 128, 128))
    first_block(0, 0, True)

    base = forward.base()

    def lead_states(b, carry):
        now, after = carry
        own = state[b]
        state[b] = now
        return after, after + own

    lax.fori_loop(0, 2 * chunks, lead_states, (base - halo_state[...], base))
    total[...] = jnp.zeros_like(total)

    def middle_part(i, carry):
        pair = (2 * i, 2 * i + 1)
        for c in pair:
            phi_q = soft_q[c].astype(BF16)
            target = held[c + 1, T].astype(F32)
            for half in range(2):
                block, span, b = pl.ds(half * w, w), slice(half * w, (half + 1) * w), 2 * c + half
                pq = phi_q[span]
                wide_pq = pq.astype(F32)
                damping = damp[c, block, :]
                high, low = split(state[b, :128, :])
                state_den = jnp.sum(wide_pq * state[b, 128:129, :], -1, keepdims=True)
                numer = numer_near[c, block, :] + damping * (dot_nn(pq, high) + dot_nn(pq, low))
                inverse = 1.0 / (denom_near[c, block, :] + damping * state_den)
                output = numer * inverse
                out_send[c, block, :] = output.astype(BF16)
                d_out = (output - target[span]) * (2.0 / total_tokens)
                d_numer = d_out * inverse
                d_denom = -jnp.sum(d_out * output, -1, keepdims=True) * inverse
                d_numer_all[c, block, :] = d_numer
                d_denom_all[c, block, :] = d_denom
                g_state = dot_tn(pq, (damping * d_numer).astype(BF16))
                g_sum = jnp.sum(damping * d_denom * wide_pq, 0, keepdims=True)
                gstate[b, :128, :] = g_state
                gstate[b, 128:, :] = jnp.broadcast_to(g_sum, (ROWS - 128, 128))
                total[:128, :] += g_state
                total[128:, :] += g_sum
        return carry

    lax.fori_loop(0, chunks // 2, middle_part, 0)
    backward.give(total[...])

    def give_out(i, carry):
        c = wrapped(p + i, PLANE)
        pltpu.make_async_remote_copy(
            src_ref=out_send.at[c], dst_ref=out_held.at[p], send_sem=send_out, recv_sem=recv_out,
            device_id=in_plane(c), device_id_type=MESH,
        ).start()
        return carry

    lax.fori_loop(1, PLANE, give_out, 0)
    pltpu.make_async_copy(out_send.at[p], out_held.at[p], recv_out).start()
    gq[...] = jnp.zeros_like(gq)
    gk[...] = jnp.zeros_like(gk)

    def far_part(i, carry):
        for c in (2 * i, 2 * i + 1):
            soft = soft_q[c]
            phi_q = soft.astype(BF16)
            d_phi, d_near = [], []
            for half in range(2):
                block, b = pl.ds(half * w, w), 2 * c + half
                if half:
                    in_far = masks(False)[1]
                    vn, pn = held[c + 1, V], phi_all[c + 1]
                else:
                    in_far = (col <= row) & ((col >= w) | has_prior | (c > 0))
                    vn, pn = ext(held.at[:, V], c, c), ext(phi_all, c, c)
                damping = damp[c, block, :]
                d_numer = d_numer_all[c, block, :]
                d_denom = d_denom_all[c, block, :]
                high, low = split(state[b, :128, :])
                dn_high, dn_low = split(d_numer)
                far_grad = damping * (dot_nt(dn_high, vn) + d_denom)
                far_grad = jnp.where(in_far, far_grad, 0.0).astype(BF16)
                through = dot_nt(dn_high, high) + dot_nt(dn_high, low) + dot_nt(dn_low, high)
                d_phi.append(dot_nn(far_grad, pn) + damping * (through + d_denom * state[b, 128:129, :]))
                d_near.append(dot_tn(far_grad, phi_q[half * w : (half + 1) * w]))
            lead[c] = d_near[0][:w]
            near[c, :w, :] = d_near[0][w:] + d_near[1][:w]
            near[c, w:, :] = d_near[1][w:]
            gq[...] += feature_grad(held[c + 1, Q], soft, jnp.concatenate(d_phi, 0))

        @pl.when((i == 0) & has_prior)
        def _():
            high, low = split(gstate[0, :128, :])
            hv = held[0, V, w:, :]
            lead[0] = lead[0] - (dot_nt(hv, high) + dot_nt(hv, low) + gstate[0, 128:129, :])
            lead_copy.start()

        return carry

    lax.fori_loop(0, chunks // 2, far_part, 0)

    base = backward.base()

    def tail_states(i, carry):
        now, after = carry
        b = 2 * chunks - 1 - i
        own = gstate[b]
        gstate[b] = now
        return after, after + own

    lax.fori_loop(0, 2 * chunks, tail_states, (base, base))

    @pl.when(has_later)
    def _():
        await_bytes(lead.at[chunks], recv_lead)

    @pl.when(jnp.logical_not(has_later))
    def _():
        lead[chunks] = jnp.zeros(lead.shape[1:], F32)

    def last_part(i, carry):
        for c in (2 * i, 2 * i + 1):
            d_phi = []
            for half in range(2):
                v, b = held[c + 1, V, half * w : (half + 1) * w, :], 2 * c + half
                high, low = split(gstate[b, :128, :])
                d_phi.append(dot_nt(v, high) + dot_nt(v, low) + gstate[b, 128:129, :])
            d_phi = [d_phi[0] + near[c, :w, :], d_phi[1] + (near[c, w:, :] + lead[c + 1])]
            gk[...] += feature_grad(held[c + 1, K], soft_k[c], jnp.concatenate(d_phi, 0))
        return carry

    lax.fori_loop(0, chunks // 2, last_part, 0)
    for k in range(PLANE):
        source = gq if k < PLANE // 2 else gk
        packed[k] = source[k % (PLANE // 2) * 8 : k % (PLANE // 2) * 8 + 8, :]
    final.give()
    await_bytes(out_held, recv_out)

    def arrange(i, carry):
        for head in (2 * i, 2 * i + 1):
            out_ref[pl.ds(head, rows, stride=heads), :] = out_held[head].astype(F32)
        return carry

    lax.fori_loop(0, heads // 2, arrange, 0)
    final.collect()
    final.spread()
    most = pl.ds(0, PLANE - 1)
    await_bytes(mine.at[most], send)
    await_bytes(out_send.at[most], send_out)
    forward.finish()
    backward.finish()

    @pl.when(has_later)
    def _():
        halo_copy.wait_send()

    @pl.when(has_prior)
    def _():
        lead_copy.wait_send()

    final.finish()


def per_device(queries, keys, values, target, map_q, map_k):
    rows, heads, size = queries.shape
    total_tokens = rows * lax.axis_size("seq")
    layers = lax.axis_size("seq") // PLANE
    others = layers * lax.axis_size("head")
    chunks = PLANE
    flat = (rows * heads, size)
    wide = pltpu.VMEM(flat, F32)
    narrow = pltpu.VMEM(flat, BF16)
    tiles = pltpu.VMEM((chunks, rows, size), F32)
    tiles16 = pltpu.VMEM((chunks, rows, size), BF16)
    column = pltpu.VMEM((chunks, rows, 1), F32)
    states = pltpu.VMEM((2 * chunks, ROWS, size), F32)
    state = pltpu.VMEM((ROWS, size), F32)
    layer = pltpu.VMEM((layers, ROWS, size), F32)
    grad = pltpu.VMEM((size, size), F32)
    slices = pltpu.VMEM((PLANE, size // PLANE, size), F32)
    dma = pltpu.SemaphoreType.DMA
    one = dma(())
    vmem = pl.BlockSpec(memory_space=pltpu.VMEM)
    hbm = pl.BlockSpec(memory_space=pl.ANY)
    output, grads = pl.pallas_call(
        functools.partial(kernel, heads, total_tokens),
        out_shape=[
            jax.ShapeDtypeStruct(flat, F32),
            jax.ShapeDtypeStruct((PLANE, size // PLANE, size), F32),
        ],
        in_specs=[hbm] * 4 + [vmem] * 2,
        out_specs=[vmem] * 2,
        scratch_shapes=[
            narrow, narrow, narrow, narrow, wide, wide, wide, wide,
            pltpu.VMEM((heads, 4, rows, size), BF16), pltpu.VMEM((chunks + 1, 4, rows, size), BF16),
            pltpu.VMEM((chunks + 1, rows, size), BF16), tiles, tiles, tiles, column, column, states, state, tiles, column,
            states, tiles, pltpu.VMEM((chunks + 1, WINDOW, size), F32), state, layer, layer, tiles16, tiles16,
            grad, grad, slices, slices, pltpu.VMEM((others, size // PLANE, size), F32),
            dma((4,)), one, dma((PLANE,)), one, one, one, one, one, one, *[one] * 10,
        ],
        compiler_params=pltpu.CompilerParams(vmem_limit_bytes=VMEM_LIMIT, collective_id=0, has_side_effects=True),
    )(*(array.reshape(flat) for array in (queries, keys, values, target)), map_q.T, map_k.T)
    hybrid = output.astype(BF16).reshape(rows, heads, size)
    grads = grads.reshape(size, size)
    return hybrid, grads[:FEAT].T, grads[FEAT:].T


def solution(mesh):
    tokens = P("seq", "head", None)
    return jax.shard_map(
        per_device,
        mesh=mesh,
        in_specs=(tokens, tokens, tokens, tokens, P(), P()),
        out_specs=(tokens, P(), P()),
        check_vma=False,
    )
```

```python
import functools

import jax
import jax.numpy as jnp
from jax import lax
from jax.experimental import pallas as pl
from jax.experimental.pallas import tpu as pltpu
from jax.sharding import PartitionSpec as P

WINDOW = 64
FEAT = 64
PLANE = 16
ROWS = 136
MESH = pl.DeviceIdType.MESH
F32 = jnp.float32
BF16 = jnp.bfloat16
VMEM_LIMIT = 56 * 1024 * 1024


def dot_nn(a, b):
    return lax.dot_general(a, b, (((1,), (0,)), ((), ())), preferred_element_type=F32)


def dot_nt(a, b):
    return lax.dot_general(a, b, (((1,), (1,)), ((), ())), preferred_element_type=F32)


def dot_tn(a, b):
    return lax.dot_general(a, b, (((0,), (0,)), ((), ())), preferred_element_type=F32)


def split(x):
    high = x.astype(BF16)
    return high, (x - high.astype(F32)).astype(BF16)


def left_half(shape):
    return lax.broadcasted_iota(jnp.int32, shape, len(shape) - 1) < FEAT


def features(x, pair_map):
    hidden = dot_nt(x, pair_map)
    left = left_half(hidden.shape)
    top_left = jnp.max(jnp.where(left, hidden, -jnp.inf), -1, keepdims=True)
    top_right = jnp.max(jnp.where(left, -jnp.inf, hidden), -1, keepdims=True)
    e = jnp.exp(hidden - jnp.where(left, top_left, top_right))
    sum_left = jnp.sum(jnp.where(left, e, 0.0), -1, keepdims=True)
    sum_right = jnp.sum(jnp.where(left, 0.0, e), -1, keepdims=True)
    return e * jnp.where(left, 1.0 / sum_left, 1.0 / sum_right)


def feature_grad(x, soft, upstream):
    left = left_half(soft.shape)
    product = soft * upstream
    inner_left = jnp.sum(jnp.where(left, product, 0.0), -1, keepdims=True)
    inner_right = jnp.sum(jnp.where(left, 0.0, product), -1, keepdims=True)
    part = soft * (upstream - jnp.where(left, inner_left, inner_right))
    u = part - pltpu.roll(part, FEAT, 1)
    return dot_tn(u.astype(BF16), x)


def head_rows(ref, head, rows, heads):
    return ref[pl.ds(head, rows, stride=heads), :]


def widen(src, dst):
    dst[...] = src[...].astype(F32)


def wrapped(k, count):
    return jnp.where(k >= count, k - count, k)


def await_bytes(ref, sem):
    pltpu.make_async_copy(ref, ref, sem).wait()


class Across:
    def __init__(self, totals, send, recv, reverse):
        self.totals, self.send, self.recv, self.reverse = totals, send, recv, reverse
        me = lax.axis_index("seq")
        self.layers = lax.axis_size("seq") // PLANE
        self.z, self.p = me // PLANE, me % PLANE

    def give(self, total):
        self.totals[self.z] = total
        for i in range(1, self.layers):
            other = wrapped(self.z + i, self.layers)
            pltpu.make_async_remote_copy(
                src_ref=self.totals.at[self.z], dst_ref=self.totals.at[self.z], send_sem=self.send, recv_sem=self.recv,
                device_id={"seq": other * PLANE + self.p}, device_id_type=MESH,
            ).start()

    def base(self):
        await_bytes(self.totals.at[pl.ds(0, self.layers - 1)], self.recv)
        base = jnp.zeros(self.totals.shape[1:], F32)
        for k in range(self.layers):
            reached = k > self.z if self.reverse else k < self.z
            base = base + jnp.where(reached, self.totals[k], 0.0)
        return base

    def finish(self):
        await_bytes(self.totals.at[pl.ds(0, self.layers - 1)], self.send)


class Total:
    def __init__(self, x, out, parts, totals, sems):
        self.x, self.out, self.parts, self.totals = x, out, parts, totals
        self.send1, self.recv1, self.send_z, self.recv_z, self.send2, self.recv2 = sems
        me, core = lax.axis_index("seq"), lax.axis_index("head")
        self.cores = lax.axis_size("head")
        self.others = lax.axis_size("seq") // PLANE * self.cores
        self.z, self.p = me // PLANE, me % PLANE
        self.here = self.z * self.cores + core

    def in_plane(self, k):
        return {"seq": self.z * PLANE + k}

    def give(self):
        for i in range(1, PLANE):
            to = wrapped(self.p + i, PLANE)
            pltpu.make_async_remote_copy(
                src_ref=self.x.at[to], dst_ref=self.parts.at[self.p], send_sem=self.send1, recv_sem=self.recv1,
                device_id=self.in_plane(to), device_id_type=MESH,
            ).start()
        pltpu.make_async_copy(self.x.at[self.p], self.parts.at[self.p], self.recv1).start()

    def collect(self):
        await_bytes(self.parts, self.recv1)
        self.totals[self.here] = jnp.sum(self.parts[...], 0)
        for i in range(1, self.others):
            at = wrapped(self.here + i, self.others)
            pltpu.make_async_remote_copy(
                src_ref=self.totals.at[self.here], dst_ref=self.totals.at[self.here],
                send_sem=self.send_z, recv_sem=self.recv_z,
                device_id={"seq": (at // self.cores) * PLANE + self.p, "head": at % self.cores}, device_id_type=MESH,
            ).start()

    def spread(self):
        await_bytes(self.totals.at[pl.ds(0, self.others - 1)], self.recv_z)
        self.out[self.p] = jnp.sum(self.totals[...], 0)
        for i in range(1, PLANE):
            pltpu.make_async_remote_copy(
                src_ref=self.out.at[self.p], dst_ref=self.out.at[self.p], send_sem=self.send2, recv_sem=self.recv2,
                device_id=self.in_plane(wrapped(self.p + i, PLANE)), device_id_type=MESH,
            ).start()

    def finish(self):
        most = pl.ds(0, PLANE - 1)
        await_bytes(self.out.at[most], self.recv2)
        await_bytes(self.out.at[most], self.send2)
        await_bytes(self.x.at[most], self.send1)
        await_bytes(self.totals.at[pl.ds(0, self.others - 1)], self.send_z)


def greet():
    me, core = lax.axis_index("seq"), lax.axis_index("head")
    count, cores = lax.axis_size("seq"), lax.axis_size("head")
    others = count // PLANE * cores
    z, p = me // PLANE, me % PLANE
    barrier = pltpu.get_barrier_semaphore()

    def plane(i, carry):
        device = {"seq": z * PLANE + (p + i) % PLANE}
        pl.semaphore_signal(barrier, inc=1, device_id=device, device_id_type=MESH)
        return carry

    def beyond(i, carry):
        at = (z * cores + core + i) % others
        device = {"seq": (at // cores) * PLANE + p, "head": at % cores}
        pl.semaphore_signal(barrier, inc=1, device_id=device, device_id_type=MESH)
        return carry

    lax.fori_loop(1, PLANE, plane, 0)
    lax.fori_loop(1, others, beyond, 0)
    return PLANE - 1 + others - 1


def kernel(
    heads, total_tokens, q_ref, k_ref, v_ref, t_ref, mq_ref, mk_ref, out_ref, grad_ref,
    k_in, v_in, q_in, t_in, k_wide, v_wide, q_wide, t_wide, mine, held,
    phi_all, soft_q, soft_k, numer_near, denom_near, damp, state, halo_state, d_numer_all, d_denom_all,
    gstate, state16, state_sum, later16, later_sum, near, lead, total, totals1, totals2, out_send, out_held, gq, gk, packed, parts3, totals3,
    load, send, recv, send_halo, recv_halo, send_lead, recv_lead, send_out, recv_out, *sems,
):
    w = WINDOW
    rows = 2 * w
    chunks = PLANE
    K, V, Q, T = range(4)
    greeted = greet()
    arrays = [(k_ref, k_in, k_wide), (v_ref, v_in, v_wide), (q_ref, q_in, q_wide), (t_ref, t_in, t_wide)]
    loads = [pltpu.make_async_copy(source, into, load.at[i]) for i, (source, into, wide) in enumerate(arrays)]
    for copy in loads:
        copy.start()
    me = lax.axis_index("seq")
    layers = lax.axis_size("seq") // PLANE
    z, p = me // PLANE, me % PLANE
    has_prior = z > 0
    has_later = z < layers - 1
    forward = Across(totals1, sems[0], sems[1], False)
    backward = Across(totals2, sems[2], sems[3], True)
    final = Total(packed, grad_ref, parts3, totals3, sems[4:10])

    def in_plane(k):
        return {"seq": z * PLANE + k}

    halo_there = held.at[0, pl.ds(0, 2), pl.ds(w, w)]
    halo_copy = pltpu.make_async_remote_copy(
        src_ref=held.at[chunks, pl.ds(0, 2), pl.ds(w, w)], dst_ref=halo_there, send_sem=send_halo, recv_sem=recv_halo,
        device_id={"seq": jnp.where(has_later, z + 1, 0) * PLANE + p}, device_id_type=MESH,
    )
    lead_copy = pltpu.make_async_remote_copy(
        src_ref=lead.at[0], dst_ref=lead.at[chunks], send_sem=send_lead, recv_sem=recv_lead,
        device_id={"seq": jnp.where(has_prior, z - 1, layers - 1) * PLANE + p}, device_id_type=MESH,
    )

    def give(wave, first):
        def step(i, carry):
            for head in (wrapped(p + 2 * i, PLANE), wrapped(p + 2 * i + 1, PLANE)):
                for j in wave:
                    mine[head, j] = head_rows(arrays[j][2], head, rows, heads).astype(BF16)
            part = pl.ds(wave[0], len(wave))
            for k in range(2):
                head = wrapped(p + 2 * i + k, PLANE)

                @pl.when(head != p)
                def _():
                    pltpu.make_async_remote_copy(
                        src_ref=mine.at[head, part], dst_ref=held.at[p + 1, part],
                        send_sem=send, recv_sem=recv.at[first + p],
                        device_id=in_plane(head), device_id_type=MESH,
                    ).start()

                @pl.when(head == p)
                def _():
                    pltpu.make_async_copy(mine.at[head, part], held.at[p + 1, part], recv.at[first + p]).start()

            return carry

        for j in wave:
            loads[j].wait()
            widen(arrays[j][1], arrays[j][2])
        if first == 0:
            pl.semaphore_wait(pltpu.get_barrier_semaphore(), greeted)
        lax.fori_loop(0, heads // 2, step, 0)

    give((K, V), 0)
    give((Q,), PLANE)
    give((T,), 2 * PLANE)

    map_q, map_k = (
        jnp.concatenate([ref[...], (-ref[...].astype(F32)).astype(BF16)], 0) for ref in (mq_ref, mk_ref)
    )
    row = lax.broadcasted_iota(jnp.int32, (w, rows), 0)
    col = lax.broadcasted_iota(jnp.int32, (w, rows), 1)
    scale = 128 ** (-0.5)
    total[...] = jnp.zeros_like(total)

    def masks(c, half):
        in_window = (col > row) & (col <= row + w)
        in_far = col <= row
        if half:
            return in_window, in_far
        live = (col >= w) | has_prior | (c > 0)
        return in_window & live, in_far & live

    def ext(ref, c):
        return jnp.concatenate([ref[c, w:, :], ref[c + 1, :w, :]], 0)

    def arriving(i):
        return wrapped(p + PLANE - 2 * i, PLANE), wrapped(p + PLANE - 2 * i - 1, PLANE)

    def key_part(i, carry):
        pair = arriving(i)
        for c in pair:
            await_bytes(held.at[c + 1, pl.ds(K, 2)], recv.at[c])

            @pl.when((c == chunks - 1) & has_later)
            def _():
                halo_copy.start()

        for c in pair:
            soft = features(held[c + 1, K], map_k)
            soft_k[c] = soft
            phi = soft.astype(BF16)
            phi_all[c + 1] = phi
            v = held[c + 1, V]
            for half in range(2):
                part = phi[half * w : (half + 1) * w]
                block_state = dot_tn(part, v[half * w : (half + 1) * w])
                block_sum = jnp.sum(part.astype(F32), 0, keepdims=True)
                state[2 * c + half, :128, :] = block_state
                state[2 * c + half, 128:, :] = jnp.broadcast_to(block_sum, (ROWS - 128, 128))
                total[:128, :] += block_state
                total[128:, :] += block_sum
        return carry

    lax.fori_loop(0, chunks // 2, key_part, 0)
    forward.give(total[...])

    @pl.when(has_prior)
    def _():
        await_bytes(halo_there, recv_halo)

    @pl.when(jnp.logical_not(has_prior))
    def _():
        held[0, :2, w:, :] = jnp.zeros((2, w, 128), BF16)

    phi_halo = jnp.where(has_prior, features(held[0, K, w:, :], map_k), 0.0).astype(BF16)
    phi_all[0, w:, :] = phi_halo
    halo_state[:128, :] = dot_tn(phi_halo, held[0, V, w:, :])
    halo_state[128:, :] = jnp.broadcast_to(jnp.sum(phi_halo.astype(F32), 0, keepdims=True), (ROWS - 128, 128))

    def near_part(i, carry):
        pair = arriving(i)
        for c in pair:
            await_bytes(held.at[c + 1, pl.ds(Q, 1)], recv.at[PLANE + c])
        for c in pair:
            soft = features(held[c + 1, Q], map_q)
            soft_q[c] = soft
            phi_q = soft.astype(BF16)
            for half in range(2):
                block, span = pl.ds(half * w, w), slice(half * w, (half + 1) * w)
                if half:
                    kn, vn, pn = held[c + 1, K], held[c + 1, V], phi_all[c + 1]
                else:
                    kn, vn, pn = ext(held.at[:, K], c), ext(held.at[:, V], c), ext(phi_all, c)
                in_window, in_far = masks(c, half)
                scores = jnp.where(in_window, dot_nt(held[c + 1, Q, span, :], kn) * scale, -jnp.inf)
                top = jnp.max(scores, -1, keepdims=True)
                damping = jnp.exp(-top)
                far = damping * dot_nt(phi_q[span], pn)
                weight = jnp.exp(scores - top) + jnp.where(in_far, far, 0.0)
                numer_near[c, block, :] = dot_nn(weight.astype(BF16), vn)
                denom_near[c, block, :] = jnp.sum(weight, -1, keepdims=True)
                damp[c, block, :] = damping
        return carry

    lax.fori_loop(0, chunks // 2, near_part, 0)

    def store_split(into, sums, b, whole):
        high, low = split(whole[:128])
        into[b, :128, :] = high
        into[b, 128:, :] = low
        sums[b] = whole[128:]

    base = forward.base()

    def lead_states(b, carry):
        now, after = carry
        own = state[b]
        store_split(state16, state_sum, b, now)
        return after, after + own

    lax.fori_loop(0, 2 * chunks, lead_states, (base - halo_state[...], base))
    total[...] = jnp.zeros_like(total)

    def middle_part(i, carry):
        pair = arriving(i)
        for c in pair:
            await_bytes(held.at[c + 1, pl.ds(T, 1)], recv.at[2 * PLANE + c])
        for c in pair:
            phi_q = soft_q[c].astype(BF16)
            target = held[c + 1, T].astype(F32)
            for half in range(2):
                block, span, b = pl.ds(half * w, w), slice(half * w, (half + 1) * w), 2 * c + half
                pq = phi_q[span]
                wide_pq = pq.astype(F32)
                damping = damp[c, block, :]
                state_den = jnp.sum(wide_pq * state_sum[b, 0:1, :], -1, keepdims=True)
                state_num = dot_nn(jnp.concatenate([pq, pq], 1), state16[b])
                numer = numer_near[c, block, :] + damping * state_num
                inverse = 1.0 / (denom_near[c, block, :] + damping * state_den)
                output = numer * inverse
                out_send[c, block, :] = output.astype(BF16)
                d_out = (output - target[span]) * (2.0 / total_tokens)
                d_numer = d_out * inverse
                d_denom = -jnp.sum(d_out * output, -1, keepdims=True) * inverse
                d_numer_all[c, block, :] = d_numer
                d_denom_all[c, block, :] = d_denom
                g_state = dot_tn(pq, (damping * d_numer).astype(BF16))
                g_sum = jnp.sum(damping * d_denom * wide_pq, 0, keepdims=True)
                gstate[b, :128, :] = g_state
                gstate[b, 128:, :] = jnp.broadcast_to(g_sum, (ROWS - 128, 128))
                total[:128, :] += g_state
                total[128:, :] += g_sum
        return carry

    lax.fori_loop(0, chunks // 2, middle_part, 0)
    backward.give(total[...])

    def give_out(i, carry):
        c = wrapped(p + i, PLANE)
        pltpu.make_async_remote_copy(
            src_ref=out_send.at[c], dst_ref=out_held.at[p], send_sem=send_out, recv_sem=recv_out,
            device_id=in_plane(c), device_id_type=MESH,
        ).start()
        return carry

    lax.fori_loop(1, PLANE, give_out, 0)
    pltpu.make_async_copy(out_send.at[p], out_held.at[p], recv_out).start()
    gq[...] = jnp.zeros_like(gq)
    gk[...] = jnp.zeros_like(gk)

    def far_part(i, carry):
        d_phi = []
        pair = pl.ds(2 * i, 2)
        for c in (2 * i, 2 * i + 1):
            phi_q = soft_q[c].astype(BF16)
            d_near = []
            for half in range(2):
                block, b = pl.ds(half * w, w), 2 * c + half
                in_far = masks(c, half)[1]
                if half:
                    vn, pn = held[c + 1, V], phi_all[c + 1]
                else:
                    vn, pn = ext(held.at[:, V], c), ext(phi_all, c)
                damping = damp[c, block, :]
                d_numer = d_numer_all[c, block, :]
                d_denom = d_denom_all[c, block, :]
                high, low = split(damping * d_numer)
                far_grad = damping * (dot_nt(d_numer.astype(BF16), vn) + d_denom)
                far_grad = jnp.where(in_far, far_grad, 0.0).astype(BF16)
                through = dot_nt(high, state16[b])
                through = through[:, :128] + through[:, 128:] + dot_nt(low, state16[b, :128, :])
                d_phi.append(dot_nn(far_grad, pn) + through + damping * d_denom * state_sum[b, 0:1, :])
                d_near.append(dot_tn(far_grad, phi_q[half * w : (half + 1) * w]))
            lead[c] = d_near[0][:w]
            near[c, :w, :] = d_near[0][w:] + d_near[1][:w]
            near[c, w:, :] = d_near[1][w:]
        x = jnp.concatenate([held[2 * i + 1, Q], held[2 * i + 2, Q]], 0)
        gq[...] += feature_grad(x, soft_q[pair].reshape(2 * rows, 128), jnp.concatenate(d_phi, 0))

        @pl.when((i == 0) & has_prior)
        def _():
            high, low = split(gstate[0, :128, :])
            hv = held[0, V, w:, :]
            lead[0] = lead[0] - (dot_nt(hv, high) + dot_nt(hv, low) + gstate[0, 128:129, :])
            lead_copy.start()

        return carry

    lax.fori_loop(0, chunks // 2, far_part, 0)

    base = backward.base()

    def tail_states(i, carry):
        now, after = carry
        b = 2 * chunks - 1 - i
        own = gstate[b]
        store_split(later16, later_sum, b, now)
        return after, after + own

    lax.fori_loop(0, 2 * chunks, tail_states, (base, base))

    @pl.when(has_later)
    def _():
        await_bytes(lead.at[chunks], recv_lead)

    @pl.when(jnp.logical_not(has_later))
    def _():
        lead[chunks] = jnp.zeros(lead.shape[1:], F32)

    def last_part(i, carry):
        d_phi = []
        pair = pl.ds(2 * i, 2)
        for c in (2 * i, 2 * i + 1):
            for half in range(2):
                span, b = slice(half * w, (half + 1) * w), 2 * c + half
                far = dot_nt(held[c + 1, V, span, :], later16[b])
                far = far[:, :128] + far[:, 128:] + later_sum[b, 0:1, :]
                d_near = near[c, span, :]
                d_phi.append(far + (d_near + lead[c + 1] if half else d_near))
        x = jnp.concatenate([held[2 * i + 1, K], held[2 * i + 2, K]], 0)
        gk[...] += feature_grad(x, soft_k[pair].reshape(2 * rows, 128), jnp.concatenate(d_phi, 0))
        return carry

    lax.fori_loop(0, chunks // 2, last_part, 0)
    for k in range(PLANE):
        source = gq if k < PLANE // 2 else gk
        packed[k] = source[k % (PLANE // 2) * 8 : k % (PLANE // 2) * 8 + 8, :]
    final.give()
    await_bytes(out_held, recv_out)

    def arrange(i, carry):
        for head in (2 * i, 2 * i + 1):
            out_ref[pl.ds(head, rows, stride=heads), :] = out_held[head].astype(F32)
        return carry

    lax.fori_loop(0, heads // 2, arrange, 0)
    final.collect()
    final.spread()
    most = pl.ds(0, PLANE - 1)
    await_bytes(mine.at[most], send)
    await_bytes(out_send.at[most], send_out)
    forward.finish()
    backward.finish()

    @pl.when(has_later)
    def _():
        halo_copy.wait_send()

    @pl.when(has_prior)
    def _():
        lead_copy.wait_send()

    final.finish()


def per_device(queries, keys, values, target, map_q, map_k):
    rows, heads, size = queries.shape
    total_tokens = rows * lax.axis_size("seq")
    layers = lax.axis_size("seq") // PLANE
    others = layers * lax.axis_size("head")
    chunks = PLANE
    flat = (rows * heads, size)
    wide = pltpu.VMEM(flat, F32)
    narrow = pltpu.VMEM(flat, BF16)
    tiles = pltpu.VMEM((chunks, rows, size), F32)
    tiles16 = pltpu.VMEM((chunks, rows, size), BF16)
    column = pltpu.VMEM((chunks, rows, 1), F32)
    states = pltpu.VMEM((2 * chunks, ROWS, size), F32)
    state = pltpu.VMEM((ROWS, size), F32)
    split_states = pltpu.VMEM((2 * chunks, 2 * size, size), BF16)
    state_sums = pltpu.VMEM((2 * chunks, ROWS - 128, size), F32)
    layer = pltpu.VMEM((layers, ROWS, size), F32)
    grad = pltpu.VMEM((size, size), F32)
    slices = pltpu.VMEM((PLANE, size // PLANE, size), F32)
    dma = pltpu.SemaphoreType.DMA
    one = dma(())
    vmem = pl.BlockSpec(memory_space=pltpu.VMEM)
    hbm = pl.BlockSpec(memory_space=pl.ANY)
    output, grads = pl.pallas_call(
        functools.partial(kernel, heads, total_tokens),
        out_shape=[
            jax.ShapeDtypeStruct(flat, F32),
            jax.ShapeDtypeStruct((PLANE, size // PLANE, size), F32),
        ],
        in_specs=[hbm] * 4 + [vmem] * 2,
        out_specs=[vmem] * 2,
        scratch_shapes=[
            narrow, narrow, narrow, narrow, wide, wide, wide, wide,
            pltpu.VMEM((heads, 4, rows, size), BF16), pltpu.VMEM((chunks + 1, 4, rows, size), BF16),
            pltpu.VMEM((chunks + 1, rows, size), BF16), tiles, tiles, tiles, column, column, states, state, tiles, column,
            states, split_states, state_sums, split_states, state_sums, tiles,
            pltpu.VMEM((chunks + 1, WINDOW, size), F32), state, layer, layer, tiles16, tiles16,
            grad, grad, slices, slices, pltpu.VMEM((others, size // PLANE, size), F32),
            dma((4,)), one, dma((3 * PLANE,)), one, one, one, one, one, one, *[one] * 10,
        ],
        compiler_params=pltpu.CompilerParams(vmem_limit_bytes=VMEM_LIMIT, collective_id=0, has_side_effects=True),
    )(*(array.reshape(flat) for array in (queries, keys, values, target)), map_q.T, map_k.T)
    hybrid = output.astype(BF16).reshape(rows, heads, size)
    grads = grads.reshape(size, size)
    return hybrid, grads[:FEAT].T, grads[FEAT:].T


def solution(mesh):
    tokens = P("seq", "head", None)
    return jax.shard_map(
        per_device,
        mesh=mesh,
        in_specs=(tokens, tokens, tokens, tokens, P(), P()),
        out_specs=(tokens, P(), P()),
        check_vma=False,
    )
```

```python
import functools

import jax
import jax.numpy as jnp
from jax import lax
from jax.experimental import pallas as pl
from jax.experimental.pallas import tpu as pltpu
from jax.sharding import PartitionSpec as P

WINDOW = 64
FEAT = 64
PLANE = 16
ROWS = 136
MESH = pl.DeviceIdType.MESH
F32 = jnp.float32
BF16 = jnp.bfloat16
VMEM_LIMIT = 56 * 1024 * 1024


def dot_nn(a, b):
    return lax.dot_general(a, b, (((1,), (0,)), ((), ())), preferred_element_type=F32)


def dot_nt(a, b):
    return lax.dot_general(a, b, (((1,), (1,)), ((), ())), preferred_element_type=F32)


def dot_tn(a, b):
    return lax.dot_general(a, b, (((0,), (0,)), ((), ())), preferred_element_type=F32)


def split(x):
    high = x.astype(BF16)
    return high, (x - high.astype(F32)).astype(BF16)


def left_half(shape):
    return lax.broadcasted_iota(jnp.int32, shape, len(shape) - 1) < FEAT


def features(x, pair_map):
    hidden = dot_nt(x, pair_map)
    left = left_half(hidden.shape)
    top_left = jnp.max(jnp.where(left, hidden, -jnp.inf), -1, keepdims=True)
    top_right = jnp.max(jnp.where(left, -jnp.inf, hidden), -1, keepdims=True)
    e = jnp.exp(hidden - jnp.where(left, top_left, top_right))
    sum_left = jnp.sum(jnp.where(left, e, 0.0), -1, keepdims=True)
    sum_right = jnp.sum(jnp.where(left, 0.0, e), -1, keepdims=True)
    return e * jnp.where(left, 1.0 / sum_left, 1.0 / sum_right)


def feature_grad(x, soft, upstream):
    left = left_half(soft.shape)
    product = soft * upstream
    inner_left = jnp.sum(jnp.where(left, product, 0.0), -1, keepdims=True)
    inner_right = jnp.sum(jnp.where(left, 0.0, product), -1, keepdims=True)
    part = soft * (upstream - jnp.where(left, inner_left, inner_right))
    u = part - pltpu.roll(part, FEAT, 1)
    return dot_tn(u.astype(BF16), x)


def head_rows(ref, head, rows, heads):
    return ref[pl.ds(head, rows, stride=heads), :]


def widen(src, dst):
    dst[...] = src[...].astype(F32)


def wrapped(k, count):
    return jnp.where(k >= count, k - count, k)


def await_bytes(ref, sem):
    pltpu.make_async_copy(ref, ref, sem).wait()


class Across:
    def __init__(self, totals, send, recv, reverse):
        self.totals, self.send, self.recv, self.reverse = totals, send, recv, reverse
        me = lax.axis_index("seq")
        self.layers = lax.axis_size("seq") // PLANE
        self.z, self.p = me // PLANE, me % PLANE

    def give(self, total):
        self.totals[self.z] = total
        for i in range(1, self.layers):
            other = wrapped(self.z + i, self.layers)
            pltpu.make_async_remote_copy(
                src_ref=self.totals.at[self.z], dst_ref=self.totals.at[self.z], send_sem=self.send, recv_sem=self.recv,
                device_id={"seq": other * PLANE + self.p}, device_id_type=MESH,
            ).start()

    def base(self):
        await_bytes(self.totals.at[pl.ds(0, self.layers - 1)], self.recv)
        base = jnp.zeros(self.totals.shape[1:], F32)
        for k in range(self.layers):
            reached = k > self.z if self.reverse else k < self.z
            base = base + jnp.where(reached, self.totals[k], 0.0)
        return base

    def finish(self):
        await_bytes(self.totals.at[pl.ds(0, self.layers - 1)], self.send)


def groups():
    me = lax.axis_index("seq")
    z, x, y = me // PLANE, (me // 4) % 4, me % 4
    low, high = x % 2, x // 2

    def first(k):
        return {"seq": (k // 2) * PLANE + (high * 2 + k % 2) * 4 + y}

    def second(k):
        return {"seq": z * PLANE + ((k % 2) * 2 + low) * 4 + k // 2}

    return (z * 2 + low, first), (y * 2 + high, second)


class Total:
    def __init__(self, grads, out, inbox, slots, sems):
        self.grads, self.out, self.inbox, self.slots, self.sems = grads, out, inbox, slots, sems
        self.core = lax.axis_index("head")

    def swap(self):
        other = 1 - self.core
        return pltpu.make_async_remote_copy(
            src_ref=self.grads.at[other], dst_ref=self.inbox, send_sem=self.sems[0], recv_sem=self.sems[1],
            device_id={"head": other}, device_id_type=MESH,
        )

    def give(self, stage, value):
        here, device = groups()[stage]
        slots, send, recv = self.slots[stage], self.sems[2 + 2 * stage], self.sems[3 + 2 * stage]
        slots[here] = value
        for i in range(1, 8):
            pltpu.make_async_remote_copy(
                src_ref=slots.at[here], dst_ref=slots.at[here], send_sem=send, recv_sem=recv,
                device_id=device(wrapped(here + i, 8)), device_id_type=MESH,
            ).start()

    def take(self, stage):
        slots = self.slots[stage]
        await_bytes(slots.at[pl.ds(0, 7)], self.sems[3 + 2 * stage])
        return jnp.sum(slots[...], 0)

    def share(self):
        return pltpu.make_async_remote_copy(
            src_ref=self.out.at[self.core], dst_ref=self.out.at[self.core], send_sem=self.sems[6], recv_sem=self.sems[7],
            device_id={"head": 1 - self.core}, device_id_type=MESH,
        )

    def finish(self):
        for stage in range(2):
            await_bytes(self.slots[stage].at[pl.ds(0, 7)], self.sems[2 + 2 * stage])


def greet():
    me, core = lax.axis_index("seq"), lax.axis_index("head")
    z, p = me // PLANE, me % PLANE
    barrier = pltpu.get_barrier_semaphore()

    def plane(i, carry):
        device = {"seq": z * PLANE + (p + i) % PLANE}
        pl.semaphore_signal(barrier, inc=1, device_id=device, device_id_type=MESH)
        return carry

    lax.fori_loop(1, PLANE, plane, 0)
    here, device = groups()[0]
    for i in range(1, 8):
        pl.semaphore_signal(barrier, inc=1, device_id=device(wrapped(here + i, 8)), device_id_type=MESH)
    pl.semaphore_signal(barrier, inc=1, device_id={"head": 1 - core}, device_id_type=MESH)
    return PLANE - 1 + 7 + 1


def kernel(
    heads, total_tokens, q_ref, k_ref, v_ref, t_ref, mq_ref, mk_ref, out_ref, grad_ref,
    k_in, v_in, q_in, t_in, k_wide, v_wide, q_wide, t_wide, mine, held,
    phi_all, soft_q, soft_k, numer_near, denom_near, damp, state, halo_state, d_numer_all, d_denom_all,
    gstate, state16, state_sum, later16, later_sum, near, lead, totals1, totals2, out_send, out_held, out_wide, gq, gk, grads, inbox, slots1, slots2,
    load, store, send, recv, send_halo, recv_halo, send_lead, recv_lead, send_out, recv_out, *sems,
):
    w = WINDOW
    rows = 2 * w
    chunks = PLANE
    K, V, Q, T = range(4)
    greeted = greet()
    arrays = [(k_ref, k_in, k_wide), (v_ref, v_in, v_wide), (q_ref, q_in, q_wide), (t_ref, t_in, t_wide)]
    loads = [pltpu.make_async_copy(source, into, load.at[i]) for i, (source, into, wide) in enumerate(arrays)]
    for j in (Q, K, V, T):
        loads[j].start()
    me = lax.axis_index("seq")
    layers = lax.axis_size("seq") // PLANE
    z, p = me // PLANE, me % PLANE
    has_prior = z > 0
    has_later = z < layers - 1
    forward = Across(totals1, sems[0], sems[1], False)
    backward = Across(totals2, sems[2], sems[3], True)
    final = Total(grads, grad_ref, inbox, (slots1, slots2), sems[4:12])

    def in_plane(k):
        return {"seq": z * PLANE + k}

    halo_there = held.at[0, pl.ds(0, 2), pl.ds(w, w)]
    halo_copy = pltpu.make_async_remote_copy(
        src_ref=held.at[chunks, pl.ds(0, 2), pl.ds(w, w)], dst_ref=halo_there, send_sem=send_halo, recv_sem=recv_halo,
        device_id={"seq": jnp.where(has_later, z + 1, 0) * PLANE + p}, device_id_type=MESH,
    )
    lead_copy = pltpu.make_async_remote_copy(
        src_ref=lead.at[0], dst_ref=lead.at[chunks], send_sem=send_lead, recv_sem=recv_lead,
        device_id={"seq": jnp.where(has_prior, z - 1, layers - 1) * PLANE + p}, device_id_type=MESH,
    )

    def give(wave, first):
        def step(i, carry):
            for head in (wrapped(p + 2 * i, PLANE), wrapped(p + 2 * i + 1, PLANE)):
                for j in wave:
                    mine[head, j] = head_rows(arrays[j][2], head, rows, heads).astype(BF16)
            part = pl.ds(wave[0], len(wave))
            for k in range(2):
                head = wrapped(p + 2 * i + k, PLANE)

                @pl.when(head != p)
                def _():
                    pltpu.make_async_remote_copy(
                        src_ref=mine.at[head, part], dst_ref=held.at[p + 1, part],
                        send_sem=send, recv_sem=recv.at[first + p],
                        device_id=in_plane(head), device_id_type=MESH,
                    ).start()

                @pl.when(head == p)
                def _():
                    pltpu.make_async_copy(mine.at[head, part], held.at[p + 1, part], recv.at[first + p]).start()

            return carry

        for j in wave:
            loads[j].wait()
            widen(arrays[j][1], arrays[j][2])
        if first == 0:
            pl.semaphore_wait(pltpu.get_barrier_semaphore(), greeted)
        lax.fori_loop(0, heads // 2, step, 0)

    give((Q,), 0)
    give((K,), PLANE)
    give((V,), 2 * PLANE)
    give((T,), 3 * PLANE)

    map_q, map_k = (
        jnp.concatenate([ref[...], (-ref[...].astype(F32)).astype(BF16)], 0) for ref in (mq_ref, mk_ref)
    )
    row = lax.broadcasted_iota(jnp.int32, (w, rows), 0)
    col = lax.broadcasted_iota(jnp.int32, (w, rows), 1)
    scale = 128 ** (-0.5)
    zero_state = jnp.zeros((ROWS, 128), F32)

    def masks(c, half):
        in_window = (col > row) & (col <= row + w)
        in_far = col <= row
        if half:
            return in_window, in_far
        live = (col >= w) | has_prior | (c > 0)
        return in_window & live, in_far & live

    def ext(ref, c):
        return jnp.concatenate([ref[c, w:, :], ref[c + 1, :w, :]], 0)

    def arriving(i):
        return wrapped(p + PLANE - 2 * i, PLANE), wrapped(p + PLANE - 2 * i - 1, PLANE)

    def query_part(i, carry):
        pair = arriving(i)
        for c in pair:
            await_bytes(held.at[c + 1, pl.ds(Q, 1)], recv.at[c])
        for c in pair:
            soft_q[c] = features(held[c + 1, Q], map_q)
        return carry

    def key_part(i, carry):
        pair = arriving(i)
        for c in pair:
            await_bytes(held.at[c + 1, pl.ds(K, 1)], recv.at[PLANE + c])
        for c in pair:
            soft = features(held[c + 1, K], map_k)
            soft_k[c] = soft
            phi_all[c + 1] = soft.astype(BF16)
        return carry

    def state_part(i, carry):
        pair = arriving(i)
        for c in pair:
            await_bytes(held.at[c + 1, pl.ds(V, 1)], recv.at[2 * PLANE + c])

            @pl.when((c == chunks - 1) & has_later)
            def _():
                halo_copy.start()

        for c in pair:
            phi = phi_all[c + 1]
            for half in range(2):
                part = phi[half * w : (half + 1) * w]
                block_sum = jnp.sum(part.astype(F32), 0, keepdims=True)
                state[2 * c + half, :128, :] = dot_tn(part, held[c + 1, V, half * w : (half + 1) * w, :])
                state[2 * c + half, 128:, :] = jnp.broadcast_to(block_sum, (ROWS - 128, 128))
        return carry

    def sum_of(ref):
        return lax.fori_loop(0, chunks, lambda i, whole: whole + (ref[2 * i] + ref[2 * i + 1]), zero_state)

    lax.fori_loop(0, chunks // 2, query_part, 0)
    lax.fori_loop(0, chunks // 2, key_part, 0)
    lax.fori_loop(0, chunks // 2, state_part, 0)
    forward.give(sum_of(state))

    def near_part(i, carry):
        @pl.when(i == chunks // 2 - 1)
        def _():
            @pl.when(has_prior)
            def _():
                await_bytes(halo_there, recv_halo)

            @pl.when(jnp.logical_not(has_prior))
            def _():
                held[0, :2, w:, :] = jnp.zeros((2, w, 128), BF16)

            phi_halo = jnp.where(has_prior, features(held[0, K, w:, :], map_k), 0.0).astype(BF16)
            phi_all[0, w:, :] = phi_halo
            halo_state[:128, :] = dot_tn(phi_halo, held[0, V, w:, :])
            halo_sum = jnp.sum(phi_halo.astype(F32), 0, keepdims=True)
            halo_state[128:, :] = jnp.broadcast_to(halo_sum, (ROWS - 128, 128))

        for c in (chunks - 1 - 2 * i, chunks - 2 - 2 * i):
            phi_q = soft_q[c].astype(BF16)
            for half in range(2):
                block, span = pl.ds(half * w, w), slice(half * w, (half + 1) * w)
                if half:
                    kn, vn, pn = held[c + 1, K], held[c + 1, V], phi_all[c + 1]
                else:
                    kn, vn, pn = ext(held.at[:, K], c), ext(held.at[:, V], c), ext(phi_all, c)
                in_window, in_far = masks(c, half)
                scores = jnp.where(in_window, dot_nt(held[c + 1, Q, span, :], kn) * scale, -jnp.inf)
                top = jnp.max(scores, -1, keepdims=True)
                damping = jnp.exp(-top)
                far = damping * dot_nt(phi_q[span], pn)
                weight = jnp.exp(scores - top) + jnp.where(in_far, far, 0.0)
                numer_near[c, block, :] = dot_nn(weight.astype(BF16), vn)
                denom_near[c, block, :] = jnp.sum(weight, -1, keepdims=True)
                damp[c, block, :] = damping
        return carry

    lax.fori_loop(0, chunks // 2, near_part, 0)

    def store_split(into, sums, b, whole):
        high, low = split(whole[:128])
        into[b, :128, :] = high
        into[b, 128:, :] = low
        sums[b] = whole[128:]

    base = forward.base()

    def lead_states(b, carry):
        now, after = carry
        own = state[b]
        store_split(state16, state_sum, b, now)
        return after, after + own

    lax.fori_loop(0, 2 * chunks, lead_states, (base - halo_state[...], base))

    def middle_part(i, carry):
        pair = arriving(i)
        for c in pair:
            await_bytes(held.at[c + 1, pl.ds(T, 1)], recv.at[3 * PLANE + c])
        for c in pair:
            phi_q = soft_q[c].astype(BF16)
            target = held[c + 1, T].astype(F32)
            for half in range(2):
                block, span, b = pl.ds(half * w, w), slice(half * w, (half + 1) * w), 2 * c + half
                pq = phi_q[span]
                wide_pq = pq.astype(F32)
                damping = damp[c, block, :]
                state_den = jnp.sum(wide_pq * state_sum[b, 0:1, :], -1, keepdims=True)
                state_num = dot_nn(jnp.concatenate([pq, pq], 1), state16[b])
                numer = numer_near[c, block, :] + damping * state_num
                inverse = 1.0 / (denom_near[c, block, :] + damping * state_den)
                output = numer * inverse
                out_send[c, block, :] = output.astype(BF16)
                d_out = (output - target[span]) * (2.0 / total_tokens)
                d_numer = d_out * inverse
                d_denom = -jnp.sum(d_out * output, -1, keepdims=True) * inverse
                d_numer_all[c, block, :] = d_numer
                d_denom_all[c, block, :] = d_denom
                g_state = dot_tn(pq, (damping * d_numer).astype(BF16))
                g_sum = jnp.sum(damping * d_denom * wide_pq, 0, keepdims=True)
                gstate[b, :128, :] = g_state
                gstate[b, 128:, :] = jnp.broadcast_to(g_sum, (ROWS - 128, 128))
        return carry

    lax.fori_loop(0, chunks // 2, middle_part, 0)
    backward.give(sum_of(gstate))

    def give_out(i, carry):
        c = wrapped(p + i, PLANE)
        pltpu.make_async_remote_copy(
            src_ref=out_send.at[c], dst_ref=out_held.at[p], send_sem=send_out, recv_sem=recv_out,
            device_id=in_plane(c), device_id_type=MESH,
        ).start()
        return carry

    lax.fori_loop(1, PLANE, give_out, 0)
    pltpu.make_async_copy(out_send.at[p], out_held.at[p], recv_out).start()
    gq[...] = jnp.zeros_like(gq)
    gk[...] = jnp.zeros_like(gk)

    def far_part(i, carry):
        d_phi = []
        pair = pl.ds(2 * i, 2)
        for c in (2 * i, 2 * i + 1):
            phi_q = soft_q[c].astype(BF16)
            d_near = []
            for half in range(2):
                block, b = pl.ds(half * w, w), 2 * c + half
                in_far = masks(c, half)[1]
                if half:
                    vn, pn = held[c + 1, V], phi_all[c + 1]
                else:
                    vn, pn = ext(held.at[:, V], c), ext(phi_all, c)
                damping = damp[c, block, :]
                d_numer = d_numer_all[c, block, :]
                d_denom = d_denom_all[c, block, :]
                high, low = split(damping * d_numer)
                far_grad = damping * (dot_nt(d_numer.astype(BF16), vn) + d_denom)
                far_grad = jnp.where(in_far, far_grad, 0.0).astype(BF16)
                through = dot_nt(high, state16[b])
                through = through[:, :128] + through[:, 128:] + dot_nt(low, state16[b, :128, :])
                d_phi.append(dot_nn(far_grad, pn) + through + damping * d_denom * state_sum[b, 0:1, :])
                d_near.append(dot_tn(far_grad, phi_q[half * w : (half + 1) * w]))
            lead[c] = d_near[0][:w]
            near[c, :w, :] = d_near[0][w:] + d_near[1][:w]
            near[c, w:, :] = d_near[1][w:]
        x = jnp.concatenate([held[2 * i + 1, Q], held[2 * i + 2, Q]], 0)
        gq[...] += feature_grad(x, soft_q[pair].reshape(2 * rows, 128), jnp.concatenate(d_phi, 0))

        @pl.when((i == 0) & has_prior)
        def _():
            high, low = split(gstate[0, :128, :])
            hv = held[0, V, w:, :]
            lead[0] = lead[0] - (dot_nt(hv, high) + dot_nt(hv, low) + gstate[0, 128:129, :])
            lead_copy.start()

        return carry

    lax.fori_loop(0, chunks // 2, far_part, 0)

    base = backward.base()

    def tail_states(i, carry):
        now, after = carry
        b = 2 * chunks - 1 - i
        own = gstate[b]
        store_split(later16, later_sum, b, now)
        return after, after + own

    lax.fori_loop(0, 2 * chunks, tail_states, (base, base))

    @pl.when(has_later)
    def _():
        await_bytes(lead.at[chunks], recv_lead)

    @pl.when(jnp.logical_not(has_later))
    def _():
        lead[chunks] = jnp.zeros(lead.shape[1:], F32)

    def last_part(i, carry):
        d_phi = []
        pair = pl.ds(2 * i, 2)
        for c in (2 * i, 2 * i + 1):
            for half in range(2):
                span, b = slice(half * w, (half + 1) * w), 2 * c + half
                far = dot_nt(held[c + 1, V, span, :], later16[b])
                far = far[:, :128] + far[:, 128:] + later_sum[b, 0:1, :]
                d_near = near[c, span, :]
                d_phi.append(far + (d_near + lead[c + 1] if half else d_near))
        x = jnp.concatenate([held[2 * i + 1, K], held[2 * i + 2, K]], 0)
        gk[...] += feature_grad(x, soft_k[pair].reshape(2 * rows, 128), jnp.concatenate(d_phi, 0))
        return carry

    lax.fori_loop(0, chunks // 2, last_part, 0)
    grads[0] = gq[:FEAT, :]
    grads[1] = gk[:FEAT, :]
    swap = final.swap()
    swap.start()
    swap.wait()
    final.give(0, grads[final.core] + inbox[...])
    await_bytes(out_held, recv_out)

    def arrange(i, carry):
        for head in (2 * i, 2 * i + 1):
            out_wide[pl.ds(head, rows, stride=heads), :] = out_held[head].astype(F32)
        return carry

    lax.fori_loop(0, heads // 2, arrange, 0)
    out_copy = pltpu.make_async_copy(out_wide, out_ref, store)
    out_copy.start()
    final.give(1, final.take(0))
    grad_ref[final.core] = final.take(1)
    share = final.share()
    share.start()
    most = pl.ds(0, PLANE - 1)
    await_bytes(mine.at[most], send)
    await_bytes(out_send.at[most], send_out)
    forward.finish()
    backward.finish()

    @pl.when(has_later)
    def _():
        halo_copy.wait_send()

    @pl.when(has_prior)
    def _():
        lead_copy.wait_send()

    final.finish()
    out_copy.wait()
    share.wait()


def per_device(queries, keys, values, target, map_q, map_k):
    rows, heads, size = queries.shape
    total_tokens = rows * lax.axis_size("seq")
    layers = lax.axis_size("seq") // PLANE
    chunks = PLANE
    flat = (rows * heads, size)
    wide = pltpu.VMEM(flat, F32)
    narrow = pltpu.VMEM(flat, BF16)
    tiles = pltpu.VMEM((chunks, rows, size), F32)
    tiles16 = pltpu.VMEM((chunks, rows, size), BF16)
    column = pltpu.VMEM((chunks, rows, 1), F32)
    states = pltpu.VMEM((2 * chunks, ROWS, size), F32)
    state = pltpu.VMEM((ROWS, size), F32)
    split_states = pltpu.VMEM((2 * chunks, 2 * size, size), BF16)
    state_sums = pltpu.VMEM((2 * chunks, ROWS - 128, size), F32)
    layer = pltpu.VMEM((layers, ROWS, size), F32)
    grad = pltpu.VMEM((size, size), F32)
    slots = pltpu.VMEM((8, FEAT, size), F32)
    dma = pltpu.SemaphoreType.DMA
    one = dma(())
    vmem = pl.BlockSpec(memory_space=pltpu.VMEM)
    hbm = pl.BlockSpec(memory_space=pl.ANY)
    output, grads = pl.pallas_call(
        functools.partial(kernel, heads, total_tokens),
        out_shape=[
            jax.ShapeDtypeStruct(flat, F32),
            jax.ShapeDtypeStruct((2, FEAT, size), F32),
        ],
        in_specs=[hbm] * 4 + [vmem] * 2,
        out_specs=[hbm, vmem],
        scratch_shapes=[
            narrow, narrow, narrow, narrow, wide, wide, wide, wide,
            pltpu.VMEM((heads, 4, rows, size), BF16), pltpu.VMEM((chunks + 1, 4, rows, size), BF16),
            pltpu.VMEM((chunks + 1, rows, size), BF16), tiles, tiles, tiles, column, column, states, state, tiles, column,
            states, split_states, state_sums, split_states, state_sums, tiles,
            pltpu.VMEM((chunks + 1, WINDOW, size), F32), layer, layer, tiles16, tiles16, wide,
            grad, grad, pltpu.VMEM((2, FEAT, size), F32), pltpu.VMEM((FEAT, size), F32), slots, slots,
            dma((4,)), one, one, dma((4 * PLANE,)), one, one, one, one, one, one, *[one] * 12,
        ],
        compiler_params=pltpu.CompilerParams(vmem_limit_bytes=VMEM_LIMIT, collective_id=0, has_side_effects=True),
    )(*(array.reshape(flat) for array in (queries, keys, values, target)), map_q.T, map_k.T)
    hybrid = output.astype(BF16).reshape(rows, heads, size)
    return hybrid, grads[0].T, grads[1].T


def solution(mesh):
    tokens = P("seq", "head", None)
    return jax.shard_map(
        per_device,
        mesh=mesh,
        in_specs=(tokens, tokens, tokens, tokens, P(), P()),
        out_specs=(tokens, P(), P()),
        check_vma=False,
    )
```

```python
import functools

import jax
import jax.numpy as jnp
from jax import lax
from jax.experimental import pallas as pl
from jax.experimental.pallas import tpu as pltpu
from jax.sharding import PartitionSpec as P

WINDOW = 64
FEAT = 64
PLANE = 16
ROWS = 136
MESH = pl.DeviceIdType.MESH
F32 = jnp.float32
BF16 = jnp.bfloat16
VMEM_LIMIT = 56 * 1024 * 1024


def dot_nn(a, b):
    return lax.dot_general(a, b, (((1,), (0,)), ((), ())), preferred_element_type=F32)


def dot_nt(a, b):
    return lax.dot_general(a, b, (((1,), (1,)), ((), ())), preferred_element_type=F32)


def dot_tn(a, b):
    return lax.dot_general(a, b, (((0,), (0,)), ((), ())), preferred_element_type=F32)


def split(x):
    high = x.astype(BF16)
    return high, (x - high.astype(F32)).astype(BF16)


def left_half(shape):
    return lax.broadcasted_iota(jnp.int32, shape, len(shape) - 1) < FEAT


def features(x, pair_map):
    hidden = dot_nt(x, pair_map)
    left = left_half(hidden.shape)
    top_left = jnp.max(jnp.where(left, hidden, -jnp.inf), -1, keepdims=True)
    top_right = jnp.max(jnp.where(left, -jnp.inf, hidden), -1, keepdims=True)
    e = jnp.exp(hidden - jnp.where(left, top_left, top_right))
    sum_left = jnp.sum(jnp.where(left, e, 0.0), -1, keepdims=True)
    sum_right = jnp.sum(jnp.where(left, 0.0, e), -1, keepdims=True)
    return e * jnp.where(left, 1.0 / sum_left, 1.0 / sum_right)


def feature_grad(x, soft, upstream):
    left = left_half(soft.shape)
    product = soft * upstream
    inner_left = jnp.sum(jnp.where(left, product, 0.0), -1, keepdims=True)
    inner_right = jnp.sum(jnp.where(left, 0.0, product), -1, keepdims=True)
    part = soft * (upstream - jnp.where(left, inner_left, inner_right))
    u = part - pltpu.roll(part, FEAT, 1)
    return dot_tn(u.astype(BF16), x)


def head_rows(ref, head, rows, heads):
    return ref[pl.ds(head, rows, stride=heads), :]


def widen(src, dst):
    dst[...] = src[...].astype(F32)


def wrapped(k, count):
    return jnp.where(k >= count, k - count, k)


def await_bytes(ref, sem):
    pltpu.make_async_copy(ref, ref, sem).wait()


class Across:
    def __init__(self, totals, send, recv, reverse):
        self.totals, self.send, self.recv, self.reverse = totals, send, recv, reverse
        me = lax.axis_index("seq")
        self.layers = lax.axis_size("seq") // PLANE
        self.z, self.p = me // PLANE, me % PLANE

    def give(self, total):
        self.totals[self.z] = total
        for i in range(1, self.layers):
            other = wrapped(self.z + i, self.layers)
            pltpu.make_async_remote_copy(
                src_ref=self.totals.at[self.z], dst_ref=self.totals.at[self.z], send_sem=self.send, recv_sem=self.recv,
                device_id={"seq": other * PLANE + self.p}, device_id_type=MESH,
            ).start()

    def base(self):
        await_bytes(self.totals.at[pl.ds(0, self.layers - 1)], self.recv)
        base = jnp.zeros(self.totals.shape[1:], F32)
        for k in range(self.layers):
            reached = k > self.z if self.reverse else k < self.z
            base = base + jnp.where(reached, self.totals[k], 0.0)
        return base

    def finish(self):
        await_bytes(self.totals.at[pl.ds(0, self.layers - 1)], self.send)


def groups():
    me = lax.axis_index("seq")
    z, x, y = me // PLANE, (me // 4) % 4, me % 4
    low, high = x % 2, x // 2

    def first(k):
        return {"seq": (k // 2) * PLANE + (high * 2 + k % 2) * 4 + y}

    def second(k):
        return {"seq": z * PLANE + ((k % 2) * 2 + low) * 4 + k // 2}

    return (z * 2 + low, first), (y * 2 + high, second)


class Total:
    def __init__(self, grads, out, inbox, slots, sems):
        self.grads, self.out, self.inbox, self.slots, self.sems = grads, out, inbox, slots, sems
        self.core = lax.axis_index("head")

    def swap(self):
        other = 1 - self.core
        return pltpu.make_async_remote_copy(
            src_ref=self.grads.at[other], dst_ref=self.inbox, send_sem=self.sems[0], recv_sem=self.sems[1],
            device_id={"head": other}, device_id_type=MESH,
        )

    def give(self, stage, value):
        here, device = groups()[stage]
        slots, send, recv = self.slots[stage], self.sems[2 + 2 * stage], self.sems[3 + 2 * stage]
        slots[here] = value
        for i in range(1, 8):
            pltpu.make_async_remote_copy(
                src_ref=slots.at[here], dst_ref=slots.at[here], send_sem=send, recv_sem=recv,
                device_id=device(wrapped(here + i, 8)), device_id_type=MESH,
            ).start()

    def take(self, stage):
        slots = self.slots[stage]
        await_bytes(slots.at[pl.ds(0, 7)], self.sems[3 + 2 * stage])
        return jnp.sum(slots[...], 0)

    def share(self):
        return pltpu.make_async_remote_copy(
            src_ref=self.out.at[self.core], dst_ref=self.out.at[self.core], send_sem=self.sems[6], recv_sem=self.sems[7],
            device_id={"head": 1 - self.core}, device_id_type=MESH,
        )

    def finish(self):
        for stage in range(2):
            await_bytes(self.slots[stage].at[pl.ds(0, 7)], self.sems[2 + 2 * stage])


def greet():
    me, core = lax.axis_index("seq"), lax.axis_index("head")
    z, p = me // PLANE, me % PLANE
    barrier = pltpu.get_barrier_semaphore()

    def plane(i, carry):
        device = {"seq": z * PLANE + (p + i) % PLANE}
        pl.semaphore_signal(barrier, inc=1, device_id=device, device_id_type=MESH)
        return carry

    lax.fori_loop(1, PLANE, plane, 0)
    here, device = groups()[0]
    for i in range(1, 8):
        pl.semaphore_signal(barrier, inc=1, device_id=device(wrapped(here + i, 8)), device_id_type=MESH)
    pl.semaphore_signal(barrier, inc=1, device_id={"head": 1 - core}, device_id_type=MESH)
    return PLANE - 1 + 7 + 1


def kernel(
    heads, total_tokens, q_ref, k_ref, v_ref, t_ref, mq_ref, mk_ref, out_ref, grad_ref,
    k_in, v_in, q_in, t_in, k_wide, v_wide, q_wide, t_wide, mine, held,
    phi_all, soft_q, soft_k, weights, numer_near, denom_near, damp, state, halo_state, d_numer_all, d_denom_all,
    gstate, state16, state_sum, later16, later_sum, near, lead, totals1, totals2, out_send, out_held, out_wide, gq, gk, grads, inbox, slots1, slots2,
    load, store, send, recv, send_halo, recv_halo, send_lead, recv_lead, send_out, recv_out, *sems,
):
    w = WINDOW
    rows = 2 * w
    chunks = PLANE
    K, V, Q, T = range(4)
    greeted = greet()
    arrays = [(k_ref, k_in, k_wide), (v_ref, v_in, v_wide), (q_ref, q_in, q_wide), (t_ref, t_in, t_wide)]
    loads = [pltpu.make_async_copy(source, into, load.at[i]) for i, (source, into, wide) in enumerate(arrays)]
    for j in (Q, K, V, T):
        loads[j].start()
    me = lax.axis_index("seq")
    layers = lax.axis_size("seq") // PLANE
    z, p = me // PLANE, me % PLANE
    has_prior = z > 0
    has_later = z < layers - 1
    forward = Across(totals1, sems[0], sems[1], False)
    backward = Across(totals2, sems[2], sems[3], True)
    final = Total(grads, grad_ref, inbox, (slots1, slots2), sems[4:12])

    def in_plane(k):
        return {"seq": z * PLANE + k}

    def halo_there(j):
        return held.at[0, pl.ds(j, 1), pl.ds(w, w)]

    def halo_copy(j):
        return pltpu.make_async_remote_copy(
            src_ref=held.at[chunks, pl.ds(j, 1), pl.ds(w, w)], dst_ref=halo_there(j),
            send_sem=send_halo.at[j], recv_sem=recv_halo.at[j],
            device_id={"seq": jnp.where(has_later, z + 1, 0) * PLANE + p}, device_id_type=MESH,
        )

    def give_halo(j, c):
        @pl.when((c == chunks - 1) & has_later)
        def _():
            halo_copy(j).start()

    def take_halo(j):
        @pl.when(has_prior)
        def _():
            await_bytes(halo_there(j), recv_halo.at[j])

        @pl.when(jnp.logical_not(has_prior))
        def _():
            held[0, j, w:, :] = jnp.zeros((w, 128), BF16)

    lead_copy = pltpu.make_async_remote_copy(
        src_ref=lead.at[0], dst_ref=lead.at[chunks], send_sem=send_lead, recv_sem=recv_lead,
        device_id={"seq": jnp.where(has_prior, z - 1, layers - 1) * PLANE + p}, device_id_type=MESH,
    )

    def give(wave, first):
        def step(i, carry):
            for head in (wrapped(p + 2 * i, PLANE), wrapped(p + 2 * i + 1, PLANE)):
                for j in wave:
                    mine[head, j] = head_rows(arrays[j][2], head, rows, heads).astype(BF16)
            part = pl.ds(wave[0], len(wave))
            for k in range(2):
                head = wrapped(p + 2 * i + k, PLANE)

                @pl.when(head != p)
                def _():
                    pltpu.make_async_remote_copy(
                        src_ref=mine.at[head, part], dst_ref=held.at[p + 1, part],
                        send_sem=send, recv_sem=recv.at[first + p],
                        device_id=in_plane(head), device_id_type=MESH,
                    ).start()

                @pl.when(head == p)
                def _():
                    pltpu.make_async_copy(mine.at[head, part], held.at[p + 1, part], recv.at[first + p]).start()

            return carry

        for j in wave:
            loads[j].wait()
            widen(arrays[j][1], arrays[j][2])
        if first == 0:
            pl.semaphore_wait(pltpu.get_barrier_semaphore(), greeted)
        lax.fori_loop(0, heads // 2, step, 0)

    give((Q,), 0)
    give((K,), PLANE)
    give((V,), 2 * PLANE)
    give((T,), 3 * PLANE)

    map_q, map_k = (
        jnp.concatenate([ref[...], (-ref[...].astype(F32)).astype(BF16)], 0) for ref in (mq_ref, mk_ref)
    )
    row = lax.broadcasted_iota(jnp.int32, (w, rows), 0)
    col = lax.broadcasted_iota(jnp.int32, (w, rows), 1)
    scale = 128 ** (-0.5)
    zero_state = jnp.zeros((ROWS, 128), F32)

    def masks(c, half):
        in_window = (col > row) & (col <= row + w)
        in_far = col <= row
        if half:
            return in_window, in_far
        live = (col >= w) | has_prior | (c > 0)
        return in_window & live, in_far & live

    def ext(ref, c):
        return jnp.concatenate([ref[c, w:, :], ref[c + 1, :w, :]], 0)

    def arriving(i):
        return wrapped(p + PLANE - 2 * i, PLANE), wrapped(p + PLANE - 2 * i - 1, PLANE)

    def query_part(i, carry):
        pair = arriving(i)
        for c in pair:
            await_bytes(held.at[c + 1, pl.ds(Q, 1)], recv.at[c])
        for c in pair:
            soft_q[c] = features(held[c + 1, Q], map_q)
        return carry

    def key_part(i, carry):
        pair = arriving(i)
        for c in pair:
            await_bytes(held.at[c + 1, pl.ds(K, 1)], recv.at[PLANE + c])
            give_halo(K, c)
        for c in pair:
            soft = features(held[c + 1, K], map_k)
            soft_k[c] = soft
            phi_all[c + 1] = soft.astype(BF16)
        return carry

    def state_part(i, carry):
        pair = arriving(i)
        for c in pair:
            await_bytes(held.at[c + 1, pl.ds(V, 1)], recv.at[2 * PLANE + c])
            give_halo(V, c)

        for c in pair:
            phi = phi_all[c + 1]
            for half in range(2):
                part = phi[half * w : (half + 1) * w]
                block_sum = jnp.sum(part.astype(F32), 0, keepdims=True)
                state[2 * c + half, :128, :] = dot_tn(part, held[c + 1, V, half * w : (half + 1) * w, :])
                state[2 * c + half, 128:, :] = jnp.broadcast_to(block_sum, (ROWS - 128, 128))
        return carry

    def sum_of(ref):
        return lax.fori_loop(0, chunks, lambda i, whole: whole + (ref[2 * i] + ref[2 * i + 1]), zero_state)

    lax.fori_loop(0, chunks // 2, query_part, 0)
    lax.fori_loop(0, chunks // 2, key_part, 0)

    def weight_part(i, carry):
        @pl.when(i == chunks // 2 - 1)
        def _():
            take_halo(K)
            phi_all[0, w:, :] = jnp.where(has_prior, features(held[0, K, w:, :], map_k), 0.0).astype(BF16)

        for c in (chunks - 1 - 2 * i, chunks - 2 - 2 * i):
            phi_q = soft_q[c].astype(BF16)
            for half in range(2):
                block, span = pl.ds(half * w, w), slice(half * w, (half + 1) * w)
                if half:
                    kn, pn = held[c + 1, K], phi_all[c + 1]
                else:
                    kn, pn = ext(held.at[:, K], c), ext(phi_all, c)
                in_window, in_far = masks(c, half)
                scores = jnp.where(in_window, dot_nt(held[c + 1, Q, span, :], kn) * scale, -jnp.inf)
                top = jnp.max(scores, -1, keepdims=True)
                damping = jnp.exp(-top)
                far = damping * dot_nt(phi_q[span], pn)
                weight = jnp.exp(scores - top) + jnp.where(in_far, far, 0.0)
                weights[c, block, :] = weight.astype(BF16)
                denom_near[c, block, :] = jnp.sum(weight, -1, keepdims=True)
                damp[c, block, :] = damping
        return carry

    def near_part(i, carry):
        @pl.when(i == chunks // 2 - 1)
        def _():
            take_halo(V)
            phi_halo = phi_all[0, w:, :]
            halo_state[:128, :] = dot_tn(phi_halo, held[0, V, w:, :])
            halo_sum = jnp.sum(phi_halo.astype(F32), 0, keepdims=True)
            halo_state[128:, :] = jnp.broadcast_to(halo_sum, (ROWS - 128, 128))

        for c in (chunks - 1 - 2 * i, chunks - 2 - 2 * i):
            numer_near[c, :w, :] = dot_nn(weights[c, :w, :], ext(held.at[:, V], c))
            numer_near[c, w:, :] = dot_nn(weights[c, w:, :], held[c + 1, V])
        return carry

    lax.fori_loop(0, chunks // 2, weight_part, 0)
    lax.fori_loop(0, chunks // 2, state_part, 0)
    forward.give(sum_of(state))
    lax.fori_loop(0, chunks // 2, near_part, 0)

    def store_split(into, sums, b, whole):
        high, low = split(whole[:128])
        into[b, :128, :] = high
        into[b, 128:, :] = low
        sums[b] = whole[128:]

    base = forward.base()

    def lead_states(b, carry):
        now, after = carry
        own = state[b]
        store_split(state16, state_sum, b, now)
        return after, after + own

    lax.fori_loop(0, 2 * chunks, lead_states, (base - halo_state[...], base))

    def middle_part(i, carry):
        pair = arriving(i)
        for c in pair:
            await_bytes(held.at[c + 1, pl.ds(T, 1)], recv.at[3 * PLANE + c])
        for c in pair:
            phi_q = soft_q[c].astype(BF16)
            target = held[c + 1, T].astype(F32)
            for half in range(2):
                block, span, b = pl.ds(half * w, w), slice(half * w, (half + 1) * w), 2 * c + half
                pq = phi_q[span]
                wide_pq = pq.astype(F32)
                damping = damp[c, block, :]
                state_den = jnp.sum(wide_pq * state_sum[b, 0:1, :], -1, keepdims=True)
                state_num = dot_nn(jnp.concatenate([pq, pq], 1), state16[b])
                numer = numer_near[c, block, :] + damping * state_num
                inverse = 1.0 / (denom_near[c, block, :] + damping * state_den)
                output = numer * inverse
                out_send[c, block, :] = output.astype(BF16)
                d_out = (output - target[span]) * (2.0 / total_tokens)
                d_numer = d_out * inverse
                d_denom = -jnp.sum(d_out * output, -1, keepdims=True) * inverse
                d_numer_all[c, block, :] = d_numer
                d_denom_all[c, block, :] = d_denom
                g_state = dot_tn(pq, (damping * d_numer).astype(BF16))
                g_sum = jnp.sum(damping * d_denom * wide_pq, 0, keepdims=True)
                gstate[b, :128, :] = g_state
                gstate[b, 128:, :] = jnp.broadcast_to(g_sum, (ROWS - 128, 128))
        return carry

    lax.fori_loop(0, chunks // 2, middle_part, 0)
    backward.give(sum_of(gstate))

    def give_out(i, carry):
        c = wrapped(p + i, PLANE)
        pltpu.make_async_remote_copy(
            src_ref=out_send.at[c], dst_ref=out_held.at[p], send_sem=send_out, recv_sem=recv_out,
            device_id=in_plane(c), device_id_type=MESH,
        ).start()
        return carry

    lax.fori_loop(1, PLANE, give_out, 0)
    pltpu.make_async_copy(out_send.at[p], out_held.at[p], recv_out).start()
    gq[...] = jnp.zeros_like(gq)
    gk[...] = jnp.zeros_like(gk)

    def far_part(i, carry):
        d_phi = []
        pair = pl.ds(2 * i, 2)
        for c in (2 * i, 2 * i + 1):
            phi_q = soft_q[c].astype(BF16)
            d_near = []
            for half in range(2):
                block, b = pl.ds(half * w, w), 2 * c + half
                in_far = masks(c, half)[1]
                if half:
                    vn, pn = held[c + 1, V], phi_all[c + 1]
                else:
                    vn, pn = ext(held.at[:, V], c), ext(phi_all, c)
                damping = damp[c, block, :]
                d_numer = d_numer_all[c, block, :]
                d_denom = d_denom_all[c, block, :]
                high, low = split(damping * d_numer)
                far_grad = damping * (dot_nt(d_numer.astype(BF16), vn) + d_denom)
                far_grad = jnp.where(in_far, far_grad, 0.0).astype(BF16)
                through = dot_nt(high, state16[b])
                through = through[:, :128] + through[:, 128:] + dot_nt(low, state16[b, :128, :])
                d_phi.append(dot_nn(far_grad, pn) + through + damping * d_denom * state_sum[b, 0:1, :])
                d_near.append(dot_tn(far_grad, phi_q[half * w : (half + 1) * w]))
            lead[c] = d_near[0][:w]
            near[c, :w, :] = d_near[0][w:] + d_near[1][:w]
            near[c, w:, :] = d_near[1][w:]
        x = jnp.concatenate([held[2 * i + 1, Q], held[2 * i + 2, Q]], 0)
        gq[...] += feature_grad(x, soft_q[pair].reshape(2 * rows, 128), jnp.concatenate(d_phi, 0))

        @pl.when((i == 0) & has_prior)
        def _():
            high, low = split(gstate[0, :128, :])
            hv = held[0, V, w:, :]
            lead[0] = lead[0] - (dot_nt(hv, high) + dot_nt(hv, low) + gstate[0, 128:129, :])
            lead_copy.start()

        return carry

    lax.fori_loop(0, chunks // 2, far_part, 0)

    base = backward.base()

    def tail_states(i, carry):
        now, after = carry
        b = 2 * chunks - 1 - i
        own = gstate[b]
        store_split(later16, later_sum, b, now)
        return after, after + own

    lax.fori_loop(0, 2 * chunks, tail_states, (base, base))

    @pl.when(has_later)
    def _():
        await_bytes(lead.at[chunks], recv_lead)

    @pl.when(jnp.logical_not(has_later))
    def _():
        lead[chunks] = jnp.zeros(lead.shape[1:], F32)

    def last_part(i, carry):
        d_phi = []
        pair = pl.ds(2 * i, 2)
        for c in (2 * i, 2 * i + 1):
            for half in range(2):
                span, b = slice(half * w, (half + 1) * w), 2 * c + half
                far = dot_nt(held[c + 1, V, span, :], later16[b])
                far = far[:, :128] + far[:, 128:] + later_sum[b, 0:1, :]
                d_near = near[c, span, :]
                d_phi.append(far + (d_near + lead[c + 1] if half else d_near))
        x = jnp.concatenate([held[2 * i + 1, K], held[2 * i + 2, K]], 0)
        gk[...] += feature_grad(x, soft_k[pair].reshape(2 * rows, 128), jnp.concatenate(d_phi, 0))
        return carry

    lax.fori_loop(0, chunks // 2, last_part, 0)
    grads[0] = gq[:FEAT, :]
    grads[1] = gk[:FEAT, :]
    swap = final.swap()
    swap.start()
    swap.wait()
    final.give(0, grads[final.core] + inbox[...])
    await_bytes(out_held, recv_out)

    def arrange(i, carry):
        for head in (2 * i, 2 * i + 1):
            out_wide[pl.ds(head, rows, stride=heads), :] = out_held[head].astype(F32)
        return carry

    lax.fori_loop(0, heads // 2, arrange, 0)
    out_copy = pltpu.make_async_copy(out_wide, out_ref, store)
    out_copy.start()
    final.give(1, final.take(0))
    grad_ref[final.core] = final.take(1)
    share = final.share()
    share.start()
    most = pl.ds(0, PLANE - 1)
    await_bytes(mine.at[most], send)
    await_bytes(out_send.at[most], send_out)
    forward.finish()
    backward.finish()

    @pl.when(has_later)
    def _():
        halo_copy(K).wait_send()
        halo_copy(V).wait_send()

    @pl.when(has_prior)
    def _():
        lead_copy.wait_send()

    final.finish()
    out_copy.wait()
    share.wait()


def per_device(queries, keys, values, target, map_q, map_k):
    rows, heads, size = queries.shape
    total_tokens = rows * lax.axis_size("seq")
    layers = lax.axis_size("seq") // PLANE
    chunks = PLANE
    flat = (rows * heads, size)
    wide = pltpu.VMEM(flat, F32)
    narrow = pltpu.VMEM(flat, BF16)
    tiles = pltpu.VMEM((chunks, rows, size), F32)
    tiles16 = pltpu.VMEM((chunks, rows, size), BF16)
    column = pltpu.VMEM((chunks, rows, 1), F32)
    states = pltpu.VMEM((2 * chunks, ROWS, size), F32)
    state = pltpu.VMEM((ROWS, size), F32)
    split_states = pltpu.VMEM((2 * chunks, 2 * size, size), BF16)
    state_sums = pltpu.VMEM((2 * chunks, ROWS - 128, size), F32)
    layer = pltpu.VMEM((layers, ROWS, size), F32)
    grad = pltpu.VMEM((size, size), F32)
    slots = pltpu.VMEM((8, FEAT, size), F32)
    dma = pltpu.SemaphoreType.DMA
    one = dma(())
    vmem = pl.BlockSpec(memory_space=pltpu.VMEM)
    hbm = pl.BlockSpec(memory_space=pl.ANY)
    output, grads = pl.pallas_call(
        functools.partial(kernel, heads, total_tokens),
        out_shape=[
            jax.ShapeDtypeStruct(flat, F32),
            jax.ShapeDtypeStruct((2, FEAT, size), F32),
        ],
        in_specs=[hbm] * 4 + [vmem] * 2,
        out_specs=[hbm, vmem],
        scratch_shapes=[
            narrow, narrow, narrow, narrow, wide, wide, wide, wide,
            pltpu.VMEM((heads, 4, rows, size), BF16), pltpu.VMEM((chunks + 1, 4, rows, size), BF16),
            pltpu.VMEM((chunks + 1, rows, size), BF16), tiles, tiles, tiles16, tiles, column, column, states, state, tiles, column,
            states, split_states, state_sums, split_states, state_sums, tiles,
            pltpu.VMEM((chunks + 1, WINDOW, size), F32), layer, layer, tiles16, tiles16, wide,
            grad, grad, pltpu.VMEM((2, FEAT, size), F32), pltpu.VMEM((FEAT, size), F32), slots, slots,
            dma((4,)), one, one, dma((4 * PLANE,)), dma((2,)), dma((2,)), one, one, one, one, *[one] * 12,
        ],
        compiler_params=pltpu.CompilerParams(vmem_limit_bytes=VMEM_LIMIT, collective_id=0, has_side_effects=True),
    )(*(array.reshape(flat) for array in (queries, keys, values, target)), map_q.T, map_k.T)
    hybrid = output.astype(BF16).reshape(rows, heads, size)
    return hybrid, grads[0].T, grads[1].T


def solution(mesh):
    tokens = P("seq", "head", None)
    return jax.shard_map(
        per_device,
        mesh=mesh,
        in_specs=(tokens, tokens, tokens, tokens, P(), P()),
        out_specs=(tokens, P(), P()),
        check_vma=False,
    )
```

```python
import functools

import jax
import jax.numpy as jnp
from jax import lax
from jax.experimental import pallas as pl
from jax.experimental.pallas import tpu as pltpu
from jax.sharding import PartitionSpec as P

WINDOW = 64
FEAT = 64
PLANE = 16
ROWS = 136
MESH = pl.DeviceIdType.MESH
F32 = jnp.float32
BF16 = jnp.bfloat16
VMEM_LIMIT = 56 * 1024 * 1024


def dot_nn(a, b):
    return lax.dot_general(a, b, (((1,), (0,)), ((), ())), preferred_element_type=F32)


def dot_nt(a, b):
    return lax.dot_general(a, b, (((1,), (1,)), ((), ())), preferred_element_type=F32)


def dot_tn(a, b):
    return lax.dot_general(a, b, (((0,), (0,)), ((), ())), preferred_element_type=F32)


def split(x):
    high = x.astype(BF16)
    return high, (x - high.astype(F32)).astype(BF16)


def left_half(shape):
    return lax.broadcasted_iota(jnp.int32, shape, len(shape) - 1) < FEAT


def features(x, pair_map):
    hidden = dot_nt(x, pair_map)
    left = left_half(hidden.shape)
    top_left = jnp.max(jnp.where(left, hidden, -jnp.inf), -1, keepdims=True)
    top_right = jnp.max(jnp.where(left, -jnp.inf, hidden), -1, keepdims=True)
    e = jnp.exp(hidden - jnp.where(left, top_left, top_right))
    sum_left = jnp.sum(jnp.where(left, e, 0.0), -1, keepdims=True)
    sum_right = jnp.sum(jnp.where(left, 0.0, e), -1, keepdims=True)
    return e * jnp.where(left, 1.0 / sum_left, 1.0 / sum_right)


def feature_grad(x, soft, upstream):
    left = left_half(soft.shape)
    product = soft * upstream
    inner_left = jnp.sum(jnp.where(left, product, 0.0), -1, keepdims=True)
    inner_right = jnp.sum(jnp.where(left, 0.0, product), -1, keepdims=True)
    part = soft * (upstream - jnp.where(left, inner_left, inner_right))
    u = part - pltpu.roll(part, FEAT, 1)
    return dot_tn(u.astype(BF16), x)


def head_rows(ref, head, rows, heads):
    return ref[pl.ds(head, rows, stride=heads), :]


def widen(src, dst):
    dst[...] = src[...].astype(F32)


def wrapped(k, count):
    return jnp.where(k >= count, k - count, k)


def await_bytes(ref, sem):
    pltpu.make_async_copy(ref, ref, sem).wait()


class Across:
    def __init__(self, totals, send, recv, reverse):
        self.totals, self.send, self.recv, self.reverse = totals, send, recv, reverse
        me = lax.axis_index("seq")
        self.layers = lax.axis_size("seq") // PLANE
        self.z, self.p = me // PLANE, me % PLANE

    def give(self, total):
        self.totals[self.z] = total
        for i in range(1, self.layers):
            other = wrapped(self.z + i, self.layers)
            pltpu.make_async_remote_copy(
                src_ref=self.totals.at[self.z], dst_ref=self.totals.at[self.z], send_sem=self.send, recv_sem=self.recv,
                device_id={"seq": other * PLANE + self.p}, device_id_type=MESH,
            ).start()

    def base(self):
        await_bytes(self.totals.at[pl.ds(0, self.layers - 1)], self.recv)
        base = jnp.zeros(self.totals.shape[1:], F32)
        for k in range(self.layers):
            reached = k > self.z if self.reverse else k < self.z
            base = base + jnp.where(reached, self.totals[k], 0.0)
        return base

    def finish(self):
        await_bytes(self.totals.at[pl.ds(0, self.layers - 1)], self.send)


def groups():
    me = lax.axis_index("seq")
    z, x, y = me // PLANE, (me // 4) % 4, me % 4
    low, high = x % 2, x // 2

    def first(k):
        return {"seq": (k // 2) * PLANE + (high * 2 + k % 2) * 4 + y}

    def second(k):
        return {"seq": z * PLANE + ((k % 2) * 2 + low) * 4 + k // 2}

    return (z * 2 + low, first), (y * 2 + high, second)


class Total:
    def __init__(self, grads, out, inbox, slots, sems):
        self.grads, self.out, self.inbox, self.slots, self.sems = grads, out, inbox, slots, sems
        self.core = lax.axis_index("head")

    def swap(self):
        other = 1 - self.core
        return pltpu.make_async_remote_copy(
            src_ref=self.grads.at[other], dst_ref=self.inbox, send_sem=self.sems[0], recv_sem=self.sems[1],
            device_id={"head": other}, device_id_type=MESH,
        )

    def give(self, stage, value):
        here, device = groups()[stage]
        slots, send, recv = self.slots[stage], self.sems[2 + 2 * stage], self.sems[3 + 2 * stage]
        slots[here] = value
        for i in range(1, 8):
            pltpu.make_async_remote_copy(
                src_ref=slots.at[here], dst_ref=slots.at[here], send_sem=send, recv_sem=recv,
                device_id=device(wrapped(here + i, 8)), device_id_type=MESH,
            ).start()

    def take(self, stage):
        slots = self.slots[stage]
        await_bytes(slots.at[pl.ds(0, 7)], self.sems[3 + 2 * stage])
        return jnp.sum(slots[...], 0)

    def share(self):
        return pltpu.make_async_remote_copy(
            src_ref=self.out.at[self.core], dst_ref=self.out.at[self.core], send_sem=self.sems[6], recv_sem=self.sems[7],
            device_id={"head": 1 - self.core}, device_id_type=MESH,
        )

    def finish(self):
        for stage in range(2):
            await_bytes(self.slots[stage].at[pl.ds(0, 7)], self.sems[2 + 2 * stage])


def greet():
    me, core = lax.axis_index("seq"), lax.axis_index("head")
    z, p = me // PLANE, me % PLANE
    barrier = pltpu.get_barrier_semaphore()

    def plane(i, carry):
        device = {"seq": z * PLANE + (p + i) % PLANE}
        pl.semaphore_signal(barrier, inc=1, device_id=device, device_id_type=MESH)
        return carry

    lax.fori_loop(1, PLANE, plane, 0)
    here, device = groups()[0]
    for i in range(1, 8):
        pl.semaphore_signal(barrier, inc=1, device_id=device(wrapped(here + i, 8)), device_id_type=MESH)
    pl.semaphore_signal(barrier, inc=1, device_id={"head": 1 - core}, device_id_type=MESH)
    return PLANE - 1 + 7 + 1


def kernel(
    heads, total_tokens, q_ref, k_ref, v_ref, t_ref, mq_ref, mk_ref, out_ref, grad_ref,
    k_in, v_in, q_in, t_in, k_wide, v_wide, q_wide, t_wide, mine, held,
    phi_all, soft_q, soft_k, weights, numer_near, denom_near, damp, state, halo_state, d_numer_all, d_denom_all,
    gstate, state16, state_sum, later16, later_sum, near, lead, totals1, totals2, out_send, out_held, out_wide, gq, gk, grads, inbox, slots1, slots2,
    load, store, send, recv, send_halo, recv_halo, send_lead, recv_lead, send_out, recv_out, *sems,
):
    w = WINDOW
    rows = 2 * w
    chunks = PLANE
    K, V, Q, T = range(4)
    greeted = greet()
    arrays = [(k_ref, k_in, k_wide), (v_ref, v_in, v_wide), (q_ref, q_in, q_wide), (t_ref, t_in, t_wide)]
    loads = [pltpu.make_async_copy(source, into, load.at[i]) for i, (source, into, wide) in enumerate(arrays)]
    for j in (Q, K, V, T):
        loads[j].start()
    me = lax.axis_index("seq")
    layers = lax.axis_size("seq") // PLANE
    z, p = me // PLANE, me % PLANE
    has_prior = z > 0
    has_later = z < layers - 1
    forward = Across(totals1, sems[0], sems[1], False)
    backward = Across(totals2, sems[2], sems[3], True)
    final = Total(grads, grad_ref, inbox, (slots1, slots2), sems[4:12])

    def in_plane(k):
        return {"seq": z * PLANE + k}

    def halo_there(j):
        return held.at[0, pl.ds(j, 1), pl.ds(w, w)]

    def halo_copy(j):
        return pltpu.make_async_remote_copy(
            src_ref=held.at[chunks, pl.ds(j, 1), pl.ds(w, w)], dst_ref=halo_there(j),
            send_sem=send_halo.at[j], recv_sem=recv_halo.at[j],
            device_id={"seq": jnp.where(has_later, z + 1, 0) * PLANE + p}, device_id_type=MESH,
        )

    def give_halo(j, c):
        @pl.when((c == chunks - 1) & has_later)
        def _():
            halo_copy(j).start()

    def take_halo(j):
        @pl.when(has_prior)
        def _():
            await_bytes(halo_there(j), recv_halo.at[j])

        @pl.when(jnp.logical_not(has_prior))
        def _():
            held[0, j, w:, :] = jnp.zeros((w, 128), BF16)

    lead_copy = pltpu.make_async_remote_copy(
        src_ref=lead.at[0], dst_ref=lead.at[chunks], send_sem=send_lead, recv_sem=recv_lead,
        device_id={"seq": jnp.where(has_prior, z - 1, layers - 1) * PLANE + p}, device_id_type=MESH,
    )

    def give(wave, first):
        def step(i, carry):
            for head in (wrapped(p + 2 * i, PLANE), wrapped(p + 2 * i + 1, PLANE)):
                for j in wave:
                    mine[head, j] = head_rows(arrays[j][2], head, rows, heads).astype(BF16)
            part = pl.ds(wave[0], len(wave))
            for k in range(2):
                head = wrapped(p + 2 * i + k, PLANE)

                @pl.when(head != p)
                def _():
                    pltpu.make_async_remote_copy(
                        src_ref=mine.at[head, part], dst_ref=held.at[p + 1, part],
                        send_sem=send, recv_sem=recv.at[first + p],
                        device_id=in_plane(head), device_id_type=MESH,
                    ).start()

                @pl.when(head == p)
                def _():
                    pltpu.make_async_copy(mine.at[head, part], held.at[p + 1, part], recv.at[first + p]).start()

            return carry

        for j in wave:
            loads[j].wait()
            widen(arrays[j][1], arrays[j][2])
        if first == 0:
            pl.semaphore_wait(pltpu.get_barrier_semaphore(), greeted)
        lax.fori_loop(0, heads // 2, step, 0)

    give((Q,), 0)
    give((K,), PLANE)
    give((V,), 2 * PLANE)
    give((T,), 3 * PLANE)

    map_q, map_k = (
        jnp.concatenate([ref[...], (-ref[...].astype(F32)).astype(BF16)], 0) for ref in (mq_ref, mk_ref)
    )
    row = lax.broadcasted_iota(jnp.int32, (w, rows), 0)
    col = lax.broadcasted_iota(jnp.int32, (w, rows), 1)
    scale = 128 ** (-0.5)
    zero_state = jnp.zeros((ROWS, 128), F32)

    def masks(c, half):
        in_window = (col > row) & (col <= row + w)
        in_far = col <= row
        if half:
            return in_window, in_far
        live = (col >= w) | has_prior | (c > 0)
        return in_window & live, in_far & live

    def ext(ref, c):
        return jnp.concatenate([ref[c, w:, :], ref[c + 1, :w, :]], 0)

    def arriving(i):
        return wrapped(p + PLANE - 2 * i, PLANE), wrapped(p + PLANE - 2 * i - 1, PLANE)

    def query_part(i, carry):
        pair = arriving(i)
        for c in pair:
            await_bytes(held.at[c + 1, pl.ds(Q, 1)], recv.at[c])
        for c in pair:
            soft_q[c] = features(held[c + 1, Q], map_q)
        return carry

    def key_part(i, carry):
        pair = arriving(i)
        for c in pair:
            await_bytes(held.at[c + 1, pl.ds(K, 1)], recv.at[PLANE + c])
            give_halo(K, c)
        for c in pair:
            soft = features(held[c + 1, K], map_k)
            soft_k[c] = soft
            phi_all[c + 1] = soft.astype(BF16)
        return carry

    def state_part(i, carry):
        pair = arriving(i)
        for c in pair:
            await_bytes(held.at[c + 1, pl.ds(V, 1)], recv.at[2 * PLANE + c])
            give_halo(V, c)

        for c in pair:
            phi = phi_all[c + 1]
            for half in range(2):
                part = phi[half * w : (half + 1) * w]
                block_sum = jnp.sum(part.astype(F32), 0, keepdims=True)
                state[2 * c + half, :128, :] = dot_tn(part, held[c + 1, V, half * w : (half + 1) * w, :])
                state[2 * c + half, 128:, :] = jnp.broadcast_to(block_sum, (ROWS - 128, 128))
        return carry

    def sum_of(ref):
        return lax.fori_loop(0, chunks, lambda i, whole: whole + (ref[2 * i] + ref[2 * i + 1]), zero_state)

    lax.fori_loop(0, chunks // 2, query_part, 0)
    lax.fori_loop(0, chunks // 2, key_part, 0)

    def weight_part(i, carry):
        @pl.when(i == chunks // 2 - 1)
        def _():
            take_halo(K)
            phi_all[0, w:, :] = jnp.where(has_prior, features(held[0, K, w:, :], map_k), 0.0).astype(BF16)

        for c in (chunks - 1 - 2 * i, chunks - 2 - 2 * i):
            phi_q = soft_q[c].astype(BF16)
            for half in range(2):
                block, span = pl.ds(half * w, w), slice(half * w, (half + 1) * w)
                if half:
                    kn, pn = held[c + 1, K], phi_all[c + 1]
                else:
                    kn, pn = ext(held.at[:, K], c), ext(phi_all, c)
                in_window, in_far = masks(c, half)
                scores = jnp.where(in_window, dot_nt(held[c + 1, Q, span, :], kn) * scale, -jnp.inf)
                top = jnp.max(scores, -1, keepdims=True)
                damping = jnp.exp(-top)
                far = damping * dot_nt(phi_q[span], pn)
                weight = jnp.exp(scores - top) + jnp.where(in_far, far, 0.0)
                weights[c, block, :] = weight.astype(BF16)
                denom_near[c, block, :] = jnp.sum(weight, -1, keepdims=True)
                damp[c, block, :] = damping
        return carry

    def near_part(i, carry):
        @pl.when(i == chunks // 2 - 1)
        def _():
            take_halo(V)
            phi_halo = phi_all[0, w:, :]
            halo_state[:128, :] = dot_tn(phi_halo, held[0, V, w:, :])
            halo_sum = jnp.sum(phi_halo.astype(F32), 0, keepdims=True)
            halo_state[128:, :] = jnp.broadcast_to(halo_sum, (ROWS - 128, 128))

        for c in (chunks - 1 - 2 * i, chunks - 2 - 2 * i):
            numer_near[c, :w, :] = dot_nn(weights[c, :w, :], ext(held.at[:, V], c))
            numer_near[c, w:, :] = dot_nn(weights[c, w:, :], held[c + 1, V])
        return carry

    lax.fori_loop(0, chunks // 2, weight_part, 0)
    lax.fori_loop(0, chunks // 2, state_part, 0)
    forward.give(sum_of(state))
    lax.fori_loop(0, chunks // 2, near_part, 0)

    def store_split(into, sums, b, whole):
        high, low = split(whole[:128])
        into[b, :128, :] = high
        into[b, 128:, :] = low
        sums[b] = whole[128:]

    base = forward.base()

    def lead_states(b, carry):
        now, after = carry
        own = state[b]
        store_split(state16, state_sum, b, now)
        return after, after + own

    lax.fori_loop(0, 2 * chunks, lead_states, (base - halo_state[...], base))

    def middle_part(i, carry):
        for c in arriving(i):
            phi_q = soft_q[c].astype(BF16)
            for half in range(2):
                block, span, b = pl.ds(half * w, w), slice(half * w, (half + 1) * w), 2 * c + half
                pq = phi_q[span]
                wide_pq = pq.astype(F32)
                damping = damp[c, block, :]
                state_den = jnp.sum(wide_pq * state_sum[b, 0:1, :], -1, keepdims=True)
                state_num = dot_nn(jnp.concatenate([pq, pq], 1), state16[b])
                numer = numer_near[c, block, :] + damping * state_num
                inverse = 1.0 / (denom_near[c, block, :] + damping * state_den)
                output = numer * inverse
                out_send[c, block, :] = output.astype(BF16)
                numer_near[c, block, :] = output
                denom_near[c, block, :] = inverse
        return carry

    def grad_part(i, carry):
        pair = arriving(i)
        for c in pair:
            await_bytes(held.at[c + 1, pl.ds(T, 1)], recv.at[3 * PLANE + c])
        for c in pair:
            phi_q = soft_q[c].astype(BF16)
            target = held[c + 1, T].astype(F32)
            for half in range(2):
                block, span, b = pl.ds(half * w, w), slice(half * w, (half + 1) * w), 2 * c + half
                pq = phi_q[span]
                wide_pq = pq.astype(F32)
                damping = damp[c, block, :]
                output, inverse = numer_near[c, block, :], denom_near[c, block, :]
                d_out = (output - target[span]) * (2.0 / total_tokens)
                d_numer = d_out * inverse
                d_denom = -jnp.sum(d_out * output, -1, keepdims=True) * inverse
                d_numer_all[c, block, :] = d_numer
                d_denom_all[c, block, :] = d_denom
                g_state = dot_tn(pq, (damping * d_numer).astype(BF16))
                g_sum = jnp.sum(damping * d_denom * wide_pq, 0, keepdims=True)
                gstate[b, :128, :] = g_state
                gstate[b, 128:, :] = jnp.broadcast_to(g_sum, (ROWS - 128, 128))
        return carry

    lax.fori_loop(0, chunks // 2, middle_part, 0)
    lax.fori_loop(0, chunks // 2, grad_part, 0)
    backward.give(sum_of(gstate))

    def give_out(i, carry):
        c = wrapped(p + i, PLANE)
        pltpu.make_async_remote_copy(
            src_ref=out_send.at[c], dst_ref=out_held.at[p], send_sem=send_out, recv_sem=recv_out,
            device_id=in_plane(c), device_id_type=MESH,
        ).start()
        return carry

    lax.fori_loop(1, PLANE, give_out, 0)
    pltpu.make_async_copy(out_send.at[p], out_held.at[p], recv_out).start()
    gq[...] = jnp.zeros_like(gq)
    gk[...] = jnp.zeros_like(gk)

    def far_part(i, carry):
        d_phi = []
        pair = pl.ds(2 * i, 2)
        for c in (2 * i, 2 * i + 1):
            phi_q = soft_q[c].astype(BF16)
            d_near = []
            for half in range(2):
                block, b = pl.ds(half * w, w), 2 * c + half
                in_far = masks(c, half)[1]
                if half:
                    vn, pn = held[c + 1, V], phi_all[c + 1]
                else:
                    vn, pn = ext(held.at[:, V], c), ext(phi_all, c)
                damping = damp[c, block, :]
                d_numer = d_numer_all[c, block, :]
                d_denom = d_denom_all[c, block, :]
                high, low = split(damping * d_numer)
                far_grad = damping * (dot_nt(d_numer.astype(BF16), vn) + d_denom)
                far_grad = jnp.where(in_far, far_grad, 0.0).astype(BF16)
                through = dot_nt(high, state16[b])
                through = through[:, :128] + through[:, 128:] + dot_nt(low, state16[b, :128, :])
                d_phi.append(dot_nn(far_grad, pn) + through + damping * d_denom * state_sum[b, 0:1, :])
                d_near.append(dot_tn(far_grad, phi_q[half * w : (half + 1) * w]))
            lead[c] = d_near[0][:w]
            near[c, :w, :] = d_near[0][w:] + d_near[1][:w]
            near[c, w:, :] = d_near[1][w:]
        x = jnp.concatenate([held[2 * i + 1, Q], held[2 * i + 2, Q]], 0)
        gq[...] += feature_grad(x, soft_q[pair].reshape(2 * rows, 128), jnp.concatenate(d_phi, 0))

        @pl.when((i == 0) & has_prior)
        def _():
            high, low = split(gstate[0, :128, :])
            hv = held[0, V, w:, :]
            lead[0] = lead[0] - (dot_nt(hv, high) + dot_nt(hv, low) + gstate[0, 128:129, :])
            lead_copy.start()

        return carry

    lax.fori_loop(0, chunks // 2, far_part, 0)

    base = backward.base()

    def tail_states(i, carry):
        now, after = carry
        b = 2 * chunks - 1 - i
        own = gstate[b]
        store_split(later16, later_sum, b, now)
        return after, after + own

    lax.fori_loop(0, 2 * chunks, tail_states, (base, base))

    @pl.when(has_later)
    def _():
        await_bytes(lead.at[chunks], recv_lead)

    @pl.when(jnp.logical_not(has_later))
    def _():
        lead[chunks] = jnp.zeros(lead.shape[1:], F32)

    def last_part(i, carry):
        d_phi = []
        pair = pl.ds(2 * i, 2)
        for c in (2 * i, 2 * i + 1):
            for half in range(2):
                span, b = slice(half * w, (half + 1) * w), 2 * c + half
                far = dot_nt(held[c + 1, V, span, :], later16[b])
                far = far[:, :128] + far[:, 128:] + later_sum[b, 0:1, :]
                d_near = near[c, span, :]
                d_phi.append(far + (d_near + lead[c + 1] if half else d_near))
        x = jnp.concatenate([held[2 * i + 1, K], held[2 * i + 2, K]], 0)
        gk[...] += feature_grad(x, soft_k[pair].reshape(2 * rows, 128), jnp.concatenate(d_phi, 0))
        return carry

    lax.fori_loop(0, chunks // 2, last_part, 0)
    grads[0] = gq[:FEAT, :]
    grads[1] = gk[:FEAT, :]
    swap = final.swap()
    swap.start()
    swap.wait()
    final.give(0, grads[final.core] + inbox[...])
    await_bytes(out_held, recv_out)

    def arrange(i, carry):
        for head in (2 * i, 2 * i + 1):
            out_wide[pl.ds(head, rows, stride=heads), :] = out_held[head].astype(F32)
        return carry

    lax.fori_loop(0, heads // 2, arrange, 0)
    out_copy = pltpu.make_async_copy(out_wide, out_ref, store)
    out_copy.start()
    final.give(1, final.take(0))
    grad_ref[final.core] = final.take(1)
    share = final.share()
    share.start()
    most = pl.ds(0, PLANE - 1)
    await_bytes(mine.at[most], send)
    await_bytes(out_send.at[most], send_out)
    forward.finish()
    backward.finish()

    @pl.when(has_later)
    def _():
        halo_copy(K).wait_send()
        halo_copy(V).wait_send()

    @pl.when(has_prior)
    def _():
        lead_copy.wait_send()

    final.finish()
    out_copy.wait()
    share.wait()


def per_device(queries, keys, values, target, map_q, map_k):
    rows, heads, size = queries.shape
    total_tokens = rows * lax.axis_size("seq")
    layers = lax.axis_size("seq") // PLANE
    chunks = PLANE
    flat = (rows * heads, size)
    wide = pltpu.VMEM(flat, F32)
    narrow = pltpu.VMEM(flat, BF16)
    tiles = pltpu.VMEM((chunks, rows, size), F32)
    tiles16 = pltpu.VMEM((chunks, rows, size), BF16)
    column = pltpu.VMEM((chunks, rows, 1), F32)
    states = pltpu.VMEM((2 * chunks, ROWS, size), F32)
    state = pltpu.VMEM((ROWS, size), F32)
    split_states = pltpu.VMEM((2 * chunks, 2 * size, size), BF16)
    state_sums = pltpu.VMEM((2 * chunks, ROWS - 128, size), F32)
    layer = pltpu.VMEM((layers, ROWS, size), F32)
    grad = pltpu.VMEM((size, size), F32)
    slots = pltpu.VMEM((8, FEAT, size), F32)
    dma = pltpu.SemaphoreType.DMA
    one = dma(())
    vmem = pl.BlockSpec(memory_space=pltpu.VMEM)
    hbm = pl.BlockSpec(memory_space=pl.ANY)
    output, grads = pl.pallas_call(
        functools.partial(kernel, heads, total_tokens),
        out_shape=[
            jax.ShapeDtypeStruct(flat, F32),
            jax.ShapeDtypeStruct((2, FEAT, size), F32),
        ],
        in_specs=[hbm] * 4 + [vmem] * 2,
        out_specs=[hbm, vmem],
        scratch_shapes=[
            narrow, narrow, narrow, narrow, wide, wide, wide, wide,
            pltpu.VMEM((heads, 4, rows, size), BF16), pltpu.VMEM((chunks + 1, 4, rows, size), BF16),
            pltpu.VMEM((chunks + 1, rows, size), BF16), tiles, tiles, tiles16, tiles, column, column, states, state, tiles, column,
            states, split_states, state_sums, split_states, state_sums, tiles,
            pltpu.VMEM((chunks + 1, WINDOW, size), F32), layer, layer, tiles16, tiles16, wide,
            grad, grad, pltpu.VMEM((2, FEAT, size), F32), pltpu.VMEM((FEAT, size), F32), slots, slots,
            dma((4,)), one, one, dma((4 * PLANE,)), dma((2,)), dma((2,)), one, one, one, one, *[one] * 12,
        ],
        compiler_params=pltpu.CompilerParams(vmem_limit_bytes=VMEM_LIMIT, collective_id=0, has_side_effects=True),
    )(*(array.reshape(flat) for array in (queries, keys, values, target)), map_q.T, map_k.T)
    hybrid = output.astype(BF16).reshape(rows, heads, size)
    return hybrid, grads[0].T, grads[1].T


def solution(mesh):
    tokens = P("seq", "head", None)
    return jax.shard_map(
        per_device,
        mesh=mesh,
        in_specs=(tokens, tokens, tokens, tokens, P(), P()),
        out_specs=(tokens, P(), P()),
        check_vma=False,
    )
```

```python
import functools

import jax
import jax.numpy as jnp
from jax import lax
from jax.experimental import pallas as pl
from jax.experimental.pallas import tpu as pltpu
from jax.sharding import PartitionSpec as P

WINDOW = 64
FEAT = 64
PLANE = 16
ROWS = 136
MESH = pl.DeviceIdType.MESH
F32 = jnp.float32
BF16 = jnp.bfloat16
VMEM_LIMIT = 56 * 1024 * 1024


def dot_nn(a, b):
    return lax.dot_general(a, b, (((1,), (0,)), ((), ())), preferred_element_type=F32)


def dot_nt(a, b):
    return lax.dot_general(a, b, (((1,), (1,)), ((), ())), preferred_element_type=F32)


def dot_tn(a, b):
    return lax.dot_general(a, b, (((0,), (0,)), ((), ())), preferred_element_type=F32)


def split(x):
    high = x.astype(BF16)
    return high, (x - high.astype(F32)).astype(BF16)


def left_half(shape):
    return lax.broadcasted_iota(jnp.int32, shape, len(shape) - 1) < FEAT


def features(x, pair_map):
    hidden = dot_nt(x, pair_map)
    left = left_half(hidden.shape)
    top_left = jnp.max(jnp.where(left, hidden, -jnp.inf), -1, keepdims=True)
    top_right = jnp.max(jnp.where(left, -jnp.inf, hidden), -1, keepdims=True)
    e = jnp.exp(hidden - jnp.where(left, top_left, top_right))
    sum_left = jnp.sum(jnp.where(left, e, 0.0), -1, keepdims=True)
    sum_right = jnp.sum(jnp.where(left, 0.0, e), -1, keepdims=True)
    return e * jnp.where(left, 1.0 / sum_left, 1.0 / sum_right)


def feature_grad(x, soft, upstream):
    left = left_half(soft.shape)
    product = soft * upstream
    inner_left = jnp.sum(jnp.where(left, product, 0.0), -1, keepdims=True)
    inner_right = jnp.sum(jnp.where(left, 0.0, product), -1, keepdims=True)
    part = soft * (upstream - jnp.where(left, inner_left, inner_right))
    u = part - pltpu.roll(part, FEAT, 1)
    return dot_tn(u.astype(BF16), x)


def head_rows(ref, head, rows, heads):
    return ref[pl.ds(head, rows, stride=heads), :]


def widen(src, dst):
    dst[...] = src[...].astype(F32)


def wrapped(k, count):
    return jnp.where(k >= count, k - count, k)


def await_bytes(ref, sem):
    pltpu.make_async_copy(ref, ref, sem).wait()


class Across:
    def __init__(self, totals, send, recv, reverse):
        self.totals, self.send, self.recv, self.reverse = totals, send, recv, reverse
        me = lax.axis_index("seq")
        self.layers = lax.axis_size("seq") // PLANE
        self.z, self.p = me // PLANE, me % PLANE

    def give(self, total):
        self.totals[self.z] = total
        for i in range(1, self.layers):
            other = wrapped(self.z + i, self.layers)
            pltpu.make_async_remote_copy(
                src_ref=self.totals.at[self.z], dst_ref=self.totals.at[self.z], send_sem=self.send, recv_sem=self.recv,
                device_id={"seq": other * PLANE + self.p}, device_id_type=MESH,
            ).start()

    def base(self):
        await_bytes(self.totals.at[pl.ds(0, self.layers - 1)], self.recv)
        base = jnp.zeros(self.totals.shape[1:], F32)
        for k in range(self.layers):
            reached = k > self.z if self.reverse else k < self.z
            base = base + jnp.where(reached, self.totals[k], 0.0)
        return base

    def finish(self):
        await_bytes(self.totals.at[pl.ds(0, self.layers - 1)], self.send)


def groups():
    me = lax.axis_index("seq")
    z, x, y = me // PLANE, (me // 4) % 4, me % 4
    low, high = x % 2, x // 2

    def first(k):
        return {"seq": (k // 2) * PLANE + (high * 2 + k % 2) * 4 + y}

    def second(k):
        return {"seq": z * PLANE + ((k % 2) * 2 + low) * 4 + k // 2}

    return (z * 2 + low, first), (y * 2 + high, second)


class Total:
    def __init__(self, grads, out, inbox, slots, sems):
        self.grads, self.out, self.inbox, self.slots, self.sems = grads, out, inbox, slots, sems
        self.core = lax.axis_index("head")

    def swap(self):
        other = 1 - self.core
        return pltpu.make_async_remote_copy(
            src_ref=self.grads.at[other], dst_ref=self.inbox, send_sem=self.sems[0], recv_sem=self.sems[1],
            device_id={"head": other}, device_id_type=MESH,
        )

    def give(self, stage, value):
        here, device = groups()[stage]
        slots, send, recv = self.slots[stage], self.sems[2 + 2 * stage], self.sems[3 + 2 * stage]
        slots[here] = value
        for i in range(1, 8):
            pltpu.make_async_remote_copy(
                src_ref=slots.at[here], dst_ref=slots.at[here], send_sem=send, recv_sem=recv,
                device_id=device(wrapped(here + i, 8)), device_id_type=MESH,
            ).start()

    def take(self, stage):
        slots = self.slots[stage]
        await_bytes(slots.at[pl.ds(0, 7)], self.sems[3 + 2 * stage])
        return jnp.sum(slots[...], 0)

    def share(self):
        return pltpu.make_async_remote_copy(
            src_ref=self.out.at[self.core], dst_ref=self.out.at[self.core], send_sem=self.sems[6], recv_sem=self.sems[7],
            device_id={"head": 1 - self.core}, device_id_type=MESH,
        )

    def finish(self):
        for stage in range(2):
            await_bytes(self.slots[stage].at[pl.ds(0, 7)], self.sems[2 + 2 * stage])


def greet():
    me, core = lax.axis_index("seq"), lax.axis_index("head")
    z, p = me // PLANE, me % PLANE
    barrier = pltpu.get_barrier_semaphore()

    def plane(i, carry):
        device = {"seq": z * PLANE + (p + i) % PLANE}
        pl.semaphore_signal(barrier, inc=1, device_id=device, device_id_type=MESH)
        return carry

    lax.fori_loop(1, PLANE, plane, 0)
    here, device = groups()[0]
    for i in range(1, 8):
        pl.semaphore_signal(barrier, inc=1, device_id=device(wrapped(here + i, 8)), device_id_type=MESH)
    pl.semaphore_signal(barrier, inc=1, device_id={"head": 1 - core}, device_id_type=MESH)
    return PLANE - 1 + 7 + 1


def kernel(
    heads, total_tokens, q_ref, k_ref, v_ref, t_ref, mq_ref, mk_ref, out_ref, grad_ref,
    k_in, v_in, q_in, t_in, k_wide, v_wide, q_wide, t_wide, mine, held,
    phi_all, soft_q, soft_k, numer_near, denom_near, damp, state, halo_state, d_numer_all, d_denom_all,
    gstate, state16, state_sum, later16, later_sum, near, lead, totals1, totals2, out_send, out_held, out_wide, gq, gk, grads, inbox, slots1, slots2,
    load, store, send, recv, send_halo, recv_halo, send_lead, recv_lead, send_out, recv_out, *sems,
):
    w = WINDOW
    rows = 2 * w
    chunks = PLANE
    K, V, Q, T = range(4)
    greeted = greet()
    arrays = [(k_ref, k_in, k_wide), (v_ref, v_in, v_wide), (q_ref, q_in, q_wide), (t_ref, t_in, t_wide)]
    loads = [pltpu.make_async_copy(source, into, load.at[i]) for i, (source, into, wide) in enumerate(arrays)]
    for j in (Q, K, V, T):
        loads[j].start()
    me = lax.axis_index("seq")
    layers = lax.axis_size("seq") // PLANE
    z, p = me // PLANE, me % PLANE
    has_prior = z > 0
    has_later = z < layers - 1
    forward = Across(totals1, sems[0], sems[1], False)
    backward = Across(totals2, sems[2], sems[3], True)
    final = Total(grads, grad_ref, inbox, (slots1, slots2), sems[4:12])

    def in_plane(k):
        return {"seq": z * PLANE + k}

    halo_there = held.at[0, pl.ds(0, 2), pl.ds(w, w)]
    halo_copy = pltpu.make_async_remote_copy(
        src_ref=held.at[chunks, pl.ds(0, 2), pl.ds(w, w)], dst_ref=halo_there, send_sem=send_halo, recv_sem=recv_halo,
        device_id={"seq": jnp.where(has_later, z + 1, 0) * PLANE + p}, device_id_type=MESH,
    )
    lead_copy = pltpu.make_async_remote_copy(
        src_ref=lead.at[0], dst_ref=lead.at[chunks], send_sem=send_lead, recv_sem=recv_lead,
        device_id={"seq": jnp.where(has_prior, z - 1, layers - 1) * PLANE + p}, device_id_type=MESH,
    )

    def give(wave, first):
        def step(i, carry):
            for head in (wrapped(p + 2 * i, PLANE), wrapped(p + 2 * i + 1, PLANE)):
                for j in wave:
                    mine[head, j] = head_rows(arrays[j][2], head, rows, heads).astype(BF16)
            part = pl.ds(wave[0], len(wave))
            for k in range(2):
                head = wrapped(p + 2 * i + k, PLANE)

                @pl.when(head != p)
                def _():
                    pltpu.make_async_remote_copy(
                        src_ref=mine.at[head, part], dst_ref=held.at[p + 1, part],
                        send_sem=send, recv_sem=recv.at[first + p],
                        device_id=in_plane(head), device_id_type=MESH,
                    ).start()

                @pl.when(head == p)
                def _():
                    pltpu.make_async_copy(mine.at[head, part], held.at[p + 1, part], recv.at[first + p]).start()

            return carry

        for j in wave:
            loads[j].wait()
            widen(arrays[j][1], arrays[j][2])
        if first == 0:
            pl.semaphore_wait(pltpu.get_barrier_semaphore(), greeted)
        lax.fori_loop(0, heads // 2, step, 0)

    give((Q,), 0)
    give((K, V), PLANE)
    give((T,), 2 * PLANE)

    map_q, map_k = (
        jnp.concatenate([ref[...], (-ref[...].astype(F32)).astype(BF16)], 0) for ref in (mq_ref, mk_ref)
    )
    row = lax.broadcasted_iota(jnp.int32, (w, rows), 0)
    col = lax.broadcasted_iota(jnp.int32, (w, rows), 1)
    scale = 128 ** (-0.5)
    zero_state = jnp.zeros((ROWS, 128), F32)

    def masks(c, half):
        in_window = (col > row) & (col <= row + w)
        in_far = col <= row
        if half:
            return in_window, in_far
        live = (col >= w) | has_prior | (c > 0)
        return in_window & live, in_far & live

    def ext(ref, c):
        return jnp.concatenate([ref[c, w:, :], ref[c + 1, :w, :]], 0)

    def arriving(i):
        return wrapped(p + PLANE - 2 * i, PLANE), wrapped(p + PLANE - 2 * i - 1, PLANE)

    def query_part(i, carry):
        pair = arriving(i)
        for c in pair:
            await_bytes(held.at[c + 1, pl.ds(Q, 1)], recv.at[c])
        for c in pair:
            soft_q[c] = features(held[c + 1, Q], map_q)
        return carry

    def key_part(i, carry):
        pair = arriving(i)
        for c in pair:
            await_bytes(held.at[c + 1, pl.ds(K, 2)], recv.at[PLANE + c])

            @pl.when((c == chunks - 1) & has_later)
            def _():
                halo_copy.start()

        for c in pair:
            soft = features(held[c + 1, K], map_k)
            soft_k[c] = soft
            phi_all[c + 1] = soft.astype(BF16)
        return carry

    def state_part(i, carry):
        for c in arriving(i):
            phi = phi_all[c + 1]
            for half in range(2):
                part = phi[half * w : (half + 1) * w]
                block_sum = jnp.sum(part.astype(F32), 0, keepdims=True)
                state[2 * c + half, :128, :] = dot_tn(part, held[c + 1, V, half * w : (half + 1) * w, :])
                state[2 * c + half, 128:, :] = jnp.broadcast_to(block_sum, (ROWS - 128, 128))
        return carry

    def sum_of(ref):
        return lax.fori_loop(0, chunks, lambda i, whole: whole + (ref[2 * i] + ref[2 * i + 1]), zero_state)

    lax.fori_loop(0, chunks // 2, query_part, 0)
    lax.fori_loop(0, chunks // 2, key_part, 0)
    lax.fori_loop(0, chunks // 2, state_part, 0)
    forward.give(sum_of(state))

    def near_part(i, carry):
        @pl.when(i == chunks // 2 - 1)
        def _():
            @pl.when(has_prior)
            def _():
                await_bytes(halo_there, recv_halo)

            @pl.when(jnp.logical_not(has_prior))
            def _():
                held[0, :2, w:, :] = jnp.zeros((2, w, 128), BF16)

            phi_halo = jnp.where(has_prior, features(held[0, K, w:, :], map_k), 0.0).astype(BF16)
            phi_all[0, w:, :] = phi_halo
            halo_state[:128, :] = dot_tn(phi_halo, held[0, V, w:, :])
            halo_sum = jnp.sum(phi_halo.astype(F32), 0, keepdims=True)
            halo_state[128:, :] = jnp.broadcast_to(halo_sum, (ROWS - 128, 128))

        for c in (chunks - 1 - 2 * i, chunks - 2 - 2 * i):
            phi_q = soft_q[c].astype(BF16)
            for half in range(2):
                block, span = pl.ds(half * w, w), slice(half * w, (half + 1) * w)
                if half:
                    kn, vn, pn = held[c + 1, K], held[c + 1, V], phi_all[c + 1]
                else:
                    kn, vn, pn = ext(held.at[:, K], c), ext(held.at[:, V], c), ext(phi_all, c)
                in_window, in_far = masks(c, half)
                scores = jnp.where(in_window, dot_nt(held[c + 1, Q, span, :], kn) * scale, -jnp.inf)
                top = jnp.max(scores, -1, keepdims=True)
                damping = jnp.exp(-top)
                far = damping * dot_nt(phi_q[span], pn)
                weight = jnp.exp(scores - top) + jnp.where(in_far, far, 0.0)
                numer_near[c, block, :] = dot_nn(weight.astype(BF16), vn)
                denom_near[c, block, :] = jnp.sum(weight, -1, keepdims=True)
                damp[c, block, :] = damping
        return carry

    lax.fori_loop(0, chunks // 2, near_part, 0)

    def store_split(into, sums, b, whole):
        high, low = split(whole[:128])
        into[b, :128, :] = high
        into[b, 128:, :] = low
        sums[b] = whole[128:]

    base = forward.base()

    def lead_states(b, carry):
        now, after = carry
        own = state[b]
        store_split(state16, state_sum, b, now)
        return after, after + own

    lax.fori_loop(0, 2 * chunks, lead_states, (base - halo_state[...], base))

    def middle_part(i, carry):
        pair = arriving(i)
        for c in pair:
            await_bytes(held.at[c + 1, pl.ds(T, 1)], recv.at[2 * PLANE + c])
        for c in pair:
            phi_q = soft_q[c].astype(BF16)
            target = held[c + 1, T].astype(F32)
            for half in range(2):
                block, span, b = pl.ds(half * w, w), slice(half * w, (half + 1) * w), 2 * c + half
                pq = phi_q[span]
                wide_pq = pq.astype(F32)
                damping = damp[c, block, :]
                state_den = jnp.sum(wide_pq * state_sum[b, 0:1, :], -1, keepdims=True)
                state_num = dot_nn(jnp.concatenate([pq, pq], 1), state16[b])
                numer = numer_near[c, block, :] + damping * state_num
                inverse = 1.0 / (denom_near[c, block, :] + damping * state_den)
                output = numer * inverse
                out_send[c, block, :] = output.astype(BF16)
                d_out = (output - target[span]) * (2.0 / total_tokens)
                d_numer = d_out * inverse
                d_denom = -jnp.sum(d_out * output, -1, keepdims=True) * inverse
                d_numer_all[c, block, :] = d_numer
                d_denom_all[c, block, :] = d_denom
                g_state = dot_tn(pq, (damping * d_numer).astype(BF16))
                g_sum = jnp.sum(damping * d_denom * wide_pq, 0, keepdims=True)
                gstate[b, :128, :] = g_state
                gstate[b, 128:, :] = jnp.broadcast_to(g_sum, (ROWS - 128, 128))
        return carry

    lax.fori_loop(0, chunks // 2, middle_part, 0)
    backward.give(sum_of(gstate))

    def give_out(i, carry):
        c = wrapped(p + i, PLANE)
        pltpu.make_async_remote_copy(
            src_ref=out_send.at[c], dst_ref=out_held.at[p], send_sem=send_out, recv_sem=recv_out,
            device_id=in_plane(c), device_id_type=MESH,
        ).start()
        return carry

    lax.fori_loop(1, PLANE, give_out, 0)
    pltpu.make_async_copy(out_send.at[p], out_held.at[p], recv_out).start()
    gq[...] = jnp.zeros_like(gq)
    gk[...] = jnp.zeros_like(gk)

    def far_part(i, carry):
        d_phi = []
        pair = pl.ds(2 * i, 2)
        for c in (2 * i, 2 * i + 1):
            phi_q = soft_q[c].astype(BF16)
            d_near = []
            for half in range(2):
                block, b = pl.ds(half * w, w), 2 * c + half
                in_far = masks(c, half)[1]
                if half:
                    vn, pn = held[c + 1, V], phi_all[c + 1]
                else:
                    vn, pn = ext(held.at[:, V], c), ext(phi_all, c)
                damping = damp[c, block, :]
                d_numer = d_numer_all[c, block, :]
                d_denom = d_denom_all[c, block, :]
                high, low = split(damping * d_numer)
                far_grad = damping * (dot_nt(d_numer.astype(BF16), vn) + d_denom)
                far_grad = jnp.where(in_far, far_grad, 0.0).astype(BF16)
                through = dot_nt(high, state16[b])
                through = through[:, :128] + through[:, 128:] + dot_nt(low, state16[b, :128, :])
                d_phi.append(dot_nn(far_grad, pn) + through + damping * d_denom * state_sum[b, 0:1, :])
                d_near.append(dot_tn(far_grad, phi_q[half * w : (half + 1) * w]))
            lead[c] = d_near[0][:w]
            near[c, :w, :] = d_near[0][w:] + d_near[1][:w]
            near[c, w:, :] = d_near[1][w:]
        x = jnp.concatenate([held[2 * i + 1, Q], held[2 * i + 2, Q]], 0)
        gq[...] += feature_grad(x, soft_q[pair].reshape(2 * rows, 128), jnp.concatenate(d_phi, 0))

        @pl.when((i == 0) & has_prior)
        def _():
            high, low = split(gstate[0, :128, :])
            hv = held[0, V, w:, :]
            lead[0] = lead[0] - (dot_nt(hv, high) + dot_nt(hv, low) + gstate[0, 128:129, :])
            lead_copy.start()

        return carry

    lax.fori_loop(0, chunks // 2, far_part, 0)

    base = backward.base()

    def tail_states(i, carry):
        now, after = carry
        b = 2 * chunks - 1 - i
        own = gstate[b]
        store_split(later16, later_sum, b, now)
        return after, after + own

    lax.fori_loop(0, 2 * chunks, tail_states, (base, base))

    @pl.when(has_later)
    def _():
        await_bytes(lead.at[chunks], recv_lead)

    @pl.when(jnp.logical_not(has_later))
    def _():
        lead[chunks] = jnp.zeros(lead.shape[1:], F32)

    def last_part(i, carry):
        d_phi = []
        pair = pl.ds(2 * i, 2)
        for c in (2 * i, 2 * i + 1):
            for half in range(2):
                span, b = slice(half * w, (half + 1) * w), 2 * c + half
                far = dot_nt(held[c + 1, V, span, :], later16[b])
                far = far[:, :128] + far[:, 128:] + later_sum[b, 0:1, :]
                d_near = near[c, span, :]
                d_phi.append(far + (d_near + lead[c + 1] if half else d_near))
        x = jnp.concatenate([held[2 * i + 1, K], held[2 * i + 2, K]], 0)
        gk[...] += feature_grad(x, soft_k[pair].reshape(2 * rows, 128), jnp.concatenate(d_phi, 0))
        return carry

    lax.fori_loop(0, chunks // 2, last_part, 0)
    grads[0] = gq[:FEAT, :]
    grads[1] = gk[:FEAT, :]
    swap = final.swap()
    swap.start()
    swap.wait()
    final.give(0, grads[final.core] + inbox[...])
    await_bytes(out_held, recv_out)

    def arrange(i, carry):
        for head in (2 * i, 2 * i + 1):
            out_wide[pl.ds(head, rows, stride=heads), :] = out_held[head].astype(F32)
        return carry

    lax.fori_loop(0, heads // 2, arrange, 0)
    out_copy = pltpu.make_async_copy(out_wide, out_ref, store)
    out_copy.start()
    final.give(1, final.take(0))
    grad_ref[final.core] = final.take(1)
    share = final.share()
    share.start()
    most = pl.ds(0, PLANE - 1)
    await_bytes(mine.at[most], send)
    await_bytes(out_send.at[most], send_out)
    forward.finish()
    backward.finish()

    @pl.when(has_later)
    def _():
        halo_copy.wait_send()

    @pl.when(has_prior)
    def _():
        lead_copy.wait_send()

    final.finish()
    out_copy.wait()
    share.wait()


def per_device(queries, keys, values, target, map_q, map_k):
    rows, heads, size = queries.shape
    total_tokens = rows * lax.axis_size("seq")
    layers = lax.axis_size("seq") // PLANE
    chunks = PLANE
    flat = (rows * heads, size)
    wide = pltpu.VMEM(flat, F32)
    narrow = pltpu.VMEM(flat, BF16)
    tiles = pltpu.VMEM((chunks, rows, size), F32)
    tiles16 = pltpu.VMEM((chunks, rows, size), BF16)
    column = pltpu.VMEM((chunks, rows, 1), F32)
    states = pltpu.VMEM((2 * chunks, ROWS, size), F32)
    state = pltpu.VMEM((ROWS, size), F32)
    split_states = pltpu.VMEM((2 * chunks, 2 * size, size), BF16)
    state_sums = pltpu.VMEM((2 * chunks, ROWS - 128, size), F32)
    layer = pltpu.VMEM((layers, ROWS, size), F32)
    grad = pltpu.VMEM((size, size), F32)
    slots = pltpu.VMEM((8, FEAT, size), F32)
    dma = pltpu.SemaphoreType.DMA
    one = dma(())
    vmem = pl.BlockSpec(memory_space=pltpu.VMEM)
    hbm = pl.BlockSpec(memory_space=pl.ANY)
    output, grads = pl.pallas_call(
        functools.partial(kernel, heads, total_tokens),
        out_shape=[
            jax.ShapeDtypeStruct(flat, F32),
            jax.ShapeDtypeStruct((2, FEAT, size), F32),
        ],
        in_specs=[hbm] * 4 + [vmem] * 2,
        out_specs=[hbm, vmem],
        scratch_shapes=[
            narrow, narrow, narrow, narrow, wide, wide, wide, wide,
            pltpu.VMEM((heads, 4, rows, size), BF16), pltpu.VMEM((chunks + 1, 4, rows, size), BF16),
            pltpu.VMEM((chunks + 1, rows, size), BF16), tiles, tiles, tiles, column, column, states, state, tiles, column,
            states, split_states, state_sums, split_states, state_sums, tiles,
            pltpu.VMEM((chunks + 1, WINDOW, size), F32), layer, layer, tiles16, tiles16, wide,
            grad, grad, pltpu.VMEM((2, FEAT, size), F32), pltpu.VMEM((FEAT, size), F32), slots, slots,
            dma((4,)), one, one, dma((3 * PLANE,)), one, one, one, one, one, one, *[one] * 12,
        ],
        compiler_params=pltpu.CompilerParams(vmem_limit_bytes=VMEM_LIMIT, collective_id=0, has_side_effects=True),
    )(*(array.reshape(flat) for array in (queries, keys, values, target)), map_q.T, map_k.T)
    hybrid = output.astype(BF16).reshape(rows, heads, size)
    return hybrid, grads[0].T, grads[1].T


def solution(mesh):
    tokens = P("seq", "head", None)
    return jax.shard_map(
        per_device,
        mesh=mesh,
        in_specs=(tokens, tokens, tokens, tokens, P(), P()),
        out_specs=(tokens, P(), P()),
        check_vma=False,
    )
```

```python
import functools

import jax
import jax.numpy as jnp
from jax import lax
from jax.experimental import pallas as pl
from jax.experimental.pallas import tpu as pltpu
from jax.sharding import PartitionSpec as P

WINDOW = 64
FEAT = 64
PLANE = 16
ROWS = 136
MESH = pl.DeviceIdType.MESH
F32 = jnp.float32
BF16 = jnp.bfloat16
VMEM_LIMIT = 56 * 1024 * 1024


def dot_nn(a, b):
    return lax.dot_general(a, b, (((1,), (0,)), ((), ())), preferred_element_type=F32)


def dot_nt(a, b):
    return lax.dot_general(a, b, (((1,), (1,)), ((), ())), preferred_element_type=F32)


def dot_tn(a, b):
    return lax.dot_general(a, b, (((0,), (0,)), ((), ())), preferred_element_type=F32)


def split(x):
    high = x.astype(BF16)
    return high, (x - high.astype(F32)).astype(BF16)


def left_half(shape):
    return lax.broadcasted_iota(jnp.int32, shape, len(shape) - 1) < FEAT


def features(x, pair_map):
    hidden = dot_nt(x, pair_map)
    left = left_half(hidden.shape)
    top_left = jnp.max(jnp.where(left, hidden, -jnp.inf), -1, keepdims=True)
    top_right = jnp.max(jnp.where(left, -jnp.inf, hidden), -1, keepdims=True)
    e = jnp.exp(hidden - jnp.where(left, top_left, top_right))
    sum_left = jnp.sum(jnp.where(left, e, 0.0), -1, keepdims=True)
    sum_right = jnp.sum(jnp.where(left, 0.0, e), -1, keepdims=True)
    return e * jnp.where(left, 1.0 / sum_left, 1.0 / sum_right)


def feature_grad(x, soft, upstream):
    left = left_half(soft.shape)
    product = soft * upstream
    inner_left = jnp.sum(jnp.where(left, product, 0.0), -1, keepdims=True)
    inner_right = jnp.sum(jnp.where(left, 0.0, product), -1, keepdims=True)
    part = soft * (upstream - jnp.where(left, inner_left, inner_right))
    u = part - pltpu.roll(part, FEAT, 1)
    return dot_tn(u.astype(BF16), x)


def head_rows(ref, head, rows, heads):
    return ref[pl.ds(head, rows, stride=heads), :]


def widen(src, dst):
    dst[...] = src[...].astype(F32)


def wrapped(k, count):
    return jnp.where(k >= count, k - count, k)


def await_bytes(ref, sem):
    pltpu.make_async_copy(ref, ref, sem).wait()


class Across:
    def __init__(self, totals, send, recv, reverse):
        self.totals, self.send, self.recv, self.reverse = totals, send, recv, reverse
        me = lax.axis_index("seq")
        self.layers = lax.axis_size("seq") // PLANE
        self.z, self.p = me // PLANE, me % PLANE

    def give(self, total):
        self.totals[self.z] = total
        for i in range(1, self.layers):
            other = wrapped(self.z + i, self.layers)
            pltpu.make_async_remote_copy(
                src_ref=self.totals.at[self.z], dst_ref=self.totals.at[self.z], send_sem=self.send, recv_sem=self.recv,
                device_id={"seq": other * PLANE + self.p}, device_id_type=MESH,
            ).start()

    def base(self):
        await_bytes(self.totals.at[pl.ds(0, self.layers - 1)], self.recv)
        base = jnp.zeros(self.totals.shape[1:], F32)
        for k in range(self.layers):
            reached = k > self.z if self.reverse else k < self.z
            base = base + jnp.where(reached, self.totals[k], 0.0)
        return base

    def finish(self):
        await_bytes(self.totals.at[pl.ds(0, self.layers - 1)], self.send)


def groups():
    me = lax.axis_index("seq")
    z, x, y = me // PLANE, (me // 4) % 4, me % 4
    low, high = x % 2, x // 2

    def first(k):
        return {"seq": (k // 2) * PLANE + (high * 2 + k % 2) * 4 + y}

    def second(k):
        return {"seq": z * PLANE + ((k % 2) * 2 + low) * 4 + k // 2}

    return (z * 2 + low, first), (y * 2 + high, second)


class Total:
    def __init__(self, grads, out, inbox, slots, sems):
        self.grads, self.out, self.inbox, self.slots, self.sems = grads, out, inbox, slots, sems
        self.core = lax.axis_index("head")

    def swap(self):
        other = 1 - self.core
        return pltpu.make_async_remote_copy(
            src_ref=self.grads.at[other], dst_ref=self.inbox, send_sem=self.sems[0], recv_sem=self.sems[1],
            device_id={"head": other}, device_id_type=MESH,
        )

    def give(self, stage, value):
        here, device = groups()[stage]
        slots, send, recv = self.slots[stage], self.sems[2 + 2 * stage], self.sems[3 + 2 * stage]
        slots[here] = value
        for i in range(1, 8):
            pltpu.make_async_remote_copy(
                src_ref=slots.at[here], dst_ref=slots.at[here], send_sem=send, recv_sem=recv,
                device_id=device(wrapped(here + i, 8)), device_id_type=MESH,
            ).start()

    def take(self, stage):
        slots = self.slots[stage]
        await_bytes(slots.at[pl.ds(0, 7)], self.sems[3 + 2 * stage])
        return jnp.sum(slots[...], 0)

    def share(self):
        return pltpu.make_async_remote_copy(
            src_ref=self.out.at[self.core], dst_ref=self.out.at[self.core], send_sem=self.sems[6], recv_sem=self.sems[7],
            device_id={"head": 1 - self.core}, device_id_type=MESH,
        )

    def finish(self):
        for stage in range(2):
            await_bytes(self.slots[stage].at[pl.ds(0, 7)], self.sems[2 + 2 * stage])


def greet():
    me, core = lax.axis_index("seq"), lax.axis_index("head")
    z, p = me // PLANE, me % PLANE
    barrier = pltpu.get_barrier_semaphore()

    def plane(i, carry):
        device = {"seq": z * PLANE + (p + i) % PLANE}
        pl.semaphore_signal(barrier, inc=1, device_id=device, device_id_type=MESH)
        return carry

    lax.fori_loop(1, PLANE, plane, 0)
    here, device = groups()[0]
    for i in range(1, 8):
        pl.semaphore_signal(barrier, inc=1, device_id=device(wrapped(here + i, 8)), device_id_type=MESH)
    pl.semaphore_signal(barrier, inc=1, device_id={"head": 1 - core}, device_id_type=MESH)
    return PLANE - 1 + 7 + 1


def kernel(
    heads, total_tokens, q_ref, k_ref, v_ref, t_ref, mq_ref, mk_ref, out_ref, grad_ref,
    k_in, v_in, q_in, t_in, k_wide, v_wide, q_wide, t_wide, mine, held,
    phi_all, soft_q, soft_k, numer_near, denom_near, damp, state, halo_state, d_numer_all, d_denom_all,
    gstate, state16, state_sum, later16, later_sum, near, lead, totals1, totals2, out_send, out_held, out_wide, gq, gk, grads, inbox, slots1, slots2,
    load, store, send, recv, send_halo, recv_halo, send_lead, recv_lead, send_out, recv_out, *sems,
):
    w = WINDOW
    rows = 2 * w
    chunks = PLANE
    K, V, Q, T = range(4)
    greeted = greet()
    arrays = [(k_ref, k_in, k_wide), (v_ref, v_in, v_wide), (q_ref, q_in, q_wide), (t_ref, t_in, t_wide)]
    loads = [pltpu.make_async_copy(source, into, load.at[i]) for i, (source, into, wide) in enumerate(arrays)]
    for j in (Q, K, V, T):
        loads[j].start()
    me = lax.axis_index("seq")
    layers = lax.axis_size("seq") // PLANE
    z, p = me // PLANE, me % PLANE
    has_prior = z > 0
    has_later = z < layers - 1
    forward = Across(totals1, sems[0], sems[1], False)
    backward = Across(totals2, sems[2], sems[3], True)
    final = Total(grads, grad_ref, inbox, (slots1, slots2), sems[4:12])

    def in_plane(k):
        return {"seq": z * PLANE + k}

    halo_there = held.at[0, pl.ds(0, 2), pl.ds(w, w)]
    halo_copy = pltpu.make_async_remote_copy(
        src_ref=held.at[chunks, pl.ds(0, 2), pl.ds(w, w)], dst_ref=halo_there, send_sem=send_halo, recv_sem=recv_halo,
        device_id={"seq": jnp.where(has_later, z + 1, 0) * PLANE + p}, device_id_type=MESH,
    )
    lead_copy = pltpu.make_async_remote_copy(
        src_ref=lead.at[0], dst_ref=lead.at[chunks], send_sem=send_lead, recv_sem=recv_lead,
        device_id={"seq": jnp.where(has_prior, z - 1, layers - 1) * PLANE + p}, device_id_type=MESH,
    )

    def give(wave, first):
        def step(i, carry):
            for head in (wrapped(p + 2 * i, PLANE), wrapped(p + 2 * i + 1, PLANE)):
                for j in wave:
                    mine[head, j] = head_rows(arrays[j][2], head, rows, heads).astype(BF16)
            part = pl.ds(wave[0], len(wave))
            for k in range(2):
                head = wrapped(p + 2 * i + k, PLANE)

                @pl.when(head != p)
                def _():
                    pltpu.make_async_remote_copy(
                        src_ref=mine.at[head, part], dst_ref=held.at[p + 1, part],
                        send_sem=send, recv_sem=recv.at[first + p],
                        device_id=in_plane(head), device_id_type=MESH,
                    ).start()

                @pl.when(head == p)
                def _():
                    pltpu.make_async_copy(mine.at[head, part], held.at[p + 1, part], recv.at[first + p]).start()

            return carry

        for j in wave:
            loads[j].wait()
            widen(arrays[j][1], arrays[j][2])
        if first == 0:
            pl.semaphore_wait(pltpu.get_barrier_semaphore(), greeted)
        lax.fori_loop(0, heads // 2, step, 0)

    give((Q,), 0)
    give((K,), PLANE)
    give((V,), 2 * PLANE)

    map_q, map_k = (
        jnp.concatenate([ref[...], (-ref[...].astype(F32)).astype(BF16)], 0) for ref in (mq_ref, mk_ref)
    )
    row = lax.broadcasted_iota(jnp.int32, (w, rows), 0)
    col = lax.broadcasted_iota(jnp.int32, (w, rows), 1)
    scale = 128 ** (-0.5)
    zero_state = jnp.zeros((ROWS, 128), F32)

    def masks(c, half):
        in_window = (col > row) & (col <= row + w)
        in_far = col <= row
        if half:
            return in_window, in_far
        live = (col >= w) | has_prior | (c > 0)
        return in_window & live, in_far & live

    def ext(ref, c):
        return jnp.concatenate([ref[c, w:, :], ref[c + 1, :w, :]], 0)

    def arriving(i):
        return wrapped(p + PLANE - 2 * i, PLANE), wrapped(p + PLANE - 2 * i - 1, PLANE)

    def query_part(i, carry):
        pair = arriving(i)
        for c in pair:
            await_bytes(held.at[c + 1, pl.ds(Q, 1)], recv.at[c])
        for c in pair:
            soft_q[c] = features(held[c + 1, Q], map_q)
        return carry

    def key_part(i, carry):
        pair = arriving(i)
        for c in pair:
            await_bytes(held.at[c + 1, pl.ds(K, 1)], recv.at[PLANE + c])
        for c in pair:
            soft = features(held[c + 1, K], map_k)
            soft_k[c] = soft
            phi_all[c + 1] = soft.astype(BF16)
        return carry

    def state_part(i, carry):
        pair = arriving(i)
        for c in pair:
            await_bytes(held.at[c + 1, pl.ds(V, 1)], recv.at[2 * PLANE + c])

            @pl.when((c == chunks - 1) & has_later)
            def _():
                halo_copy.start()

        for c in pair:
            phi = phi_all[c + 1]
            for half in range(2):
                part = phi[half * w : (half + 1) * w]
                block_sum = jnp.sum(part.astype(F32), 0, keepdims=True)
                state[2 * c + half, :128, :] = dot_tn(part, held[c + 1, V, half * w : (half + 1) * w, :])
                state[2 * c + half, 128:, :] = jnp.broadcast_to(block_sum, (ROWS - 128, 128))
        return carry

    def sum_of(ref):
        return lax.fori_loop(0, chunks, lambda i, whole: whole + (ref[2 * i] + ref[2 * i + 1]), zero_state)

    lax.fori_loop(0, chunks // 2, query_part, 0)
    give((T,), 3 * PLANE)
    lax.fori_loop(0, chunks // 2, key_part, 0)
    lax.fori_loop(0, chunks // 2, state_part, 0)
    forward.give(sum_of(state))

    def near_part(i, carry):
        @pl.when(i == chunks // 2 - 1)
        def _():
            @pl.when(has_prior)
            def _():
                await_bytes(halo_there, recv_halo)

            @pl.when(jnp.logical_not(has_prior))
            def _():
                held[0, :2, w:, :] = jnp.zeros((2, w, 128), BF16)

            phi_halo = jnp.where(has_prior, features(held[0, K, w:, :], map_k), 0.0).astype(BF16)
            phi_all[0, w:, :] = phi_halo
            halo_state[:128, :] = dot_tn(phi_halo, held[0, V, w:, :])
            halo_sum = jnp.sum(phi_halo.astype(F32), 0, keepdims=True)
            halo_state[128:, :] = jnp.broadcast_to(halo_sum, (ROWS - 128, 128))

        for c in (chunks - 1 - 2 * i, chunks - 2 - 2 * i):
            phi_q = soft_q[c].astype(BF16)
            for half in range(2):
                block, span = pl.ds(half * w, w), slice(half * w, (half + 1) * w)
                if half:
                    kn, vn, pn = held[c + 1, K], held[c + 1, V], phi_all[c + 1]
                else:
                    kn, vn, pn = ext(held.at[:, K], c), ext(held.at[:, V], c), ext(phi_all, c)
                in_window, in_far = masks(c, half)
                scores = jnp.where(in_window, dot_nt(held[c + 1, Q, span, :], kn) * scale, -jnp.inf)
                top = jnp.max(scores, -1, keepdims=True)
                damping = jnp.exp(-top)
                far = damping * dot_nt(phi_q[span], pn)
                weight = jnp.exp(scores - top) + jnp.where(in_far, far, 0.0)
                numer_near[c, block, :] = dot_nn(weight.astype(BF16), vn)
                denom_near[c, block, :] = jnp.sum(weight, -1, keepdims=True)
                damp[c, block, :] = damping
        return carry

    lax.fori_loop(0, chunks // 2, near_part, 0)

    def store_split(into, sums, b, whole):
        high, low = split(whole[:128])
        into[b, :128, :] = high
        into[b, 128:, :] = low
        sums[b] = whole[128:]

    base = forward.base()

    def lead_states(b, carry):
        now, after = carry
        own = state[b]
        store_split(state16, state_sum, b, now)
        return after, after + own

    lax.fori_loop(0, 2 * chunks, lead_states, (base - halo_state[...], base))

    def middle_part(i, carry):
        pair = arriving(i)
        for c in pair:
            await_bytes(held.at[c + 1, pl.ds(T, 1)], recv.at[3 * PLANE + c])
        for c in pair:
            phi_q = soft_q[c].astype(BF16)
            target = held[c + 1, T].astype(F32)
            for half in range(2):
                block, span, b = pl.ds(half * w, w), slice(half * w, (half + 1) * w), 2 * c + half
                pq = phi_q[span]
                wide_pq = pq.astype(F32)
                damping = damp[c, block, :]
                state_den = jnp.sum(wide_pq * state_sum[b, 0:1, :], -1, keepdims=True)
                state_num = dot_nn(jnp.concatenate([pq, pq], 1), state16[b])
                numer = numer_near[c, block, :] + damping * state_num
                inverse = 1.0 / (denom_near[c, block, :] + damping * state_den)
                output = numer * inverse
                out_send[c, block, :] = output.astype(BF16)
                d_out = (output - target[span]) * (2.0 / total_tokens)
                d_numer = d_out * inverse
                d_denom = -jnp.sum(d_out * output, -1, keepdims=True) * inverse
                d_numer_all[c, block, :] = d_numer
                d_denom_all[c, block, :] = d_denom
                g_state = dot_tn(pq, (damping * d_numer).astype(BF16))
                g_sum = jnp.sum(damping * d_denom * wide_pq, 0, keepdims=True)
                gstate[b, :128, :] = g_state
                gstate[b, 128:, :] = jnp.broadcast_to(g_sum, (ROWS - 128, 128))
        return carry

    lax.fori_loop(0, chunks // 2, middle_part, 0)
    backward.give(sum_of(gstate))

    def give_out(i, carry):
        c = wrapped(p + i, PLANE)
        pltpu.make_async_remote_copy(
            src_ref=out_send.at[c], dst_ref=out_held.at[p], send_sem=send_out, recv_sem=recv_out,
            device_id=in_plane(c), device_id_type=MESH,
        ).start()
        return carry

    lax.fori_loop(1, PLANE, give_out, 0)
    pltpu.make_async_copy(out_send.at[p], out_held.at[p], recv_out).start()
    gq[...] = jnp.zeros_like(gq)
    gk[...] = jnp.zeros_like(gk)

    def far_part(i, carry):
        d_phi = []
        pair = pl.ds(2 * i, 2)
        for c in (2 * i, 2 * i + 1):
            phi_q = soft_q[c].astype(BF16)
            d_near = []
            for half in range(2):
                block, b = pl.ds(half * w, w), 2 * c + half
                in_far = masks(c, half)[1]
                if half:
                    vn, pn = held[c + 1, V], phi_all[c + 1]
                else:
                    vn, pn = ext(held.at[:, V], c), ext(phi_all, c)
                damping = damp[c, block, :]
                d_numer = d_numer_all[c, block, :]
                d_denom = d_denom_all[c, block, :]
                high, low = split(damping * d_numer)
                far_grad = damping * (dot_nt(d_numer.astype(BF16), vn) + d_denom)
                far_grad = jnp.where(in_far, far_grad, 0.0).astype(BF16)
                through = dot_nt(high, state16[b])
                through = through[:, :128] + through[:, 128:] + dot_nt(low, state16[b, :128, :])
                d_phi.append(dot_nn(far_grad, pn) + through + damping * d_denom * state_sum[b, 0:1, :])
                d_near.append(dot_tn(far_grad, phi_q[half * w : (half + 1) * w]))
            lead[c] = d_near[0][:w]
            near[c, :w, :] = d_near[0][w:] + d_near[1][:w]
            near[c, w:, :] = d_near[1][w:]
        x = jnp.concatenate([held[2 * i + 1, Q], held[2 * i + 2, Q]], 0)
        gq[...] += feature_grad(x, soft_q[pair].reshape(2 * rows, 128), jnp.concatenate(d_phi, 0))

        @pl.when((i == 0) & has_prior)
        def _():
            high, low = split(gstate[0, :128, :])
            hv = held[0, V, w:, :]
            lead[0] = lead[0] - (dot_nt(hv, high) + dot_nt(hv, low) + gstate[0, 128:129, :])
            lead_copy.start()

        return carry

    lax.fori_loop(0, chunks // 2, far_part, 0)

    base = backward.base()

    def tail_states(i, carry):
        now, after = carry
        b = 2 * chunks - 1 - i
        own = gstate[b]
        store_split(later16, later_sum, b, now)
        return after, after + own

    lax.fori_loop(0, 2 * chunks, tail_states, (base, base))

    @pl.when(has_later)
    def _():
        await_bytes(lead.at[chunks], recv_lead)

    @pl.when(jnp.logical_not(has_later))
    def _():
        lead[chunks] = jnp.zeros(lead.shape[1:], F32)

    def last_part(i, carry):
        d_phi = []
        pair = pl.ds(2 * i, 2)
        for c in (2 * i, 2 * i + 1):
            for half in range(2):
                span, b = slice(half * w, (half + 1) * w), 2 * c + half
                far = dot_nt(held[c + 1, V, span, :], later16[b])
                far = far[:, :128] + far[:, 128:] + later_sum[b, 0:1, :]
                d_near = near[c, span, :]
                d_phi.append(far + (d_near + lead[c + 1] if half else d_near))
        x = jnp.concatenate([held[2 * i + 1, K], held[2 * i + 2, K]], 0)
        gk[...] += feature_grad(x, soft_k[pair].reshape(2 * rows, 128), jnp.concatenate(d_phi, 0))
        return carry

    lax.fori_loop(0, chunks // 2, last_part, 0)
    grads[0] = gq[:FEAT, :]
    grads[1] = gk[:FEAT, :]
    swap = final.swap()
    swap.start()
    swap.wait()
    final.give(0, grads[final.core] + inbox[...])
    await_bytes(out_held, recv_out)

    def arrange(i, carry):
        for head in (2 * i, 2 * i + 1):
            out_wide[pl.ds(head, rows, stride=heads), :] = out_held[head].astype(F32)
        return carry

    lax.fori_loop(0, heads // 2, arrange, 0)
    out_copy = pltpu.make_async_copy(out_wide, out_ref, store)
    out_copy.start()
    final.give(1, final.take(0))
    grad_ref[final.core] = final.take(1)
    share = final.share()
    share.start()
    most = pl.ds(0, PLANE - 1)
    await_bytes(mine.at[most], send)
    await_bytes(out_send.at[most], send_out)
    forward.finish()
    backward.finish()

    @pl.when(has_later)
    def _():
        halo_copy.wait_send()

    @pl.when(has_prior)
    def _():
        lead_copy.wait_send()

    final.finish()
    out_copy.wait()
    share.wait()


def per_device(queries, keys, values, target, map_q, map_k):
    rows, heads, size = queries.shape
    total_tokens = rows * lax.axis_size("seq")
    layers = lax.axis_size("seq") // PLANE
    chunks = PLANE
    flat = (rows * heads, size)
    wide = pltpu.VMEM(flat, F32)
    narrow = pltpu.VMEM(flat, BF16)
    tiles = pltpu.VMEM((chunks, rows, size), F32)
    tiles16 = pltpu.VMEM((chunks, rows, size), BF16)
    column = pltpu.VMEM((chunks, rows, 1), F32)
    states = pltpu.VMEM((2 * chunks, ROWS, size), F32)
    state = pltpu.VMEM((ROWS, size), F32)
    split_states = pltpu.VMEM((2 * chunks, 2 * size, size), BF16)
    state_sums = pltpu.VMEM((2 * chunks, ROWS - 128, size), F32)
    layer = pltpu.VMEM((layers, ROWS, size), F32)
    grad = pltpu.VMEM((size, size), F32)
    slots = pltpu.VMEM((8, FEAT, size), F32)
    dma = pltpu.SemaphoreType.DMA
    one = dma(())
    vmem = pl.BlockSpec(memory_space=pltpu.VMEM)
    hbm = pl.BlockSpec(memory_space=pl.ANY)
    output, grads = pl.pallas_call(
        functools.partial(kernel, heads, total_tokens),
        out_shape=[
            jax.ShapeDtypeStruct(flat, F32),
            jax.ShapeDtypeStruct((2, FEAT, size), F32),
        ],
        in_specs=[hbm] * 4 + [vmem] * 2,
        out_specs=[hbm, vmem],
        scratch_shapes=[
            narrow, narrow, narrow, narrow, wide, wide, wide, wide,
            pltpu.VMEM((heads, 4, rows, size), BF16), pltpu.VMEM((chunks + 1, 4, rows, size), BF16),
            pltpu.VMEM((chunks + 1, rows, size), BF16), tiles, tiles, tiles, column, column, states, state, tiles, column,
            states, split_states, state_sums, split_states, state_sums, tiles,
            pltpu.VMEM((chunks + 1, WINDOW, size), F32), layer, layer, tiles16, tiles16, wide,
            grad, grad, pltpu.VMEM((2, FEAT, size), F32), pltpu.VMEM((FEAT, size), F32), slots, slots,
            dma((4,)), one, one, dma((4 * PLANE,)), one, one, one, one, one, one, *[one] * 12,
        ],
        compiler_params=pltpu.CompilerParams(vmem_limit_bytes=VMEM_LIMIT, collective_id=0, has_side_effects=True),
    )(*(array.reshape(flat) for array in (queries, keys, values, target)), map_q.T, map_k.T)
    hybrid = output.astype(BF16).reshape(rows, heads, size)
    return hybrid, grads[0].T, grads[1].T


def solution(mesh):
    tokens = P("seq", "head", None)
    return jax.shard_map(
        per_device,
        mesh=mesh,
        in_specs=(tokens, tokens, tokens, tokens, P(), P()),
        out_specs=(tokens, P(), P()),
        check_vma=False,
    )
```
